32 devices in a mesh: seq: 8 (over z, x), head: 4 (over y, core).
Axes of the slice: x: 2, y: 2, z: 4, core: 2. Of those that a mesh axis runs over, the one named last changes fastest.
Arguments:
- hidden_states: bfloat16 [4096, 2048], P('seq', 'head'), may hold values from -7 to 7
- proj_ba: bfloat16 [2048, 64], P('head'), may hold values from -0.125 to 0.125
- query_in: bfloat16 [4096, 2048], P('seq', 'head'), may hold values from -6 to 6
- key_in: bfloat16 [4096, 2048], P('seq', 'head'), may hold values from -6 to 6
- value_in: bfloat16 [4096, 4096], P('seq', 'head'), may hold values from -6 to 6
- conv_query: bfloat16 [4, 2048], P(None, 'head'), may hold values from -2 to 2
- conv_key: bfloat16 [4, 2048], P(None, 'head'), may hold values from -2 to 2
- convolution_value_taps: bfloat16 [4, 4096], P(None, 'head'), may hold values from -2.5 to 2.5
- decay_scale: float32 [32], P('head'), may hold values from 1 to 16
- dt_bias: float32 [32], P('head'), may hold values from -30 to -2
Outputs:
- layer_output: float32 [4096, 4096], P('seq', 'head')
The draws below stay inside these ranges and needn't reach their ends.
All inputs are finite; a program needn't handle non-finite values.
Results may differ from the reference program's by a relative error of at most 0.0003.
Values may be sent and summed in bfloat16 or wider, within the bound.
No kernel may reach another device: no remote copies, remote signals or barrier semaphores. Data moves between devices by JAX's collectives and lax.ppermute only.
A program may use at most 128 MiB of HBM per device.

```python
import math
import jax
import jax.numpy as jnp
from jax import lax

D = 2048
HK = 16
HV = 32
DK = 128
DV = 128
KCONV = 4
BLOCK = 128
TOKENS = 4096


def sudden_sign_flip(key):
    coin_flips = jax.random.bernoulli(jax.random.fold_in(key, 11), 0.5, (D,))
    return jnp.where(coin_flips, 1.0, -1.0).astype(jnp.float32)


def draw_hidden_states(key, part):
    row_of_signs = sudden_sign_flip(key)
    normal_part = jax.random.normal(jax.random.fold_in(key, 1), (TOKENS, D), jnp.float32)
    places = jax.random.randint(jax.random.fold_in(key, 2), (8,), 0, TOKENS)
    row_ids = jnp.arange(TOKENS)[:, None]
    marked = jnp.any(row_ids == places[None, :], axis=1)[:, None]
    blended = jnp.where(marked, 0.3 * normal_part + 4.0 * row_of_signs[None, :], normal_part)
    return jnp.clip(blended, -7.0, 7.0).astype(jnp.bfloat16)


def draw_proj_ba(key, part):
    row_of_signs = sudden_sign_flip(key)
    random_part = jax.random.normal(jax.random.fold_in(key, 4), (D, 2 * HV), jnp.float32)
    column_ids = jnp.arange(2 * HV)
    is_gate = jnp.where(column_ids % 2 == 0, 1.0, 0.0)[None, :]
    planted = 2.25 * row_of_signs[:, None] * is_gate / D
    return jnp.clip(random_part / math.sqrt(D) + planted, -0.125, 0.125).astype(jnp.bfloat16)


def convolution_taps(key, salt_value):
    channel_scale = jnp.exp(jax.random.uniform(jax.random.fold_in(key, salt_value), (HK * DK,), jnp.float32, math.log(0.02), 0.0))
    tap_values = 0.5 * jax.random.normal(jax.random.fold_in(key, salt_value + 1), (KCONV, HK * DK), jnp.float32)
    return jnp.clip(tap_values * channel_scale[None, :], -2.0, 2.0).astype(jnp.bfloat16)


def draw_conv_query(key, part):
    return convolution_taps(key, 31)


def draw_conv_key(key, part):
    return convolution_taps(key, 41)


def draw_dt_bias(key, part):
    lowest = math.log(1.0 / (16.0 * TOKENS))
    slow_share = 0.5
    slow_mask = jax.random.bernoulli(jax.random.fold_in(key, 21), slow_share, (HV,))
    slow_value = lowest + jax.random.uniform(jax.random.fold_in(key, 22), (HV,), jnp.float32, 0.0, 2.0)
    fast_value = jax.random.uniform(jax.random.fold_in(key, 23), (HV,), jnp.float32, -4.5, -3.0)
    return jnp.where(slow_mask, slow_value, fast_value).astype(jnp.float32)


def block_scale(rng, dims, split, least, largest):
    loudness = 1.0
    for axis_at, shards_of in split:
        steps = jax.random.uniform(jax.random.fold_in(jax.random.fold_in(rng, 6), axis_at), (shards_of,), jnp.float32, least / len(split), largest / len(split))
        loudness = loudness * jnp.repeat(jnp.exp(steps), dims[axis_at] // shards_of).reshape((-1,) + (1,) * (len(dims) - 1 - axis_at))
    return loudness


def gaussian(stream_key, dims, width, limit, cuts=(), held_as=jnp.bfloat16):
    entries = width * jax.random.normal(stream_key, dims, jnp.float32)
    if cuts:
        entries = entries * block_scale(stream_key, dims, cuts, -0.22, 0.18)
    return jnp.clip(entries, -limit, limit).astype(held_as)


def setup_inputs(seed: int = 0) -> dict:
    keys = jax.random.split(jax.random.key(seed), 11)
    return {
        "hidden_states": draw_hidden_states(jax.random.fold_in(keys[10], 71), 0),
        "proj_ba": draw_proj_ba(jax.random.fold_in(keys[10], 71), 0),
        "query_in": gaussian(keys[2], (TOKENS, HK * DK), 1.0, 6.0, ((0, 8), (1, 4))),
        "key_in": gaussian(keys[3], (TOKENS, HK * DK), 1.0, 6.0, ((0, 8), (1, 4))),
        "value_in": gaussian(keys[4], (TOKENS, HV * DV), 1.0, 6.0, ((0, 8), (1, 4))),
        "conv_query": draw_conv_query(jax.random.fold_in(keys[10], 71), 0),
        "conv_key": draw_conv_key(jax.random.fold_in(keys[10], 71), 0),
        "convolution_value_taps": gaussian(keys[7], (KCONV, HV * DV), 0.5, 2.5, ((1, 4),)),
        "decay_scale": jnp.clip(jnp.exp(math.log(16.0) - 2.7725887 * jax.random.uniform(keys[8], (HV,), jnp.float32) ** block_scale(keys[8], (HV,), ((0, 4),), -0.2, 0.2)), 1.0, 16.0),
        "dt_bias": draw_dt_bias(jax.random.fold_in(keys[10], 71), 0),
    }


highest = lax.Precision.HIGHEST

def causal_conv(inputs, weights):
    padded = jnp.pad(inputs.astype(jnp.float32), ((KCONV - 1, 0), (0, 0)))
    length = inputs.shape[0]
    kernel = weights.astype(jnp.float32)
    summed = jnp.zeros((length, inputs.shape[1]), jnp.float32)
    for offset in range(KCONV):
        summed = summed + kernel[offset][None, :] * lax.slice_in_dim(padded, offset, offset + length, axis=0)
    return jax.nn.silu(summed)

def unit_norm(features, factor):
    return features * lax.rsqrt(lax.optimization_barrier(jnp.sum(features * features, axis=-1, keepdims=True)) + 1e-06) * factor

def block_terms(queries, key_rows, values, log_decay, write_rate):
    block_length = queries.shape[-2]
    cumulative = jnp.cumsum(log_decay, axis=-1)
    row_index = lax.broadcasted_iota(jnp.int32, (block_length, block_length), 0)
    column_index = lax.broadcasted_iota(jnp.int32, (block_length, block_length), 1)
    causal = row_index >= column_index
    strict = row_index > column_index
    spread = cumulative[..., :, None] - cumulative[..., None, :]
    decay_table = jnp.where(causal, jnp.exp(jnp.where(causal, spread, 0.0)), 0.0)
    key_dots = jnp.einsum('...td,...sd->...ts', key_rows, key_rows, precision=highest)
    lower_part = jnp.where(strict, write_rate[..., :, None] * decay_table * key_dots, 0.0)
    system = lower_part + jnp.eye(block_length, dtype=jnp.float32)
    growth = jnp.exp(cumulative)
    stacked = jnp.concatenate([write_rate[..., None] * values, (write_rate * growth)[..., None] * key_rows], axis=-1)
    solved = jax.scipy.linalg.solve_triangular(system, stacked, lower=True, unit_diagonal=True)
    value_width = values.shape[-1]
    update_value = solved[..., :value_width]
    update_key = solved[..., value_width:]
    query_dots = jnp.einsum('...td,...sd->...ts', queries, key_rows, precision=highest)
    attend = jnp.where(causal, query_dots * decay_table, 0.0)
    scaled_query = growth[..., None] * queries
    tail_keys = jnp.exp(cumulative[..., -1:] - cumulative)[..., None] * key_rows
    end_decay = growth[..., -1]
    return (scaled_query, attend, update_value, update_key, tail_keys, end_decay)

def reference(hidden_states, proj_ba, query_in, key_in, value_in, conv_query, conv_key, convolution_value_taps, decay_scale, dt_bias):
    logits = jnp.dot(hidden_states.astype(jnp.float32), proj_ba.astype(jnp.float32), preferred_element_type=jnp.float32)
    log_decay = -decay_scale[None, :] * jax.nn.softplus(logits[:, 0::2] + dt_bias[None, :])
    write_rate = jax.nn.sigmoid(logits[:, 1::2])
    group_size = HV // HK
    block_count = TOKENS // BLOCK
    query_scale = 1.0 / math.sqrt(DK)

    def one_head(head_index):
        key_start = head_index // group_size * DK
        value_start = head_index * DV
        query_cols = lax.dynamic_slice_in_dim(query_in, key_start, DK, 1)
        key_cols = lax.dynamic_slice_in_dim(key_in, key_start, DK, 1)
        value_cols = lax.dynamic_slice_in_dim(value_in, value_start, DV, 1)
        query_taps = lax.dynamic_slice_in_dim(conv_query, key_start, DK, 1)
        key_taps = lax.dynamic_slice_in_dim(conv_key, key_start, DK, 1)
        value_taps = lax.dynamic_slice_in_dim(convolution_value_taps, value_start, DV, 1)
        unit_query = unit_norm(causal_conv(query_cols, query_taps), query_scale)
        unit_keys = unit_norm(causal_conv(key_cols, key_taps), 1.0)
        mixed_values = causal_conv(value_cols, value_taps)
        decay_col = lax.dynamic_slice_in_dim(log_decay, head_index, 1, 1)[:, 0]
        rate_col = lax.dynamic_slice_in_dim(write_rate, head_index, 1, 1)[:, 0]
        pieces = block_terms(unit_query.reshape(block_count, BLOCK, DK), unit_keys.reshape(block_count, BLOCK, DK), mixed_values.reshape(block_count, BLOCK, DV), decay_col.reshape(block_count, BLOCK), rate_col.reshape(block_count, BLOCK))

        def block_step(state_now, piece_set):
            query_part, attend_part, value_part, key_part, tail_part, end_part = piece_set
            errors = value_part - jnp.dot(key_part, state_now, precision=highest)
            produced = jnp.dot(query_part, state_now, precision=highest) + jnp.dot(attend_part, errors, precision=highest)
            next_state = end_part * state_now + jnp.dot(tail_part.T, errors, precision=highest)
            return (next_state, produced)
        initial = jnp.zeros((DK, DV), jnp.float32)
        unused, produced = lax.scan(block_step, initial, pieces)
        return produced.reshape(TOKENS, DV)
    stacked = lax.map(one_head, jnp.arange(HV, dtype=jnp.int32))
    return jnp.transpose(stacked, (1, 0, 2)).reshape(TOKENS, HV * DV)
```

```python
import functools
import math

import jax
import jax.numpy as jnp
from jax import lax
from jax.experimental import pallas as pl
from jax.experimental.pallas import tpu as pltpu
from jax.sharding import PartitionSpec as P

DK = 128
DV = 128
KCONV = 4
BLOCK = 128
SUB = 16
EDGE = 16

f32 = jnp.float32
bf16 = jnp.bfloat16
VMEM = pltpu.VMEM
FAR = -1e30


def split(x):
    hi = x.astype(bf16)
    return hi, (x - hi.astype(f32)).astype(bf16)


def dot_split(a, b, contract=((1,), (0,))):
    (ah, al), (bh, bl) = a, b
    (ca,), (cb,) = contract
    left = jnp.concatenate([ah, al, ah], axis=ca)
    right = jnp.concatenate([bh, bh, bl], axis=cb)
    return lax.dot_general(left, right, (contract, ((), ())), preferred_element_type=f32)


NN = ((1,), (0,))
NT = ((1,), (1,))
TN = ((0,), (0,))


def silu(x):
    return x / (1.0 + jnp.exp(-x))


def unit(x, factor=1.0):
    return x * (lax.rsqrt(jnp.sum(x * x, axis=-1, keepdims=True) + 1e-6) * factor)


def conv_rows(padded_ref, taps, rows, columns):
    total = taps[0:1] * padded_ref[pl.ds(8 - KCONV + 1, rows), columns]
    for j in range(1, KCONV):
        total = total + taps[j : j + 1] * padded_ref[pl.ds(8 - KCONV + 1 + j, rows), columns]
    return silu(total)


def iotas(rows=BLOCK, columns=BLOCK):
    return (
        lax.broadcasted_iota(jnp.int32, (rows, columns), 0),
        lax.broadcasted_iota(jnp.int32, (rows, columns), 1),
    )


def lanes(start, size):
    return pl.ds(pl.multiple_of(start, 128), size)


def logits_kernel(head_count, hidden_ref, proj_ref, q_ref, k_ref, v_ref, *refs):
    outs, tail_ref, held = refs[:head_count], refs[head_count], refs[head_count + 1]
    rows = proj_ref.shape[1] // head_count
    everything = lax.dot_general(
        proj_ref[...], hidden_ref[...], (((0,), (1,)), ((), ())), preferred_element_type=f32
    )
    for m in range(head_count):
        held[m] = everything[m * rows : (m + 1) * rows]
    me = lax.axis_index("head")
    for d in range(head_count):
        outs[d][...] = held[me ^ d]
    dk = q_ref.shape[1]
    tail_ref[:, 0:dk] = q_ref[...]
    tail_ref[:, dk : 2 * dk] = k_ref[...]
    tail_ref[:, 2 * dk :] = v_ref[...]


def mix_kernel(k_ref, v_ref, kt_ref, vt_ref, unit_ref, dots_ref, mixed_ref, padded):
    tokens = k_ref.shape[0]
    padded[0:8] = jnp.zeros((8, padded.shape[1]), f32)
    padded[8:, 0:DK] = k_ref[...].astype(f32)
    padded[8:, DK:] = v_ref[...].astype(f32)
    key_taps = kt_ref[...].astype(f32)
    value_taps = vt_ref[...].astype(f32)
    keys = unit(conv_rows(padded, key_taps, tokens, slice(0, DK)))
    unit_ref[0] = keys
    for c in range(tokens // BLOCK):
        part = split(keys[c * BLOCK : (c + 1) * BLOCK])
        dots_ref[0, c] = dot_split(part, part, NT)
    mixed_ref[0] = conv_rows(padded, value_taps, tokens, slice(DK, None))


def softplus(u):
    e = jnp.exp(-jnp.abs(u))
    small = e * (1.0 - e * (0.5 - e * (1.0 / 3.0 - e * (0.25 - e * 0.2))))
    return jnp.maximum(u, 0.0) + jnp.where(e < 0.03, small, jnp.log(1.0 + e))


def invert_all(lowers):
    count = len(lowers)
    row, column = iotas()
    blocks = (row // SUB) == (column // SUB)
    folded = []
    for lower in lowers:
        kept = jnp.where(blocks, lower, 0.0)
        total = kept[0:SUB]
        for b in range(1, BLOCK // SUB):
            total = total + kept[b * SUB : (b + 1) * SUB]
        folded.append(total)
    spread = jnp.concatenate(split(jnp.concatenate(folded, axis=0)), axis=1)
    pick = [
        jnp.where(row == (column // SUB) * SUB + j, 1.0, 0.0).astype(bf16) for j in range(SUB - 1)
    ]
    pick = jnp.concatenate(pick, axis=1)
    pick = jnp.concatenate([pick, pick], axis=0)
    wide = jnp.dot(spread, pick, preferred_element_type=f32).reshape(
        count, SUB, (SUB - 1) * BLOCK
    )
    srow, scolumn = iotas(SUB, BLOCK)
    inverse = jnp.broadcast_to(
        jnp.where(srow == scolumn % SUB, 1.0, 0.0)[None], (count, SUB, BLOCK)
    )
    for j in range(SUB - 1):
        inverse = inverse - wide[:, :, j * BLOCK : (j + 1) * BLOCK] * inverse[:, j : j + 1, :]
    full = [
        jnp.where(blocks, jnp.concatenate([inverse[i]] * (BLOCK // SUB), axis=0), 0.0)
        for i in range(count)
    ]
    size = SUB
    while size < BLOCK:
        across = ((row // (2 * size)) == (column // (2 * size))) & ((row // size) > (column // size))
        halves = [split(x) for x in full]
        first = [
            dot_split(halves[i], split(jnp.where(across, lowers[i], 0.0))) for i in range(count)
        ]
        full = [full[i] - dot_split(split(first[i]), halves[i]) for i in range(count)]
        size *= 2
    return full


def solve_kernel(
    slots,
    group,
    pieces,
    scale_ref,
    bias_ref,
    *refs,
):
    logit_refs, refs = refs[:pieces], refs[pieces:]
    (unit_ref, dots_ref, mixed_ref, k_ref, v_ref, before_ref, kt_ref, vt_ref), refs = (
        refs[:8],
        refs[8:],
    )
    count = len(slots)
    message_refs, refs = refs[:count], refs[count:]
    solved_ref, moves_ref, cumulative_ref, first_ref, padded = refs
    tokens = unit_ref.shape[1]
    blocks = tokens // BLOCK
    key_width = kt_ref.shape[1]
    place = lax.axis_index("seq") % group
    row, column = iotas()
    upper = jnp.where(row <= column, 1.0, 0.0)
    identity = row == column
    strict = row > column

    systems, rights, tails, ends, key_parts = [], [], [], [], []
    for at, s in enumerate(slots):
        p = place ^ (group - 1 - s)
        kcol, vcol = p * DK, p * 2 * DV
        padded[0:8, 0:DK] = before_ref[:, lanes(key_width + kcol, DK)].astype(f32)[EDGE - 8 :]
        padded[0:8, DK:] = before_ref[:, lanes(2 * key_width + vcol, 2 * DV)].astype(f32)[EDGE - 8 :]
        padded[8:, 0:DK] = k_ref[:, lanes(kcol, DK)].astype(f32)
        padded[8:, DK:] = v_ref[:, lanes(vcol, 2 * DV)].astype(f32)
        key_taps = kt_ref[:, lanes(kcol, DK)].astype(f32)
        value_taps = vt_ref[:, lanes(vcol, 2 * DV)].astype(f32)
        edge_keys = unit(conv_rows(padded, key_taps, EDGE, slice(0, DK)))
        edge_values = conv_rows(padded, value_taps, EDGE, slice(DK, None))
        decays, rates = [], []
        for b in range(2):
            h = 2 * p + b
            u = logit_refs[0][pl.ds(2 * h, 1), :]
            w = logit_refs[0][pl.ds(2 * h + 1, 1), :]
            for ref in logit_refs[1:]:
                u = u + ref[pl.ds(2 * h, 1), :]
                w = w + ref[pl.ds(2 * h + 1, 1), :]
            decays.append(-scale_ref[h] * softplus(u + bias_ref[h]))
            rates.append(1.0 / (1.0 + jnp.exp(-w)))
        decay_rows = jnp.concatenate(
            [d[:, c * BLOCK : (c + 1) * BLOCK] for d in decays for c in range(blocks)], axis=0
        )
        rate_rows = jnp.concatenate(
            [r[:, c * BLOCK : (c + 1) * BLOCK] for r in rates for c in range(blocks)], axis=0
        )
        sums = jnp.dot(
            decay_rows, upper, precision=lax.Precision.HIGHEST, preferred_element_type=f32
        )
        cumulative_ref[at] = sums
        cum_columns = jnp.transpose(sums)
        rate_columns = jnp.transpose(rate_rows)
        growth_columns = jnp.exp(cum_columns)
        last = sums[:, BLOCK - 1 : BLOCK]
        tail_columns = jnp.exp(jnp.transpose(last - sums))
        end_values = jnp.exp(last)
        for c in range(blocks):
            keys = unit_ref[p, pl.ds(c * BLOCK, BLOCK), :]
            values = mixed_ref[p, pl.ds(c * BLOCK, BLOCK), :]
            if c == 0:
                keys = jnp.concatenate([edge_keys, keys[EDGE:]], axis=0)
                values = jnp.concatenate([edge_values, values[EDGE:]], axis=0)
                first_ref[at] = keys
            parts = split(keys)
            key_parts.append(parts)
            dots = dot_split(parts, parts, NT) if c == 0 else dots_ref[p, c]
            for b in range(2):
                r = b * blocks + c
                rate = rate_columns[:, r : r + 1]
                spread = cum_columns[:, r : r + 1] - sums[r : r + 1, :]
                table = jnp.exp(jnp.where(strict, spread, FAR))
                systems.append(rate * table * dots)
                rights.append(
                    jnp.concatenate(
                        [
                            rate * values[:, b * DV : (b + 1) * DV],
                            (rate * growth_columns[:, r : r + 1]) * keys,
                        ],
                        axis=1,
                    )
                )
                tails.append(tail_columns[:, r : r + 1])
                ends.append(end_values[r : r + 1, :])

    inverses = invert_all(systems)
    solved = [dot_split(split(x), split(r)) for x, r in zip(inverses, rights)]
    for at in range(count):
        moves = {}
        for c in range(blocks):
            i = (at * blocks + c) * 2
            both = jnp.concatenate([tails[i] * solved[i], tails[i + 1] * solved[i + 1]], axis=1)
            grown = dot_split(key_parts[at * blocks + c], split(both), TN)
            for b in range(2):
                solved_ref[at, b, pl.ds(c * BLOCK, BLOCK), :] = solved[i + b]
                added = grown[:, b * 2 * DK : b * 2 * DK + DV]
                move = (
                    jnp.where(identity, ends[i + b], 0.0)
                    - grown[:, b * 2 * DK + DV : (b + 1) * 2 * DK]
                )
                moves[b, c] = (added, move)
                if c < blocks - 1:
                    moves_ref[at, b, c, :, 0:DV] = added
                    moves_ref[at, b, c, :, DV:] = move
        for b in range(2):
            added, move = moves[b, 0]
            both = jnp.concatenate([added, move], axis=1)
            for c in range(1, blocks):
                added, move = moves[b, c]
                both = dot_split(split(move), split(both))
                both = jnp.concatenate([both[:, :DV] + added, both[:, DV:]], axis=1)
            message_refs[at][b] = both


def query_kernel(
    group, q_ref, before_ref, qt_ref, unit_ref, first_ref, cumulative_ref, solved_ref, out_ref, padded
):
    s = pl.program_id(0)
    place = lax.axis_index("seq") % group
    p = place ^ (group - 1 - s)
    tokens = q_ref.shape[0]
    blocks = tokens // BLOCK
    columns = lanes(p * DK, DK)
    padded[0:8] = before_ref[:, columns].astype(f32)[EDGE - 8 :]
    padded[8:] = q_ref[:, columns].astype(f32)
    taps = qt_ref[:, columns].astype(f32)
    queries = unit(conv_rows(padded, taps, tokens, slice(None)), 1.0 / math.sqrt(DK))
    row, column = iotas()
    causal = row >= column
    sums = cumulative_ref[0]
    cum_columns = jnp.transpose(sums)
    growth_columns = jnp.exp(cum_columns)
    for c in range(blocks):
        here = queries[c * BLOCK : (c + 1) * BLOCK]
        keys = first_ref[0] if c == 0 else unit_ref[p, pl.ds(c * BLOCK, BLOCK), :]
        dots = dot_split(split(here), split(keys), NT)
        for b in range(2):
            r = b * blocks + c
            spread = cum_columns[:, r : r + 1] - sums[r : r + 1, :]
            attend = dots * jnp.exp(jnp.where(causal, spread, FAR))
            seen = dot_split(split(attend), split(solved_ref[0, b, pl.ds(c * BLOCK, BLOCK), :]))
            out_ref[0, b, pl.ds(c * BLOCK, BLOCK), 0:DV] = seen[:, :DV]
            out_ref[0, b, pl.ds(c * BLOCK, BLOCK), DV:] = (
                growth_columns[:, r : r + 1] * here - seen[:, DV:]
            )


def prefix_kernel(group, entering_ref, *refs):
    messages, refs = refs[:group], refs[group:]
    outs, refs = refs[: group + 1], refs[group + 1 :]
    held, sems = refs
    place = lax.axis_index("seq") % group
    copies = [
        pltpu.make_async_copy(messages[d], held.at[place ^ d], sems.at[d]) for d in range(group)
    ]
    for copy in copies:
        copy.start()
    for copy in copies:
        copy.wait()
    heads = entering_ref.shape[0]
    states = [entering_ref[b] for b in range(heads)]
    chain = []
    for i in range(group):
        chain.append(states)
        states = [
            held[i, b, :, 0:DV] + dot_split(split(held[i, b, :, DV:]), split(states[b]))
            for b in range(heads)
        ]
    for b in range(heads):
        outs[group][b] = states[b]
    for j in range(group):

        @pl.when(place == j)
        def _():
            for i in range(group):
                for b in range(heads):
                    outs[j ^ i][b] = chain[i][b]


def output_kernel(group, reads_ref, moves_ref, *refs):
    entering, (out_ref,) = refs[:group], refs[group:]
    place = lax.axis_index("seq") % group
    tokens = out_ref.shape[0]
    blocks = tokens // BLOCK
    for s in range(group):
        p = place ^ (group - 1 - s)
        for b in range(2):
            state = entering[group - 1 - s][b]
            for c in range(blocks):
                reads = reads_ref[s, b, pl.ds(c * BLOCK, BLOCK), DV:]
                if c < blocks - 1:
                    reads = jnp.concatenate([reads, moves_ref[s, b, c, :, DV:]], axis=0)
                product = dot_split(split(reads), split(state))
                out_ref[pl.ds(c * BLOCK, BLOCK), lanes(p * 2 * DV + b * DV, DV)] = (
                    reads_ref[s, b, pl.ds(c * BLOCK, BLOCK), 0:DV] + product[:BLOCK]
                )
                if c < blocks - 1:
                    state = moves_ref[s, b, c, :, 0:DV] + product[BLOCK:]


def shape(*dims, dtype=f32):
    return jax.ShapeDtypeStruct(dims, dtype)


def params(mib=56):
    return pltpu.CompilerParams(vmem_limit_bytes=mib << 20)


def whole(space=VMEM):
    return pl.BlockSpec(memory_space=space)


def per_device(
    hidden_states,
    proj_ba,
    query_in,
    key_in,
    value_in,
    conv_query,
    conv_key,
    convolution_value_taps,
    decay_scale,
    dt_bias,
):
    tokens = hidden_states.shape[0]
    heads = decay_scale.shape[0]
    pairs = key_in.shape[1] // DK
    blocks = tokens // BLOCK
    key_width, value_width = key_in.shape[1], value_in.shape[1]
    seq, head_count = lax.axis_size("seq"), lax.axis_size("head")
    group = pairs

    def full(block):
        return pl.BlockSpec(block, lambda i: (0,) * len(block))

    last_rows = tokens // EDGE - 1
    *partial, tail = pl.pallas_call(
        functools.partial(logits_kernel, head_count),
        grid=(1,),
        in_specs=[
            full(hidden_states.shape),
            full(proj_ba.shape),
            pl.BlockSpec((EDGE, key_width), lambda i: (last_rows, 0)),
            pl.BlockSpec((EDGE, key_width), lambda i: (last_rows, 0)),
            pl.BlockSpec((EDGE, value_width), lambda i: (last_rows, 0)),
        ],
        out_specs=[full((2 * heads, tokens))] * head_count
        + [full((EDGE, 2 * key_width + value_width))],
        out_shape=[shape(2 * heads, tokens)] * head_count
        + [shape(EDGE, 2 * key_width + value_width, dtype=bf16)],
        scratch_shapes=[VMEM((head_count, 2 * heads, tokens), f32)],
        compiler_params=params(),
        name="logits",
    )(hidden_states, proj_ba, query_in, key_in, value_in)

    logits = [partial[0]] + [
        lax.ppermute(partial[d], "head", [(i, i ^ d) for i in range(head_count)])
        for d in range(1, head_count)
    ]
    before = lax.ppermute(tail, "seq", [(i, i + 1) for i in range(seq - 1)])

    unit_keys, key_dots, mixed = pl.pallas_call(
        mix_kernel,
        grid=(pairs,),
        in_specs=[
            pl.BlockSpec((tokens, DK), lambda i: (0, i)),
            pl.BlockSpec((tokens, 2 * DV), lambda i: (0, i)),
            pl.BlockSpec((KCONV, DK), lambda i: (0, i)),
            pl.BlockSpec((KCONV, 2 * DV), lambda i: (0, i)),
        ],
        out_specs=[
            pl.BlockSpec((1, tokens, DK), lambda i: (i, 0, 0)),
            pl.BlockSpec((1, blocks, BLOCK, BLOCK), lambda i: (i, 0, 0, 0)),
            pl.BlockSpec((1, tokens, 2 * DV), lambda i: (i, 0, 0)),
        ],
        out_shape=[
            shape(pairs, tokens, DK),
            shape(pairs, blocks, BLOCK, BLOCK),
            shape(pairs, tokens, 2 * DV),
        ],
        scratch_shapes=[VMEM((tokens + 8, DK + 2 * DV), f32)],
        compiler_params=params(),
        cost_estimate=pl.CostEstimate(
            flops=4_000_000_000, bytes_accessed=6_000_000, transcendentals=0
        ),
        name="mix",
    )(key_in, value_in, conv_key, convolution_value_taps)

    def solve(slots):
        count = len(slots)
        return pl.pallas_call(
            functools.partial(solve_kernel, slots, group, head_count),
            grid=(1,),
            in_specs=[whole(pltpu.SMEM)] * 2
            + [whole()] * (head_count + 3)
            + [
                pl.BlockSpec((EDGE, key_width), lambda i: (0, 0)),
                pl.BlockSpec((EDGE, value_width), lambda i: (0, 0)),
            ]
            + [whole()] * 3,
            out_specs=[whole()] * (count + 4),
            out_shape=[shape(2, DK, 2 * DK)] * count
            + [
                shape(count, 2, tokens, 2 * DK),
                shape(count, 2, blocks - 1, DK, 2 * DK),
                shape(count, 2 * blocks, BLOCK),
                shape(count, BLOCK, DK),
            ],
            scratch_shapes=[VMEM((EDGE + 8, DK + 2 * DV), f32)],
            compiler_params=params(),
            cost_estimate=pl.CostEstimate(
                flops=4_000_000_000 * count, bytes_accessed=4_000_000 * count, transcendentals=0
            ),
            name="solve",
        )(
            decay_scale,
            dt_bias,
            *logits,
            unit_keys,
            key_dots,
            mixed,
            key_in,
            value_in,
            before,
            conv_key,
            convolution_value_taps,
        )

    *messages, solved, moves, cumulative, first_keys = solve(tuple(range(group)))

    arrived = [messages[group - 1]]
    for d in range(1, group):
        arrived.append(
            lax.ppermute(messages[group - 1 - d], "seq", [(i, i ^ d) for i in range(seq)])
        )

    reads = pl.pallas_call(
        functools.partial(query_kernel, group),
        grid=(pairs,),
        in_specs=[
            full(query_in.shape),
            full(tail.shape),
            full(conv_query.shape),
            full(unit_keys.shape),
            pl.BlockSpec((1, BLOCK, DK), lambda i: (i, 0, 0)),
            pl.BlockSpec((1, 2 * blocks, BLOCK), lambda i: (i, 0, 0)),
            pl.BlockSpec((1, 2, tokens, 2 * DK), lambda i: (i, 0, 0, 0)),
        ],
        out_specs=pl.BlockSpec((1, 2, tokens, 2 * DK), lambda i: (i, 0, 0, 0)),
        out_shape=shape(pairs, 2, tokens, 2 * DK),
        scratch_shapes=[VMEM((tokens + 8, DK), f32)],
        compiler_params=params(),
        cost_estimate=pl.CostEstimate(
            flops=4_000_000_000, bytes_accessed=8_000_000, transcendentals=0
        ),
        name="query",
    )(query_in, before, conv_query, unit_keys, first_keys, cumulative, solved)

    prefix = pl.pallas_call(
        functools.partial(prefix_kernel, group),
        in_specs=[whole()] + [whole(pl.ANY)] * group,
        out_specs=[whole()] * (group + 1),
        out_shape=[shape(2, DK, DV)] * (group + 1),
        scratch_shapes=[VMEM((group, 2, DK, 2 * DK), f32), pltpu.SemaphoreType.DMA((group,))],
        compiler_params=params(),
        name="prefix",
    )
    *entering, leaving = prefix(jnp.zeros((2, DK, DV), f32), *arrived)
    for _ in range(seq // group - 1):
        received = lax.ppermute(leaving, "seq", [(i, i + group) for i in range(seq - group)])
        *entering, leaving = prefix(received, *arrived)

    states = [entering[0]] + [
        lax.ppermute(entering[d], "seq", [(i, i ^ d) for i in range(seq)]) for d in range(1, group)
    ]
    return pl.pallas_call(
        functools.partial(output_kernel, group),
        in_specs=[whole()] * (2 + group),
        out_specs=whole(),
        out_shape=shape(tokens, value_width),
        compiler_params=params(),
        name="outputs",
    )(reads, moves, *states)


def solution(mesh):
    placed = (
        P("seq", "head"),
        P("head", None),
        P("seq", "head"),
        P("seq", "head"),
        P("seq", "head"),
        P(None, "head"),
        P(None, "head"),
        P(None, "head"),
        P("head"),
        P("head"),
    )
    return jax.shard_map(
        per_device, mesh=mesh, in_specs=placed, out_specs=P("seq", "head"), check_vma=False
    )
```

```python
import functools
import math

import jax
import jax.numpy as jnp
from jax import lax
from jax.experimental import pallas as pl
from jax.experimental.pallas import tpu as pltpu
from jax.sharding import PartitionSpec as P

DK = 128
DV = 128
KCONV = 4
BLOCK = 128
SUB = 16
EDGE = 16

f32 = jnp.float32
bf16 = jnp.bfloat16
VMEM = pltpu.VMEM
FAR = -1e30


def split(x):
    hi = x.astype(bf16)
    return hi, (x - hi.astype(f32)).astype(bf16)


def dot_split(a, b, contract=((1,), (0,))):
    (ah, al), (bh, bl) = a, b
    (ca,), (cb,) = contract
    left = jnp.concatenate([ah, al, ah], axis=ca)
    right = jnp.concatenate([bh, bh, bl], axis=cb)
    return lax.dot_general(left, right, (contract, ((), ())), preferred_element_type=f32)


NN = ((1,), (0,))
NT = ((1,), (1,))
TN = ((0,), (0,))


def silu(x):
    return x / (1.0 + jnp.exp(-x))


def unit(x, factor=1.0):
    return x * (lax.rsqrt(jnp.sum(x * x, axis=-1, keepdims=True) + 1e-6) * factor)


def conv_rows(padded_ref, taps, rows, columns):
    total = taps[0:1] * padded_ref[pl.ds(8 - KCONV + 1, rows), columns]
    for j in range(1, KCONV):
        total = total + taps[j : j + 1] * padded_ref[pl.ds(8 - KCONV + 1 + j, rows), columns]
    return silu(total)


def iotas(rows=BLOCK, columns=BLOCK):
    return (
        lax.broadcasted_iota(jnp.int32, (rows, columns), 0),
        lax.broadcasted_iota(jnp.int32, (rows, columns), 1),
    )


def slot_partner(group, slot):
    order = [d for d in range(group - 1, 0, -1) if d % 2] + [
        d for d in range(group - 1, 0, -1) if d % 2 == 0
    ]
    return (order + [0])[slot]


def solve_calls(group):
    half = group // 2
    return [tuple(range(half))] + [(s,) for s in range(half, group)]


def in_hbm(x):
    return pltpu.with_memory_space_constraint(x, pltpu.HBM)


def lanes(start, size):
    return pl.ds(pl.multiple_of(start, 128), size)


def logits_kernel(head_count, hidden_ref, proj_ref, q_ref, k_ref, v_ref, *refs):
    outs, tail_ref, held = refs[:head_count], refs[head_count], refs[head_count + 1]
    rows = proj_ref.shape[0] // head_count
    everything = lax.dot_general(
        proj_ref[...], hidden_ref[...], (NT, ((), ())), preferred_element_type=f32
    )
    for m in range(head_count):
        held[m] = everything[m * rows : (m + 1) * rows]
    me = lax.axis_index("head")
    for d in range(head_count):
        outs[d][...] = held[me ^ d]
    dk = q_ref.shape[1]
    tail_ref[:, 0:dk] = q_ref[...]
    tail_ref[:, dk : 2 * dk] = k_ref[...]
    tail_ref[:, 2 * dk :] = v_ref[...]


def mix_kernel(k_ref, v_ref, kt_ref, vt_ref, unit_ref, dots_ref, mixed_ref, padded):
    tokens = k_ref.shape[0]
    padded[0:8] = jnp.zeros((8, padded.shape[1]), f32)
    padded[8:, 0:DK] = k_ref[...].astype(f32)
    padded[8:, DK:] = v_ref[...].astype(f32)
    key_taps = kt_ref[...].astype(f32)
    value_taps = vt_ref[...].astype(f32)
    keys = unit(conv_rows(padded, key_taps, tokens, slice(0, DK)))
    unit_ref[0] = keys
    for c in range(tokens // BLOCK):
        part = split(keys[c * BLOCK : (c + 1) * BLOCK])
        dots_ref[0, c] = dot_split(part, part, NT)
    mixed_ref[0] = conv_rows(padded, value_taps, tokens, slice(DK, None))


def softplus(u):
    e = jnp.exp(-jnp.abs(u))
    small = e * (1.0 - e * (0.5 - e * (1.0 / 3.0 - e * (0.25 - e * 0.2))))
    return jnp.maximum(u, 0.0) + jnp.where(e < 0.03, small, jnp.log(1.0 + e))


def invert_all(lowers):
    count = len(lowers)
    row, column = iotas()
    blocks = (row // SUB) == (column // SUB)
    folded = []
    for lower in lowers:
        kept = jnp.where(blocks, lower, 0.0)
        total = kept[0:SUB]
        for b in range(1, BLOCK // SUB):
            total = total + kept[b * SUB : (b + 1) * SUB]
        folded.append(total)
    spread = jnp.concatenate(split(jnp.concatenate(folded, axis=0)), axis=1)
    pick = [
        jnp.where(row == (column // SUB) * SUB + j, 1.0, 0.0).astype(bf16) for j in range(SUB - 1)
    ]
    pick = jnp.concatenate(pick, axis=1)
    pick = jnp.concatenate([pick, pick], axis=0)
    wide = jnp.dot(spread, pick, preferred_element_type=f32).reshape(
        count, SUB, (SUB - 1) * BLOCK
    )
    srow, scolumn = iotas(SUB, BLOCK)
    inverse = jnp.broadcast_to(
        jnp.where(srow == scolumn % SUB, 1.0, 0.0)[None], (count, SUB, BLOCK)
    )
    for j in range(SUB - 1):
        inverse = inverse - wide[:, :, j * BLOCK : (j + 1) * BLOCK] * inverse[:, j : j + 1, :]
    full = [
        jnp.where(blocks, jnp.concatenate([inverse[i]] * (BLOCK // SUB), axis=0), 0.0)
        for i in range(count)
    ]
    size = SUB
    while size < BLOCK:
        across = ((row // (2 * size)) == (column // (2 * size))) & ((row // size) > (column // size))
        halves = [split(x) for x in full]
        first = [
            dot_split(halves[i], split(jnp.where(across, lowers[i], 0.0))) for i in range(count)
        ]
        full = [full[i] - dot_split(split(first[i]), halves[i]) for i in range(count)]
        size *= 2
    return full


def solve_kernel(
    slots,
    group,
    pieces,
    scale_ref,
    bias_ref,
    *refs,
):
    logit_refs, refs = refs[:pieces], refs[pieces:]
    (unit_ref, dots_ref, mixed_ref, k_ref, v_ref, before_ref, kt_ref, vt_ref), refs = (
        refs[:8],
        refs[8:],
    )
    count = len(slots)
    message_refs, refs = refs[:count], refs[count:]
    solved_ref, starts_ref, cumulative_ref, first_ref, padded = refs
    tokens = unit_ref.shape[1]
    blocks = tokens // BLOCK
    key_width = kt_ref.shape[1]
    place = lax.axis_index("seq") % group
    row, column = iotas()
    upper = jnp.where(row <= column, 1.0, 0.0)
    identity = row == column
    strict = row > column

    systems, rights, tails, ends, key_parts = [], [], [], [], []
    for at, s in enumerate(slots):
        p = place ^ slot_partner(group, s)
        kcol, vcol = p * DK, p * 2 * DV
        padded[0:8, 0:DK] = before_ref[:, lanes(key_width + kcol, DK)].astype(f32)[EDGE - 8 :]
        padded[0:8, DK:] = before_ref[:, lanes(2 * key_width + vcol, 2 * DV)].astype(f32)[EDGE - 8 :]
        padded[8:, 0:DK] = k_ref[:, lanes(kcol, DK)].astype(f32)
        padded[8:, DK:] = v_ref[:, lanes(vcol, 2 * DV)].astype(f32)
        key_taps = kt_ref[:, lanes(kcol, DK)].astype(f32)
        value_taps = vt_ref[:, lanes(vcol, 2 * DV)].astype(f32)
        edge_keys = unit(conv_rows(padded, key_taps, EDGE, slice(0, DK)))
        edge_values = conv_rows(padded, value_taps, EDGE, slice(DK, None))
        decays, rates = [], []
        for b in range(2):
            h = 2 * p + b
            u = logit_refs[0][pl.ds(2 * h, 1), :]
            w = logit_refs[0][pl.ds(2 * h + 1, 1), :]
            for ref in logit_refs[1:]:
                u = u + ref[pl.ds(2 * h, 1), :]
                w = w + ref[pl.ds(2 * h + 1, 1), :]
            decays.append(-scale_ref[h] * softplus(u + bias_ref[h]))
            rates.append(1.0 / (1.0 + jnp.exp(-w)))
        decay_rows = jnp.concatenate(
            [d[:, c * BLOCK : (c + 1) * BLOCK] for d in decays for c in range(blocks)], axis=0
        )
        rate_rows = jnp.concatenate(
            [r[:, c * BLOCK : (c + 1) * BLOCK] for r in rates for c in range(blocks)], axis=0
        )
        sums = jnp.dot(
            decay_rows, upper, precision=lax.Precision.HIGHEST, preferred_element_type=f32
        )
        cumulative_ref[at] = sums
        cum_columns = jnp.transpose(sums)
        rate_columns = jnp.transpose(rate_rows)
        growth_columns = jnp.exp(cum_columns)
        last = sums[:, BLOCK - 1 : BLOCK]
        tail_columns = jnp.exp(jnp.transpose(last - sums))
        end_values = jnp.exp(last)
        for c in range(blocks):
            keys = unit_ref[p, pl.ds(c * BLOCK, BLOCK), :]
            values = mixed_ref[p, pl.ds(c * BLOCK, BLOCK), :]
            if c == 0:
                keys = jnp.concatenate([edge_keys, keys[EDGE:]], axis=0)
                values = jnp.concatenate([edge_values, values[EDGE:]], axis=0)
                first_ref[at] = keys
            parts = split(keys)
            key_parts.append(parts)
            dots = dot_split(parts, parts, NT) if c == 0 else dots_ref[p, c]
            for b in range(2):
                r = b * blocks + c
                rate = rate_columns[:, r : r + 1]
                spread = cum_columns[:, r : r + 1] - sums[r : r + 1, :]
                table = jnp.exp(jnp.where(strict, spread, FAR))
                systems.append(rate * table * dots)
                rights.append(
                    jnp.concatenate(
                        [
                            rate * values[:, b * DV : (b + 1) * DV],
                            (rate * growth_columns[:, r : r + 1]) * keys,
                        ],
                        axis=1,
                    )
                )
                tails.append(tail_columns[:, r : r + 1])
                ends.append(end_values[r : r + 1, :])

    inverses = invert_all(systems)
    solved = [dot_split(split(x), split(r)) for x, r in zip(inverses, rights)]
    for at in range(count):
        moves = {}
        for c in range(blocks):
            i = (at * blocks + c) * 2
            both = jnp.concatenate([tails[i] * solved[i], tails[i + 1] * solved[i + 1]], axis=1)
            grown = dot_split(key_parts[at * blocks + c], split(both), TN)
            for b in range(2):
                solved_ref[at, b, pl.ds(c * BLOCK, BLOCK), :] = solved[i + b]
                added = grown[:, b * 2 * DK : b * 2 * DK + DV]
                move = (
                    jnp.where(identity, ends[i + b], 0.0)
                    - grown[:, b * 2 * DK + DV : (b + 1) * 2 * DK]
                )
                moves[b, c] = (added, move)
        for b in range(2):
            both = jnp.concatenate(moves[b, 0], axis=1)
            for c in range(1, blocks):
                starts_ref[at, b, c - 1] = both
                added, move = moves[b, c]
                both = dot_split(split(move), split(both))
                both = jnp.concatenate([both[:, :DV] + added, both[:, DV:]], axis=1)
            message_refs[at][b] = both


def query_kernel(
    slots,
    group,
    q_ref,
    before_ref,
    qt_ref,
    unit_ref,
    first_ref,
    cumulative_ref,
    solved_ref,
    starts_ref,
    own_ref,
    high_ref,
    low_ref,
    padded,
):
    place = lax.axis_index("seq") % group
    tokens = q_ref.shape[0]
    blocks = tokens // BLOCK
    row, column = iotas()
    causal = row >= column
    work = []
    for at, s in enumerate(slots):
        p = place ^ slot_partner(group, s)
        columns = lanes(p * DK, DK)
        padded[0:8] = before_ref[:, columns].astype(f32)[EDGE - 8 :]
        padded[8:] = q_ref[:, columns].astype(f32)
        taps = qt_ref[:, columns].astype(f32)
        queries = unit(conv_rows(padded, taps, tokens, slice(None)), 1.0 / math.sqrt(DK))
        sums = cumulative_ref[at]
        cum_columns = jnp.transpose(sums)
        growth_columns = jnp.exp(cum_columns)
        for c in range(blocks):
            here = queries[c * BLOCK : (c + 1) * BLOCK]
            keys = first_ref[at] if c == 0 else unit_ref[p, pl.ds(c * BLOCK, BLOCK), :]
            dots = dot_split(split(here), split(keys), NT)
            for b in range(2):
                r = b * blocks + c
                spread = cum_columns[:, r : r + 1] - sums[r : r + 1, :]
                attend = dots * jnp.exp(jnp.where(causal, spread, FAR))
                grown = growth_columns[:, r : r + 1] * here
                work.append((at, b, c, split(attend), grown))
    seen = [
        dot_split(attend, split(solved_ref[at, b, pl.ds(c * BLOCK, BLOCK), :]))
        for at, b, c, attend, grown in work
    ]
    for (at, b, c, attend, grown), one in zip(work, seen):
        own, reads = one[:, :DV], grown - one[:, DV:]
        if c > 0:
            through = dot_split(split(reads), split(starts_ref[at, b, c - 1]))
            own, reads = own + through[:, :DV], through[:, DV:]
        here = pl.ds(c * BLOCK, BLOCK)
        own_ref[at, b, here, :] = own
        high_ref[at, b, here, :], low_ref[at, b, here, :] = split(reads)


def prefix_kernel(group, *refs):
    messages, refs = refs[:group], refs[group:]
    chain_ref, leaving_ref, held, sems = refs
    place = lax.axis_index("seq") % group
    copies = [
        pltpu.make_async_copy(messages[d], held.at[place ^ d], sems.at[d]) for d in range(group)
    ]
    for copy in copies:
        copy.start()
    for copy in copies:
        copy.wait()
    heads = leaving_ref.shape[0]
    chain = [held[0, b] for b in range(heads)]
    for i in range(1, group):
        for b in range(heads):
            chain_ref[i - 1, b] = chain[b]
        chain = [
            dot_split(split(held[i, b, :, DV:]), split(chain[b])) for b in range(heads)
        ]
        chain = [
            jnp.concatenate([chain[b][:, :DV] + held[i, b, :, 0:DV], chain[b][:, DV:]], axis=1)
            for b in range(heads)
        ]
    for b in range(heads):
        chain_ref[group - 1, b] = chain[b]
        leaving_ref[b] = chain[b][:, :DV]


def enter_kernel(group, entering_ref, chain_ref, *refs):
    *outs, leaving_ref = refs
    place = lax.axis_index("seq") % group
    heads = entering_ref.shape[0]
    states = [[entering_ref[b] for b in range(heads)]] + [[] for i in range(group)]
    for b in range(heads):
        moves = jnp.concatenate([chain_ref[i, b, :, DV:] for i in range(group)], axis=0)
        moved = dot_split(split(moves), split(states[0][b]))
        for i in range(group):
            states[i + 1].append(chain_ref[i, b, :, 0:DV] + moved[i * DK : (i + 1) * DK])
    for b in range(heads):
        leaving_ref[b] = states[group][b]
    for j in range(group):

        @pl.when(place == j)
        def _():
            for i in range(group):
                for b in range(heads):
                    outs[j ^ i][b] = states[i][b]


def output_kernel(group, calls, *refs):
    reads, entering, (out_ref,) = refs[: 3 * len(calls)], refs[3 * len(calls) : -1], refs[-1:]
    place = lax.axis_index("seq") % group
    for k, slots in enumerate(calls):
        own_ref, high_ref, low_ref = reads[3 * k : 3 * k + 3]
        for at, s in enumerate(slots):
            d = slot_partner(group, s)
            p = place ^ d
            for b in range(2):
                product = dot_split((high_ref[at, b], low_ref[at, b]), split(entering[d][b]))
                out_ref[:, lanes(p * 2 * DV + b * DV, DV)] = own_ref[at, b] + product


def shape(*dims, dtype=f32):
    return jax.ShapeDtypeStruct(dims, dtype)


def params(mib=24):
    return pltpu.CompilerParams(vmem_limit_bytes=mib << 20)


def whole(space=VMEM):
    return pl.BlockSpec(memory_space=space)


def per_device(
    hidden_states,
    proj_ba,
    query_in,
    key_in,
    value_in,
    conv_query,
    conv_key,
    convolution_value_taps,
    decay_scale,
    dt_bias,
):
    tokens = hidden_states.shape[0]
    heads = decay_scale.shape[0]
    pairs = key_in.shape[1] // DK
    blocks = tokens // BLOCK
    key_width, value_width = key_in.shape[1], value_in.shape[1]
    seq, head_count = lax.axis_size("seq"), lax.axis_size("head")
    group = pairs

    def full(block):
        return pl.BlockSpec(block, lambda i: (0,) * len(block))

    last_rows = tokens // EDGE - 1
    *partial, tail = pl.pallas_call(
        functools.partial(logits_kernel, head_count),
        grid=(1,),
        in_specs=[
            full(hidden_states.shape),
            full(proj_ba.shape[::-1]),
            pl.BlockSpec((EDGE, key_width), lambda i: (last_rows, 0)),
            pl.BlockSpec((EDGE, key_width), lambda i: (last_rows, 0)),
            pl.BlockSpec((EDGE, value_width), lambda i: (last_rows, 0)),
        ],
        out_specs=[full((2 * heads, tokens))] * head_count
        + [full((EDGE, 2 * key_width + value_width))],
        out_shape=[shape(2 * heads, tokens)] * head_count
        + [shape(EDGE, 2 * key_width + value_width, dtype=bf16)],
        scratch_shapes=[VMEM((head_count, 2 * heads, tokens), f32)],
        compiler_params=params(),
        name="logits",
    )(in_hbm(hidden_states), in_hbm(proj_ba.T), in_hbm(query_in), in_hbm(key_in), in_hbm(value_in))

    logits = [partial[0]] + [
        lax.ppermute(partial[d], "head", [(i, i ^ d) for i in range(head_count)])
        for d in range(1, head_count)
    ]
    before = lax.ppermute(tail, "seq", [(i, i + 1) for i in range(seq - 1)])

    unit_keys, key_dots, mixed = pl.pallas_call(
        mix_kernel,
        grid=(pairs,),
        in_specs=[
            pl.BlockSpec((tokens, DK), lambda i: (0, i)),
            pl.BlockSpec((tokens, 2 * DV), lambda i: (0, i)),
            pl.BlockSpec((KCONV, DK), lambda i: (0, i)),
            pl.BlockSpec((KCONV, 2 * DV), lambda i: (0, i)),
        ],
        out_specs=[
            pl.BlockSpec((1, tokens, DK), lambda i: (i, 0, 0)),
            pl.BlockSpec((1, blocks, BLOCK, BLOCK), lambda i: (i, 0, 0, 0)),
            pl.BlockSpec((1, tokens, 2 * DV), lambda i: (i, 0, 0)),
        ],
        out_shape=[
            shape(pairs, tokens, DK),
            shape(pairs, blocks, BLOCK, BLOCK),
            shape(pairs, tokens, 2 * DV),
        ],
        scratch_shapes=[VMEM((tokens + 8, DK + 2 * DV), f32)],
        compiler_params=params(),
        cost_estimate=pl.CostEstimate(
            flops=4_000_000_000, bytes_accessed=6_000_000, transcendentals=0
        ),
        name="mix",
    )(in_hbm(key_in), in_hbm(value_in), in_hbm(conv_key), in_hbm(convolution_value_taps))

    def solve(slots):
        count = len(slots)
        return pl.pallas_call(
            functools.partial(solve_kernel, slots, group, head_count),
            grid=(1,),
            in_specs=[whole(pltpu.SMEM)] * 2
            + [whole()] * (head_count + 3)
            + [
                pl.BlockSpec((EDGE, key_width), lambda i: (0, 0)),
                pl.BlockSpec((EDGE, value_width), lambda i: (0, 0)),
            ]
            + [whole()] * 3,
            out_specs=[whole()] * (count + 4),
            out_shape=[shape(2, DK, 2 * DK)] * count
            + [
                shape(count, 2, tokens, 2 * DK),
                shape(count, 2, blocks - 1, DK, 2 * DK),
                shape(count, 2 * blocks, BLOCK),
                shape(count, BLOCK, DK),
            ],
            scratch_shapes=[VMEM((EDGE + 8, DK + 2 * DV), f32)],
            compiler_params=params(),
            cost_estimate=pl.CostEstimate(
                flops=4_000_000_000 * count, bytes_accessed=2_000_000 * count, transcendentals=0
            ),
            name="solve",
        )(
            decay_scale,
            dt_bias,
            *logits,
            unit_keys,
            key_dots,
            mixed,
            in_hbm(key_in),
            in_hbm(value_in),
            before,
            in_hbm(conv_key),
            in_hbm(convolution_value_taps),
        )

    def query(slots, solved, starts, cumulative, first_keys):
        count = len(slots)
        return pl.pallas_call(
            functools.partial(query_kernel, slots, group),
            in_specs=[whole()] * 8,
            out_specs=[whole()] * 3,
            out_shape=[shape(count, 2, tokens, DV)]
            + [shape(count, 2, tokens, DK, dtype=bf16)] * 2,
            scratch_shapes=[VMEM((tokens + 8, DK), f32)],
            compiler_params=params(),
            cost_estimate=pl.CostEstimate(
                flops=2_000_000_000 * count, bytes_accessed=2_000_000 * count, transcendentals=0
            ),
            name="query",
        )(in_hbm(query_in), before, in_hbm(conv_query), unit_keys, first_keys, cumulative, solved, starts)

    calls = solve_calls(group)
    messages, rest = [], []
    for slots in calls:
        results = solve(slots)
        messages += results[: len(slots)]
        rest.append(results[len(slots) :])

    arrived = [None] * group
    for s in range(group):
        d = slot_partner(group, s)
        arrived[d] = (
            lax.ppermute(messages[s], "seq", [(i, i ^ d) for i in range(seq)]) if d else messages[s]
        )

    reads = [query(calls[0], *rest[0])]
    arrived, reads[0] = lax.optimization_barrier((arrived, reads[0]))
    chain, leaving = pl.pallas_call(
        functools.partial(prefix_kernel, group),
        in_specs=[whole(pl.ANY)] * group,
        out_specs=[whole()] * 2,
        out_shape=[shape(group, 2, DK, 2 * DK), shape(2, DK, DV)],
        scratch_shapes=[VMEM((group, 2, DK, 2 * DK), f32), pltpu.SemaphoreType.DMA((group,))],
        compiler_params=params(),
        name="prefix",
    )(*arrived)
    enter = pl.pallas_call(
        functools.partial(enter_kernel, group),
        in_specs=[whole()] * 2,
        out_specs=[whole()] * (group + 1),
        out_shape=[shape(2, DK, DV)] * (group + 1),
        compiler_params=params(),
        name="enter",
    )
    for hop in range(seq // group - 1):
        received = lax.ppermute(leaving, "seq", [(i, i + group) for i in range(seq - group)])
        if hop == 0:
            reads += [query(slots, *outs) for slots, outs in zip(calls[1:-1], rest[1:-1])]
            received, reads = lax.optimization_barrier((received, reads))
        *entering, leaving = enter(received, chain)

    states = [entering[0]] + [
        lax.ppermute(entering[d], "seq", [(i, i ^ d) for i in range(seq)]) for d in range(1, group)
    ]
    reads.append(query(calls[-1], *rest[-1]))
    return pl.pallas_call(
        functools.partial(output_kernel, group, calls),
        in_specs=[whole()] * (3 * len(calls) + group),
        out_specs=whole(),
        out_shape=shape(tokens, value_width),
        compiler_params=params(),
        name="outputs",
    )(*[x for three in reads for x in three], *states)


def solution(mesh):
    placed = (
        P("seq", "head"),
        P("head", None),
        P("seq", "head"),
        P("seq", "head"),
        P("seq", "head"),
        P(None, "head"),
        P(None, "head"),
        P(None, "head"),
        P("head"),
        P("head"),
    )
    return jax.shard_map(
        per_device, mesh=mesh, in_specs=placed, out_specs=P("seq", "head"), check_vma=False
    )
```

```python
import functools
import math

import jax
import jax.numpy as jnp
import numpy as np
from jax import lax
from jax.experimental import pallas as pl
from jax.experimental.pallas import tpu as pltpu
from jax.sharding import PartitionSpec as P

DK = 128
DV = 128
KCONV = 4
BLOCK = 128
SUB = 16
EDGE = 16

f32 = jnp.float32
bf16 = jnp.bfloat16
VMEM = pltpu.VMEM
FAR = -1e30


def split(x):
    hi = x.astype(bf16)
    return hi, (x - hi.astype(f32)).astype(bf16)


def dot_split(a, b, contract=((1,), (0,))):
    (ah, al), (bh, bl) = a, b
    (ca,), (cb,) = contract
    left = jnp.concatenate([ah, al, ah], axis=ca)
    right = jnp.concatenate([bh, bh, bl], axis=cb)
    return lax.dot_general(left, right, (contract, ((), ())), preferred_element_type=f32)


NN = ((1,), (0,))
NT = ((1,), (1,))
TN = ((0,), (0,))


def silu(x):
    return x / (1.0 + jnp.exp(-x))


def unit(x, factor=1.0):
    return x * (lax.rsqrt(jnp.sum(x * x, axis=-1, keepdims=True) + 1e-6) * factor)


def conv_rows(padded_ref, taps, rows, columns):
    total = taps[0:1] * padded_ref[pl.ds(8 - KCONV + 1, rows), columns]
    for j in range(1, KCONV):
        total = total + taps[j : j + 1] * padded_ref[pl.ds(8 - KCONV + 1 + j, rows), columns]
    return silu(total)


def iotas(rows=BLOCK, columns=BLOCK):
    return (
        lax.broadcasted_iota(jnp.int32, (rows, columns), 0),
        lax.broadcasted_iota(jnp.int32, (rows, columns), 1),
    )


def slot_partner(group, slot):
    order = [d for d in range(group - 1, 0, -1) if d % 2] + [
        d for d in range(group - 1, 0, -1) if d % 2 == 0
    ]
    return (order + [0])[slot]


def solve_calls(group):
    half = group // 2
    return [(s,) for s in range(group)]


def in_hbm(x):
    return pltpu.with_memory_space_constraint(x, pltpu.HBM)


def rows_before(before_ref, columns):
    rows = before_ref[:, columns].astype(f32)[EDGE - 8 :]
    return jnp.where(lax.axis_index("seq") > 0, rows, 0.0)


def lanes(start, size):
    return pl.ds(pl.multiple_of(start, 128), size)


def logits_kernel(
    head_count,
    scale_ref,
    bias_ref,
    hidden_ref,
    proj_ref,
    q_first,
    k_first,
    v_first,
    q_last,
    k_last,
    v_last,
    q_taps,
    k_taps,
    v_taps,
    kept_ref,
    given_ref,
    tail_ref,
    edge_ref,
    scales_ref,
    held,
):
    rows = proj_ref.shape[0] // head_count
    everything = lax.dot_general(
        proj_ref[...], hidden_ref[...], (NT, ((), ())), preferred_element_type=f32
    )
    for m in range(head_count):
        held[m] = everything[m * rows : (m + 1) * rows]
    me = lax.axis_index("head")
    for n in range(head_count // 2):
        kept_ref[n] = held[me ^ (2 * n)]
        given_ref[n] = held[me ^ (2 * n + 1)]
    heads = rows // 2
    row, column = iotas(heads, heads)
    scale, bias = (
        jnp.sum(jnp.where(row == column, ref[...], 0.0), axis=1, keepdims=True)
        for ref in (scale_ref, bias_ref)
    )
    scales_ref[...] = jnp.broadcast_to(scale, scales_ref.shape)
    for h in range(heads):
        kept_ref[0, 2 * h : 2 * h + 1, :] = kept_ref[0, 2 * h : 2 * h + 1, :] + bias[h : h + 1]
    edge_ref[...] = jnp.zeros_like(edge_ref)
    start = 0
    for first, last, taps in ((q_first, q_last, q_taps), (k_first, k_last, k_taps), (v_first, v_last, v_taps)):
        here = slice(start, start + first.shape[1])
        tail_ref[:, here] = last[...]
        edge_ref[0:EDGE, here] = first[...].astype(f32)
        edge_ref[EDGE : EDGE + KCONV, here] = taps[...].astype(f32)
        start += first.shape[1]


def mix_kernel(slots, group, key_width, edge_ref, k_ref, v_ref, unit_ref, dots_ref, mixed_ref, k_held, v_held, padded, sems):
    tokens = k_ref.shape[0]
    place = lax.axis_index("seq") % group
    copies = []
    for at, s in enumerate(slots):
        p = place ^ slot_partner(group, s)
        copies.append(
            (
                pltpu.make_async_copy(k_ref.at[:, lanes(p * DK, DK)], k_held.at[at], sems.at[at, 0]),
                pltpu.make_async_copy(
                    v_ref.at[:, lanes(p * 2 * DV, 2 * DV)], v_held.at[at], sems.at[at, 1]
                ),
            )
        )
    for both in copies:
        for copy in both:
            copy.start()
    for at, s in enumerate(slots):
        p = place ^ slot_partner(group, s)
        key_taps = edge_ref[EDGE : EDGE + KCONV, lanes(key_width + p * DK, DK)]
        value_taps = edge_ref[EDGE : EDGE + KCONV, lanes(2 * key_width + p * 2 * DV, 2 * DV)]
        padded[at, 0:8] = jnp.zeros((8, padded.shape[2]), f32)
        copies[at][0].wait()
        padded[at, 8:, 0:DK] = k_held[at].astype(f32)
        copies[at][1].wait()
        padded[at, 8:, DK:] = v_held[at].astype(f32)
        keys = unit(conv_rows(padded.at[at], key_taps, tokens, slice(0, DK)))
        unit_ref[at] = keys
        for c in range(tokens // BLOCK):
            part = split(keys[c * BLOCK : (c + 1) * BLOCK])
            dots_ref[at, c] = dot_split(part, part, NT)
        mixed_ref[at] = conv_rows(padded.at[at], value_taps, tokens, slice(DK, None))


def softplus(u):
    e = jnp.exp(-jnp.abs(u))
    small = e * (1.0 - e * (0.5 - e * (1.0 / 3.0 - e * (0.25 - e * 0.2))))
    return jnp.maximum(u, 0.0) + jnp.where(e < 0.03, small, jnp.log(1.0 + e))


def dot_wide(a, b):
    rows, columns = a[0].shape[0], b[0].shape[1]
    four = jnp.dot(
        jnp.concatenate(a, axis=0), jnp.concatenate(b, axis=1), preferred_element_type=f32
    )
    return four[:rows, :columns] + (four[:rows, columns:] + four[rows:, :columns])


def pick_matrix():
    row, column = np.arange(BLOCK)[:, None], np.arange((SUB - 1) * BLOCK)[None, :]
    pick = row == (column % BLOCK) // SUB * SUB + column // BLOCK
    return np.concatenate([pick, pick], axis=0).astype(bf16)


def invert_all(lowers, pick):
    count = len(lowers)
    row, column = iotas()
    blocks = (row // SUB) == (column // SUB)
    folded = []
    for lower in lowers:
        kept = jnp.where(blocks, lower, 0.0)
        total = kept[0:SUB]
        for b in range(1, BLOCK // SUB):
            total = total + kept[b * SUB : (b + 1) * SUB]
        folded.append(total)
    spread = jnp.concatenate(split(jnp.concatenate(folded, axis=0)), axis=1)
    wide = jnp.dot(spread, pick, preferred_element_type=f32).reshape(
        count, SUB, (SUB - 1) * BLOCK
    )
    srow, scolumn = iotas(SUB, BLOCK)
    inverse = jnp.broadcast_to(
        jnp.where(srow == scolumn % SUB, 1.0, 0.0)[None], (count, SUB, BLOCK)
    )
    for j in range(SUB - 1):
        inverse = inverse - wide[:, :, j * BLOCK : (j + 1) * BLOCK] * inverse[:, j : j + 1, :]
    inverses = [inverse[i] for i in range(count)]
    halves = [split(x) for x in lowers]
    size = SUB
    while size < BLOCK:
        same = (row // size) == (column // size)
        across = ((row // (2 * size)) == (column // (2 * size))) & ((row // size) > (column // size))
        same, across = (jnp.where(m, 1.0, 0.0).astype(bf16) for m in (same, across))
        odd = iotas(size, BLOCK)[1] // size % 2 == 1
        dot = dot_wide if size < 64 else dot_split
        parts = [split(x) for x in inverses]
        first = [dot(x, tuple(h * across for h in low)) for x, low in zip(parts, halves)]
        spread = [
            tuple(jnp.concatenate([h] * (BLOCK // size), axis=0) * same for h in x) for x in parts
        ]
        second = [dot(split(x), y) for x, y in zip(first, spread)]
        inverses = [
            jnp.concatenate([jnp.where(odd, 0.0, x), jnp.where(odd, x, -y)], axis=0)
            for x, y in zip(inverses, second)
        ]
        size *= 2
    return inverses


def followed(later, both):
    added, move = later
    both = dot_split(split(move), split(both))
    return jnp.concatenate([both[:, :DV] + added, both[:, DV:]], axis=1)


def solve_kernel(
    slots,
    start,
    group,
    key_width,
    pieces,
    scales_ref,
    *refs,
):
    logit_refs, refs = refs[:pieces], refs[pieces:]
    (unit_ref, dots_ref, mixed_ref, before_ref, edge_ref, pick_ref), refs = refs[:6], refs[6:]
    count = len(slots)
    message_refs, refs = refs[:count], refs[count:]
    solved_ref, starts_ref, cumulative_ref, first_ref, padded = refs
    tokens = unit_ref.shape[1]
    blocks = tokens // BLOCK
    place = lax.axis_index("seq") % group
    row, column = iotas()
    upper = jnp.where(row <= column, 1.0, 0.0)
    identity = row == column
    strict = row > column

    systems, rights, tails, ends, key_parts = [], [], [], [], []
    for at, s in enumerate(slots):
        p = place ^ slot_partner(group, s)
        kcol, vcol = lanes(key_width + p * DK, DK), lanes(2 * key_width + p * 2 * DV, 2 * DV)
        padded[0:8, 0:DK] = rows_before(before_ref, kcol)
        padded[0:8, DK:] = rows_before(before_ref, vcol)
        padded[8:, 0:DK] = edge_ref[0:EDGE, kcol]
        padded[8:, DK:] = edge_ref[0:EDGE, vcol]
        key_taps = edge_ref[EDGE : EDGE + KCONV, kcol]
        value_taps = edge_ref[EDGE : EDGE + KCONV, vcol]
        edge_keys = unit(conv_rows(padded, key_taps, EDGE, slice(0, DK)))
        edge_values = conv_rows(padded, value_taps, EDGE, slice(DK, None))
        decays, rates = [], []
        for b in range(2):
            h = 2 * p + b
            u = logit_refs[0][0, pl.ds(2 * h, 1), :] + logit_refs[1][0, pl.ds(2 * h, 1), :]
            w = logit_refs[0][0, pl.ds(2 * h + 1, 1), :] + logit_refs[1][0, pl.ds(2 * h + 1, 1), :]
            for ref in logit_refs[2:]:
                u = u + ref[pl.ds(2 * h, 1), :]
                w = w + ref[pl.ds(2 * h + 1, 1), :]
            decays.append(-scales_ref[pl.ds(h, 1), :] * softplus(u))
            rates.append(1.0 / (1.0 + jnp.exp(-w)))
        decay_rows = jnp.concatenate(
            [d[:, c * BLOCK : (c + 1) * BLOCK] for d in decays for c in range(blocks)], axis=0
        )
        rate_rows = jnp.concatenate(
            [r[:, c * BLOCK : (c + 1) * BLOCK] for r in rates for c in range(blocks)], axis=0
        )
        sums = jnp.dot(
            decay_rows, upper, precision=lax.Precision.HIGHEST, preferred_element_type=f32
        )
        cumulative_ref[at] = sums
        cum_columns = jnp.transpose(sums)
        rate_columns = jnp.transpose(rate_rows)
        growth_columns = jnp.exp(cum_columns)
        last = sums[:, BLOCK - 1 : BLOCK]
        tail_columns = jnp.exp(jnp.transpose(last - sums))
        end_values = jnp.exp(last)
        for c in range(blocks):
            keys = unit_ref[start + at, pl.ds(c * BLOCK, BLOCK), :]
            values = mixed_ref[start + at, pl.ds(c * BLOCK, BLOCK), :]
            if c == 0:
                keys = jnp.concatenate([edge_keys, keys[EDGE:]], axis=0)
                values = jnp.concatenate([edge_values, values[EDGE:]], axis=0)
                first_ref[at] = keys
            parts = split(keys)
            key_parts.append(parts)
            dots = dot_split(parts, parts, NT) if c == 0 else dots_ref[start + at, c]
            for b in range(2):
                r = b * blocks + c
                rate = rate_columns[:, r : r + 1]
                spread = cum_columns[:, r : r + 1] - sums[r : r + 1, :]
                table = jnp.exp(jnp.where(strict, spread, FAR))
                systems.append(rate * table * dots)
                rights.append(
                    jnp.concatenate(
                        [
                            rate * values[:, b * DV : (b + 1) * DV],
                            (rate * growth_columns[:, r : r + 1]) * keys,
                        ],
                        axis=1,
                    )
                )
                tails.append(tail_columns[:, r : r + 1])
                ends.append(end_values[r : r + 1, :])

    inverses = invert_all(systems, pick_ref[...])
    solved = [dot_split(split(x), split(r)) for x, r in zip(inverses, rights)]
    for at in range(count):
        moves = {}
        for c in range(blocks):
            i = (at * blocks + c) * 2
            both = jnp.concatenate([tails[i] * solved[i], tails[i + 1] * solved[i + 1]], axis=1)
            grown = dot_split(key_parts[at * blocks + c], split(both), TN)
            for b in range(2):
                solved_ref[at, b, pl.ds(c * BLOCK, BLOCK), :] = solved[i + b]
                added = grown[:, b * 2 * DK : b * 2 * DK + DV]
                move = (
                    jnp.where(identity, ends[i + b], 0.0)
                    - grown[:, b * 2 * DK + DV : (b + 1) * 2 * DK]
                )
                moves[b, c] = (added, move)
        for b in range(2):
            half = blocks // 2
            parts = []
            for begin in (0, half):
                both = jnp.concatenate(moves[b, begin], axis=1)
                for c in range(begin + 1, begin + half):
                    if begin == 0:
                        starts_ref[at, b, c - 1] = both
                    both = followed(moves[b, c], both)
                parts.append(both)
            both = parts[0]
            for c in range(half, blocks):
                starts_ref[at, b, c - 1] = both
                if c < blocks - 1:
                    both = followed(moves[b, c], both)
            both = followed((parts[1][:, :DV], parts[1][:, DV:]), parts[0])
            message_refs[at][b] = both


def mix_and_solve_kernel(slots, group, key_width, pieces, *refs):
    count = len(slots)
    (scales_ref, *logit_refs), refs = refs[: 1 + pieces], refs[1 + pieces :]
    (before_ref, edge_ref, pick_ref, k_ref, v_ref), refs = refs[:5], refs[5:]
    outs, refs = refs[: count + 4], refs[count + 4 :]
    unit_ref, dots_ref, mixed_ref, k_held, v_held, padded, sems, few = refs
    mix_kernel(
        slots, group, key_width, edge_ref, k_ref, v_ref, unit_ref, dots_ref, mixed_ref, k_held, v_held, padded, sems
    )
    solve_kernel(
        slots,
        0,
        group,
        key_width,
        pieces,
        scales_ref,
        *logit_refs,
        unit_ref,
        dots_ref,
        mixed_ref,
        before_ref,
        edge_ref,
        pick_ref,
        *outs,
        few,
    )


def query_kernel(
    slots,
    start,
    group,
    q_ref,
    before_ref,
    edge_ref,
    unit_ref,
    first_ref,
    cumulative_ref,
    solved_ref,
    starts_ref,
    own_ref,
    high_ref,
    low_ref,
    padded,
):
    place = lax.axis_index("seq") % group
    tokens = q_ref.shape[0]
    blocks = tokens // BLOCK
    row, column = iotas()
    causal = row >= column
    work = []
    for at, s in enumerate(slots):
        p = place ^ slot_partner(group, s)
        columns = lanes(p * DK, DK)
        padded[0:8] = rows_before(before_ref, columns)
        padded[8:] = q_ref[:, columns].astype(f32)
        taps = edge_ref[EDGE : EDGE + KCONV, columns]
        queries = unit(conv_rows(padded, taps, tokens, slice(None)), 1.0 / math.sqrt(DK))
        sums = cumulative_ref[at]
        cum_columns = jnp.transpose(sums)
        growth_columns = jnp.exp(cum_columns)
        for c in range(blocks):
            here = queries[c * BLOCK : (c + 1) * BLOCK]
            keys = first_ref[at] if c == 0 else unit_ref[start + at, pl.ds(c * BLOCK, BLOCK), :]
            dots = dot_split(split(here), split(keys), NT)
            for b in range(2):
                r = b * blocks + c
                spread = cum_columns[:, r : r + 1] - sums[r : r + 1, :]
                attend = dots * jnp.exp(jnp.where(causal, spread, FAR))
                grown = growth_columns[:, r : r + 1] * here
                work.append((at, b, c, split(attend), grown))
    seen = [
        dot_split(attend, split(solved_ref[at, b, pl.ds(c * BLOCK, BLOCK), :]))
        for at, b, c, attend, grown in work
    ]
    for (at, b, c, attend, grown), one in zip(work, seen):
        own, reads = one[:, :DV], grown - one[:, DV:]
        if c > 0:
            through = dot_split(split(reads), split(starts_ref[at, b, c - 1]))
            own, reads = own + through[:, :DV], through[:, DV:]
        here = pl.ds(c * BLOCK, BLOCK)
        own_ref[at, b, here, :] = own
        high_ref[at, b, here, :], low_ref[at, b, here, :] = split(reads)


def prefix_kernel(group, *refs):
    messages, refs = refs[:group], refs[group:]
    chain_ref, leaving_ref, held, sems = refs
    place = lax.axis_index("seq") % group
    copies = [
        pltpu.make_async_copy(messages[d], held.at[place ^ d], sems.at[d]) for d in range(group)
    ]
    for copy in copies:
        copy.start()
    for copy in copies:
        copy.wait()
    heads = leaving_ref.shape[0]
    chain = [held[0, b] for b in range(heads)]
    for i in range(1, group):
        for b in range(heads):
            chain_ref[i - 1, b] = chain[b]
        chain = [
            dot_split(split(held[i, b, :, DV:]), split(chain[b])) for b in range(heads)
        ]
        chain = [
            jnp.concatenate([chain[b][:, :DV] + held[i, b, :, 0:DV], chain[b][:, DV:]], axis=1)
            for b in range(heads)
        ]
    for b in range(heads):
        chain_ref[group - 1, b] = chain[b]
        leaving_ref[b] = chain[b][:, :DV]


def enter_kernel(group, entering_ref, chain_ref, *refs):
    *outs, leaving_ref = refs
    place = lax.axis_index("seq") % group
    heads = entering_ref.shape[0]
    states = [[entering_ref[b] for b in range(heads)]] + [[] for i in range(group)]
    for b in range(heads):
        moves = jnp.concatenate([chain_ref[i, b, :, DV:] for i in range(group)], axis=0)
        moved = dot_split(split(moves), split(states[0][b]))
        for i in range(group):
            states[i + 1].append(chain_ref[i, b, :, 0:DV] + moved[i * DK : (i + 1) * DK])
    for b in range(heads):
        leaving_ref[b] = states[group][b]
    for j in range(group):

        @pl.when(place == j)
        def _():
            for i in range(group):
                for b in range(heads):
                    outs[j ^ i][b] = states[i][b]


def output_kernel(group, calls, *refs):
    reads, entering, (out_ref,) = refs[: 3 * len(calls)], refs[3 * len(calls) : -1], refs[-1:]
    place = lax.axis_index("seq") % group
    for k, slots in enumerate(calls):
        own_ref, high_ref, low_ref = reads[3 * k : 3 * k + 3]
        for at, s in enumerate(slots):
            d = slot_partner(group, s)
            p = place ^ d
            for b in range(2):
                product = dot_split((high_ref[at, b], low_ref[at, b]), split(entering[d][b]))
                out_ref[:, lanes(p * 2 * DV + b * DV, DV)] = own_ref[at, b] + product


def shape(*dims, dtype=f32):
    return jax.ShapeDtypeStruct(dims, dtype)


def params(mib=24):
    return pltpu.CompilerParams(vmem_limit_bytes=mib << 20)


def whole(space=VMEM):
    return pl.BlockSpec(memory_space=space)


def per_device(
    hidden_states,
    proj_ba,
    query_in,
    key_in,
    value_in,
    conv_query,
    conv_key,
    convolution_value_taps,
    decay_scale,
    dt_bias,
):
    tokens = hidden_states.shape[0]
    heads = decay_scale.shape[0]
    pairs = key_in.shape[1] // DK
    blocks = tokens // BLOCK
    key_width, value_width = key_in.shape[1], value_in.shape[1]
    seq, head_count = lax.axis_size("seq"), lax.axis_size("head")
    group = pairs

    def full(block):
        return pl.BlockSpec(block, lambda i: (0,) * len(block))

    last_rows = tokens // EDGE - 1
    width = 2 * key_width + value_width
    inputs = (query_in, key_in, value_in)
    taps = (conv_query, conv_key, convolution_value_taps)
    kept, given, tail, edge, scales = pl.pallas_call(
        functools.partial(logits_kernel, head_count),
        grid=(1,),
        in_specs=[full((1, heads))] * 2 + [full(hidden_states.shape), full(proj_ba.shape[::-1])]
        + [pl.BlockSpec((EDGE, x.shape[1]), lambda i: (0, 0)) for x in inputs]
        + [pl.BlockSpec((EDGE, x.shape[1]), lambda i: (last_rows, 0)) for x in inputs]
        + [full(x.shape) for x in taps],
        out_specs=[whole()] * 5,
        out_shape=[shape(head_count // 2, 2 * heads, tokens)] * 2
        + [shape(EDGE, width, dtype=bf16), shape(EDGE + 8, width), shape(heads, tokens)],
        scratch_shapes=[VMEM((head_count, 2 * heads, tokens), f32)],
        compiler_params=params(),
        name="logits",
    )(
        *[in_hbm(x.reshape(1, heads)) for x in (decay_scale, dt_bias)],
        *[in_hbm(x) for x in (hidden_states, proj_ba.T, *inputs, *inputs, *taps)],
    )

    taken = lax.ppermute(given, "head", [(i, i ^ 1) for i in range(head_count)])
    logits = [kept, taken] + [
        lax.ppermute(kept[n] + taken[n], "head", [(i, i ^ (2 * n)) for i in range(head_count)])
        for n in range(1, head_count // 2)
    ]
    before = lax.ppermute(tail, "seq", [(i, (i + 1) % seq) for i in range(seq)])

    pick = jnp.asarray(pick_matrix())

    def mix_shapes(count):
        return [(count, tokens, DK), (count, blocks, BLOCK, BLOCK), (count, tokens, 2 * DV)]

    def mix_scratch(count):
        return [
            VMEM((count, tokens, DK), bf16),
            VMEM((count, tokens, 2 * DV), bf16),
            VMEM((count, tokens + 8, DK + 2 * DV), f32),
            pltpu.SemaphoreType.DMA((count, 2)),
        ]

    def solve_shapes(count):
        return [shape(2, DK, 2 * DK)] * count + [
            shape(count, 2, tokens, 2 * DK),
            shape(count, 2, blocks - 1, DK, 2 * DK),
            shape(count, 2 * blocks, BLOCK),
            shape(count, BLOCK, DK),
        ]

    def mix(slots):
        count = len(slots)
        return pl.pallas_call(
            functools.partial(mix_kernel, slots, group, key_width),
            in_specs=[whole(), whole(pl.ANY), whole(pl.ANY)],
            out_specs=[whole()] * 3,
            out_shape=[shape(*dims) for dims in mix_shapes(count)],
            scratch_shapes=mix_scratch(count),
            compiler_params=params(),
            name="mix",
        )(edge, in_hbm(key_in), in_hbm(value_in))

    def solve(slots, start, logits, unit_keys, key_dots, mixed):
        count = len(slots)
        return pl.pallas_call(
            functools.partial(solve_kernel, slots, start, group, key_width, len(logits)),
            in_specs=[whole()] * (len(logits) + 7),
            out_specs=[whole()] * (count + 4),
            out_shape=solve_shapes(count),
            scratch_shapes=[VMEM((EDGE + 8, DK + 2 * DV), f32)],
            compiler_params=params(),
            name="solve",
        )(scales, *logits, unit_keys, key_dots, mixed, before, edge, pick)

    def mix_and_solve(slots, logits):
        count = len(slots)
        unit_shape, *others = mix_shapes(count)
        return pl.pallas_call(
            functools.partial(mix_and_solve_kernel, slots, group, key_width, len(logits)),
            in_specs=[whole()] * (len(logits) + 4) + [whole(pl.ANY)] * 2,
            out_specs=[whole()] * (count + 5),
            out_shape=solve_shapes(count) + [shape(*unit_shape)],
            scratch_shapes=[VMEM(dims, f32) for dims in others]
            + mix_scratch(count)
            + [VMEM((EDGE + 8, DK + 2 * DV), f32)],
            compiler_params=params(),
            name="mix_and_solve",
        )(scales, *logits, before, edge, pick, in_hbm(key_in), in_hbm(value_in))

    def query(slots, start, unit_keys, solved, starts, cumulative, first_keys):
        count = len(slots)
        return pl.pallas_call(
            functools.partial(query_kernel, slots, start, group),
            in_specs=[whole()] * 8,
            out_specs=[whole()] * 3,
            out_shape=[shape(count, 2, tokens, DV)]
            + [shape(count, 2, tokens, DK, dtype=bf16)] * 2,
            scratch_shapes=[VMEM((tokens + 8, DK), f32)],
            compiler_params=params(),
            cost_estimate=pl.CostEstimate(
                flops=2_000_000_000 * count, bytes_accessed=2_000_000 * count, transcendentals=0
            ),
            name="query",
        )(query_in, before, edge, unit_keys, first_keys, cumulative, solved, starts)

    calls = solve_calls(group)
    messages, rest = [], []
    early = sum(calls[:-1], ())
    early_mixed = mix(early)
    start = 0
    for slots in calls[:-1]:
        results = solve(slots, start, logits, *early_mixed)
        results, logits = lax.optimization_barrier((results, logits))
        messages += results[: len(slots)]
        rest.append([start, early_mixed[0], *results[len(slots) :]])
        start += len(slots)
    *results, unit_keys = mix_and_solve(calls[-1], logits)
    messages += results[:1]
    rest.append([0, unit_keys, *results[1:]])

    arrived = [None] * group
    for s in range(group):
        d = slot_partner(group, s)
        arrived[d] = (
            lax.ppermute(messages[s], "seq", [(i, i ^ d) for i in range(seq)]) if d else messages[s]
        )

    reads = []
    chain, leaving = pl.pallas_call(
        functools.partial(prefix_kernel, group),
        in_specs=[whole(pl.ANY)] * group,
        out_specs=[whole()] * 2,
        out_shape=[shape(group, 2, DK, 2 * DK), shape(2, DK, DV)],
        scratch_shapes=[VMEM((group, 2, DK, 2 * DK), f32), pltpu.SemaphoreType.DMA((group,))],
        compiler_params=params(),
        name="prefix",
    )(*arrived)
    leaving, rest = lax.optimization_barrier((leaving, [x[1:] for x in rest]))
    starts = [sum(len(c) for c in calls[:k]) for k in range(len(calls) - 1)] + [0]
    enter = pl.pallas_call(
        functools.partial(enter_kernel, group),
        in_specs=[whole()] * 2,
        out_specs=[whole()] * (group + 1),
        out_shape=[shape(2, DK, DV)] * (group + 1),
        compiler_params=params(),
        name="enter",
    )
    for hop in range(seq // group - 1):
        received = lax.ppermute(leaving, "seq", [(i, i + group) for i in range(seq - group)])
        if hop == 0:
            reads += [query(*x, *outs) for *x, outs in zip(calls[:-1], starts, rest)]
            received, reads = lax.optimization_barrier((received, reads))
        *entering, leaving = enter(received, chain)

    states = [entering[0]] + [
        lax.ppermute(entering[d], "seq", [(i, i ^ d) for i in range(seq)]) for d in range(1, group)
    ]
    reads.append(query(calls[-1], starts[-1], *rest[-1]))
    return pl.pallas_call(
        functools.partial(output_kernel, group, calls),
        in_specs=[whole()] * (3 * len(calls) + group),
        out_specs=whole(),
        out_shape=shape(tokens, value_width),
        compiler_params=params(),
        name="outputs",
    )(*[x for three in reads for x in three], *states)


def solution(mesh):
    placed = (
        P("seq", "head"),
        P("head", None),
        P("seq", "head"),
        P("seq", "head"),
        P("seq", "head"),
        P(None, "head"),
        P(None, "head"),
        P(None, "head"),
        P("head"),
        P("head"),
    )
    return jax.shard_map(
        per_device, mesh=mesh, in_specs=placed, out_specs=P("seq", "head"), check_vma=False
    )
```

```python
import functools
import math

import jax
import jax.numpy as jnp
import numpy as np
from jax import lax
from jax.experimental import pallas as pl
from jax.experimental.pallas import tpu as pltpu
from jax.sharding import PartitionSpec as P

DK = 128
DV = 128
KCONV = 4
BLOCK = 128
SUB = 16
EDGE = 16

f32 = jnp.float32
bf16 = jnp.bfloat16
VMEM = pltpu.VMEM
FAR = -1e30


def split(x):
    hi = x.astype(bf16)
    return hi, (x - hi.astype(f32)).astype(bf16)


def dot_split(a, b, contract=((1,), (0,))):
    (ah, al), (bh, bl) = a, b
    (ca,), (cb,) = contract
    left = jnp.concatenate([ah, al, ah], axis=ca)
    right = jnp.concatenate([bh, bh, bl], axis=cb)
    return lax.dot_general(left, right, (contract, ((), ())), preferred_element_type=f32)


NN = ((1,), (0,))
NT = ((1,), (1,))
TN = ((0,), (0,))


def silu(x):
    return x / (1.0 + jnp.exp(-x))


def unit(x, factor=1.0):
    return x * (lax.rsqrt(jnp.sum(x * x, axis=-1, keepdims=True) + 1e-6) * factor)


def conv_rows(padded_ref, taps, rows):
    total = taps[0:1] * padded_ref[pl.ds(8 - KCONV + 1, rows), :]
    for j in range(1, KCONV):
        total = total + taps[j : j + 1] * padded_ref[pl.ds(8 - KCONV + 1 + j, rows), :]
    return silu(total)


def iotas(rows=BLOCK, columns=BLOCK):
    return (
        lax.broadcasted_iota(jnp.int32, (rows, columns), 0),
        lax.broadcasted_iota(jnp.int32, (rows, columns), 1),
    )


def slot_partner(group, slot):
    order = [d for d in range(group - 1, 0, -1) if d % 2] + [
        d for d in range(group - 1, 0, -1) if d % 2 == 0
    ]
    return (order + [0])[slot]


def solve_calls(group):
    return [(0,), tuple(range(1, group - 1)), (group - 1,)] if group > 2 else [(0,), (1,)]


def in_hbm(x):
    return pltpu.with_memory_space_constraint(x, pltpu.HBM)


def rows_before(before_ref, columns):
    rows = before_ref[:, columns].astype(f32)[EDGE - 8 :]
    return jnp.where(lax.axis_index("seq") > 0, rows, 0.0)


def lanes(start, size):
    return pl.ds(pl.multiple_of(start, 128), size)


def logits_kernel(
    head_count,
    scale_ref,
    bias_ref,
    hidden_ref,
    proj_ref,
    q_first,
    k_first,
    v_first,
    q_last,
    k_last,
    v_last,
    q_taps,
    k_taps,
    v_taps,
    kept_ref,
    given_ref,
    tail_ref,
    edge_ref,
    scales_ref,
    held,
):
    rows = proj_ref.shape[0] // head_count
    everything = lax.dot_general(
        proj_ref[...], hidden_ref[...], (NT, ((), ())), preferred_element_type=f32
    )
    for m in range(head_count):
        held[m] = everything[m * rows : (m + 1) * rows]
    me = lax.axis_index("head")
    for n in range(head_count // 2):
        kept_ref[n] = held[me ^ (2 * n)]
        given_ref[n] = held[me ^ (2 * n + 1)]
    heads = rows // 2
    row, column = iotas(heads, heads)
    scale, bias = (
        jnp.sum(jnp.where(row == column, ref[...], 0.0), axis=1, keepdims=True)
        for ref in (scale_ref, bias_ref)
    )
    scales_ref[...] = jnp.broadcast_to(scale, scales_ref.shape)
    for h in range(heads):
        kept_ref[0, 2 * h : 2 * h + 1, :] = kept_ref[0, 2 * h : 2 * h + 1, :] + bias[h : h + 1]
    edge_ref[...] = jnp.zeros_like(edge_ref)
    start = 0
    for first, last, taps in ((q_first, q_last, q_taps), (k_first, k_last, k_taps), (v_first, v_last, v_taps)):
        here = slice(start, start + first.shape[1])
        tail_ref[:, here] = last[...]
        edge_ref[0:EDGE, here] = first[...].astype(f32)
        edge_ref[EDGE : EDGE + KCONV, here] = taps[...].astype(f32)
        start += first.shape[1]


def mix_kernel(slots, group, key_width, edge_ref, k_ref, v_ref, unit_ref, dots_ref, mixed_ref, k_held, v_held, padded, sems):
    tokens = k_ref.shape[0]
    place = lax.axis_index("seq") % group
    copies = []
    for at, s in enumerate(slots):
        p = place ^ slot_partner(group, s)
        copies.append(
            (
                pltpu.make_async_copy(k_ref.at[:, lanes(p * DK, DK)], k_held.at[at], sems.at[at, 0]),
                pltpu.make_async_copy(
                    v_ref.at[:, lanes(p * 2 * DV, 2 * DV)], v_held.at[at], sems.at[at, 1]
                ),
            )
        )
    for both in copies:
        for copy in both:
            copy.start()
    for at, s in enumerate(slots):
        p = place ^ slot_partner(group, s)
        key_taps = edge_ref[EDGE : EDGE + KCONV, lanes(key_width + p * DK, DK)]
        value_taps = edge_ref[EDGE : EDGE + KCONV, lanes(2 * key_width + p * 2 * DV, 2 * DV)]
        for n in range(3):
            padded[at, n, 0:8] = jnp.zeros((8, DK), f32)
        copies[at][0].wait()
        padded[at, 0, 8:] = k_held[at].astype(f32)
        keys = unit(conv_rows(padded.at[at, 0], key_taps, tokens))
        unit_ref[at] = keys
        for c in range(tokens // BLOCK):
            part = split(keys[c * BLOCK : (c + 1) * BLOCK])
            dots_ref[at, c] = dot_split(part, part, NT)
        copies[at][1].wait()
        for b in range(2):
            here = slice(b * DV, (b + 1) * DV)
            padded[at, 1 + b, 8:] = v_held[at, :, here].astype(f32)
            mixed_ref[at, :, here] = conv_rows(padded.at[at, 1 + b], value_taps[:, here], tokens)


def softplus(u):
    e = jnp.exp(-jnp.abs(u))
    small = e * (1.0 - e * (0.5 - e * (1.0 / 3.0 - e * (0.25 - e * 0.2))))
    return jnp.maximum(u, 0.0) + jnp.where(e < 0.03, small, jnp.log(1.0 + e))


def dot_wide(a, b):
    rows, columns = a[0].shape[0], b[0].shape[1]
    four = jnp.dot(
        jnp.concatenate(a, axis=0), jnp.concatenate(b, axis=1), preferred_element_type=f32
    )
    return four[:rows, :columns] + (four[:rows, columns:] + four[rows:, :columns])


def pick_matrix():
    row, column = np.arange(BLOCK)[:, None], np.arange((SUB - 1) * BLOCK)[None, :]
    pick = row == (column % BLOCK) // SUB * SUB + column // BLOCK
    return np.concatenate([pick, pick], axis=0).astype(bf16)


def invert_all(lowers, pick):
    count = len(lowers)
    row, column = iotas()
    blocks = (row // SUB) == (column // SUB)
    folded = []
    for lower in lowers:
        kept = jnp.where(blocks, lower, 0.0)
        total = kept[0:SUB]
        for b in range(1, BLOCK // SUB):
            total = total + kept[b * SUB : (b + 1) * SUB]
        folded.append(total)
    spread = jnp.concatenate(split(jnp.concatenate(folded, axis=0)), axis=1)
    wide = jnp.dot(spread, pick, preferred_element_type=f32).reshape(
        count, SUB, (SUB - 1) * BLOCK
    )
    srow, scolumn = iotas(SUB, BLOCK)
    inverse = jnp.broadcast_to(
        jnp.where(srow == scolumn % SUB, 1.0, 0.0)[None], (count, SUB, BLOCK)
    )
    for j in range(SUB - 1):
        inverse = inverse - wide[:, :, j * BLOCK : (j + 1) * BLOCK] * inverse[:, j : j + 1, :]
    inverses = [inverse[i] for i in range(count)]
    halves = [split(x) for x in lowers]
    size = SUB
    while size < BLOCK:
        same = (row // size) == (column // size)
        across = ((row // (2 * size)) == (column // (2 * size))) & ((row // size) > (column // size))
        same, across = (jnp.where(m, 1.0, 0.0).astype(bf16) for m in (same, across))
        odd = iotas(size, BLOCK)[1] // size % 2 == 1
        dot = dot_wide if size < 64 else dot_split
        parts = [split(x) for x in inverses]
        if 2 * size < BLOCK:
            first = [dot(x, tuple(h * across for h in low)) for x, low in zip(parts, halves)]
        else:
            first = [
                dot(split(jnp.where(odd, x, 0.0)), low) for x, low in zip(inverses, halves)
            ]
        spread = [
            tuple(jnp.concatenate([h] * (BLOCK // size), axis=0) * same for h in x) for x in parts
        ]
        second = [dot(split(x), y) for x, y in zip(first, spread)]
        inverses = [
            jnp.concatenate([jnp.where(odd, 0.0, x), jnp.where(odd, x, -y)], axis=0)
            for x, y in zip(inverses, second)
        ]
        size *= 2
    return inverses


def followed(later, both):
    added, move = later
    both = dot_split(split(move), split(both))
    return jnp.concatenate([both[:, :DV] + added, both[:, DV:]], axis=1)


def solve_kernel(
    slots,
    start,
    group,
    key_width,
    pieces,
    scales_ref,
    *refs,
):
    logit_refs, refs = refs[:pieces], refs[pieces:]
    (unit_ref, dots_ref, mixed_ref, before_ref, edge_ref, pick_ref), refs = refs[:6], refs[6:]
    count = len(slots)
    message_refs, refs = refs[:count], refs[count:]
    solved_ref, starts_ref, cumulative_ref, first_ref, padded = refs
    tokens = unit_ref.shape[1]
    blocks = tokens // BLOCK
    place = lax.axis_index("seq") % group
    row, column = iotas()
    upper = jnp.where(row <= column, 1.0, 0.0)
    identity = row == column
    strict = row > column

    systems, rights, tails, ends, key_parts = [], [], [], [], []
    for at, s in enumerate(slots):
        p = place ^ slot_partner(group, s)
        kcol, vcol = lanes(key_width + p * DK, DK), lanes(2 * key_width + p * 2 * DV, 2 * DV)
        key_taps = edge_ref[EDGE : EDGE + KCONV, kcol]
        value_taps = edge_ref[EDGE : EDGE + KCONV, vcol]
        padded[0, 0:8] = rows_before(before_ref, kcol)
        padded[0, 8:] = edge_ref[0:EDGE, kcol]
        edge_keys = unit(conv_rows(padded.at[0], key_taps, EDGE))
        first_values, edge_values = rows_before(before_ref, vcol), edge_ref[0:EDGE, vcol]
        edges = []
        for b in range(2):
            here = slice(b * DV, (b + 1) * DV)
            padded[1 + b, 0:8] = first_values[:, here]
            padded[1 + b, 8:] = edge_values[:, here]
            edges.append(conv_rows(padded.at[1 + b], value_taps[:, here], EDGE))
        edge_values = jnp.concatenate(edges, axis=1)
        decays, rates = [], []
        for b in range(2):
            h = 2 * p + b
            u = logit_refs[0][0, pl.ds(2 * h, 1), :] + logit_refs[1][0, pl.ds(2 * h, 1), :]
            w = logit_refs[0][0, pl.ds(2 * h + 1, 1), :] + logit_refs[1][0, pl.ds(2 * h + 1, 1), :]
            for ref in logit_refs[2:]:
                u = u + ref[pl.ds(2 * h, 1), :]
                w = w + ref[pl.ds(2 * h + 1, 1), :]
            decays.append(-scales_ref[pl.ds(h, 1), :] * softplus(u))
            rates.append(1.0 / (1.0 + jnp.exp(-w)))
        decay_rows = jnp.concatenate(
            [d[:, c * BLOCK : (c + 1) * BLOCK] for d in decays for c in range(blocks)], axis=0
        )
        rate_rows = jnp.concatenate(
            [r[:, c * BLOCK : (c + 1) * BLOCK] for r in rates for c in range(blocks)], axis=0
        )
        sums = jnp.dot(
            decay_rows, upper, precision=lax.Precision.HIGHEST, preferred_element_type=f32
        )
        cumulative_ref[at] = sums
        cum_columns = jnp.transpose(sums)
        rate_columns = jnp.transpose(rate_rows)
        growth_columns = jnp.exp(cum_columns)
        last = sums[:, BLOCK - 1 : BLOCK]
        tail_columns = jnp.exp(jnp.transpose(last - sums))
        end_values = jnp.exp(last)
        for c in range(blocks):
            keys = unit_ref[start + at, pl.ds(c * BLOCK, BLOCK), :]
            values = mixed_ref[start + at, pl.ds(c * BLOCK, BLOCK), :]
            if c == 0:
                keys = jnp.concatenate([edge_keys, keys[EDGE:]], axis=0)
                values = jnp.concatenate([edge_values, values[EDGE:]], axis=0)
                first_ref[at] = keys
            parts = split(keys)
            key_parts.append(parts)
            dots = dot_split(parts, parts, NT) if c == 0 else dots_ref[start + at, c]
            for b in range(2):
                r = b * blocks + c
                rate = rate_columns[:, r : r + 1]
                spread = cum_columns[:, r : r + 1] - sums[r : r + 1, :]
                table = jnp.exp(jnp.where(strict, spread, FAR))
                systems.append(rate * table * dots)
                rights.append(
                    jnp.concatenate(
                        [
                            rate * values[:, b * DV : (b + 1) * DV],
                            (rate * growth_columns[:, r : r + 1]) * keys,
                        ],
                        axis=1,
                    )
                )
                tails.append(tail_columns[:, r : r + 1])
                ends.append(end_values[r : r + 1, :])

    inverses = invert_all(systems, pick_ref[...])
    solved = [dot_split(split(x), split(r)) for x, r in zip(inverses, rights)]
    for at in range(count):
        moves = {}
        for c in range(blocks):
            i = (at * blocks + c) * 2
            both = jnp.concatenate([tails[i] * solved[i], tails[i + 1] * solved[i + 1]], axis=1)
            grown = dot_split(key_parts[at * blocks + c], split(both), TN)
            for b in range(2):
                solved_ref[at, b, pl.ds(c * BLOCK, BLOCK), :] = solved[i + b]
                added = grown[:, b * 2 * DK : b * 2 * DK + DV]
                move = (
                    jnp.where(identity, ends[i + b], 0.0)
                    - grown[:, b * 2 * DK + DV : (b + 1) * 2 * DK]
                )
                moves[b, c] = (added, move)
        for b in range(2):
            half = blocks // 2
            parts = []
            for begin in (0, half):
                both = jnp.concatenate(moves[b, begin], axis=1)
                for c in range(begin + 1, begin + half):
                    if begin == 0:
                        starts_ref[at, b, c - 1] = both
                    both = followed(moves[b, c], both)
                parts.append(both)
            both = parts[0]
            for c in range(half, blocks):
                starts_ref[at, b, c - 1] = both
                if c < blocks - 1:
                    both = followed(moves[b, c], both)
            both = followed((parts[1][:, :DV], parts[1][:, DV:]), parts[0])
            message_refs[at][b] = both


def query_kernel(
    slots,
    start,
    group,
    q_ref,
    before_ref,
    edge_ref,
    unit_ref,
    first_ref,
    cumulative_ref,
    solved_ref,
    starts_ref,
    own_ref,
    high_ref,
    low_ref,
    padded,
):
    place = lax.axis_index("seq") % group
    tokens = q_ref.shape[0]
    blocks = tokens // BLOCK
    row, column = iotas()
    causal = row >= column
    work = []
    for at, s in enumerate(slots):
        p = place ^ slot_partner(group, s)
        columns = lanes(p * DK, DK)
        padded[0:8] = rows_before(before_ref, columns)
        padded[8:] = q_ref[:, columns].astype(f32)
        taps = edge_ref[EDGE : EDGE + KCONV, columns]
        queries = unit(conv_rows(padded, taps, tokens), 1.0 / math.sqrt(DK))
        sums = cumulative_ref[at]
        cum_columns = jnp.transpose(sums)
        growth_columns = jnp.exp(cum_columns)
        for c in range(blocks):
            here = queries[c * BLOCK : (c + 1) * BLOCK]
            keys = first_ref[at] if c == 0 else unit_ref[start + at, pl.ds(c * BLOCK, BLOCK), :]
            dots = dot_split(split(here), split(keys), NT)
            for b in range(2):
                r = b * blocks + c
                spread = cum_columns[:, r : r + 1] - sums[r : r + 1, :]
                attend = dots * jnp.exp(jnp.where(causal, spread, FAR))
                grown = growth_columns[:, r : r + 1] * here
                work.append((at, b, c, split(attend), grown))
    seen = [
        dot_split(attend, split(solved_ref[at, b, pl.ds(c * BLOCK, BLOCK), :]))
        for at, b, c, attend, grown in work
    ]
    for (at, b, c, attend, grown), one in zip(work, seen):
        own, reads = one[:, :DV], grown - one[:, DV:]
        if c > 0:
            through = dot_split(split(reads), split(starts_ref[at, b, c - 1]))
            own, reads = own + through[:, :DV], through[:, DV:]
        here = pl.ds(c * BLOCK, BLOCK)
        own_ref[at, b, here, :] = own
        high_ref[at, b, here, :], low_ref[at, b, here, :] = split(reads)


def prefix_kernel(group, *refs):
    messages, refs = refs[:group], refs[group:]
    chain_ref, leaving_ref, held, sems = refs
    place = lax.axis_index("seq") % group
    copies = [
        pltpu.make_async_copy(messages[d], held.at[place ^ d], sems.at[d]) for d in range(group)
    ]
    for copy in copies:
        copy.start()
    for copy in copies:
        copy.wait()
    heads = leaving_ref.shape[0]
    chain = [held[0, b] for b in range(heads)]
    for i in range(1, group):
        for b in range(heads):
            chain_ref[i - 1, b] = chain[b]
        chain = [
            dot_split(split(held[i, b, :, DV:]), split(chain[b])) for b in range(heads)
        ]
        chain = [
            jnp.concatenate([chain[b][:, :DV] + held[i, b, :, 0:DV], chain[b][:, DV:]], axis=1)
            for b in range(heads)
        ]
    for b in range(heads):
        chain_ref[group - 1, b] = chain[b]
        leaving_ref[b] = chain[b][:, :DV]


def enter_kernel(group, onward, entering_ref, chain_ref, *refs):
    outs = refs[:group]
    place = lax.axis_index("seq") % group
    heads = entering_ref.shape[0]
    count = group if onward else group - 1
    states = [[entering_ref[b] for b in range(heads)]] + [[] for i in range(count)]
    for b in range(heads):
        moves = jnp.concatenate([chain_ref[i, b, :, DV:] for i in range(count)], axis=0)
        moved = dot_split(split(moves), split(states[0][b]))
        for i in range(count):
            states[i + 1].append(chain_ref[i, b, :, 0:DV] + moved[i * DK : (i + 1) * DK])
    if onward:
        for b in range(heads):
            refs[group][b] = states[group][b]
    for j in range(group):

        @pl.when(place == j)
        def _():
            for i in range(group):
                for b in range(heads):
                    outs[j ^ i][b] = states[i][b]


def output_kernel(group, slots, *refs):
    reads, refs = refs[: 3 * len(slots)], refs[3 * len(slots) :]
    entering, (out_ref, held, sems) = refs[: len(slots)], refs[-3:]
    place = lax.axis_index("seq") % group
    copies = []
    for n, (s, at) in enumerate(slots):
        own_ref, high_ref, low_ref = reads[3 * n : 3 * n + 3]
        p = place ^ slot_partner(group, s)
        for b in range(2):
            product = dot_split((high_ref[at, b], low_ref[at, b]), split(entering[n][b]))
            held[n, :, b * DV : (b + 1) * DV] = own_ref[at, b] + product
        copies.append(
            pltpu.make_async_copy(held.at[n], out_ref.at[:, lanes(p * 2 * DV, 2 * DV)], sems.at[n])
        )
        copies[-1].start()
    for copy in copies:
        copy.wait()


def shape(*dims, dtype=f32):
    return jax.ShapeDtypeStruct(dims, dtype)


def params(mib=24):
    return pltpu.CompilerParams(vmem_limit_bytes=mib << 20)


def whole(space=VMEM):
    return pl.BlockSpec(memory_space=space)


def per_device(
    hidden_states,
    proj_ba,
    query_in,
    key_in,
    value_in,
    conv_query,
    conv_key,
    convolution_value_taps,
    decay_scale,
    dt_bias,
):
    tokens = hidden_states.shape[0]
    heads = decay_scale.shape[0]
    pairs = key_in.shape[1] // DK
    blocks = tokens // BLOCK
    key_width, value_width = key_in.shape[1], value_in.shape[1]
    seq, head_count = lax.axis_size("seq"), lax.axis_size("head")
    group = pairs

    def full(block):
        return pl.BlockSpec(block, lambda i: (0,) * len(block))

    last_rows = tokens // EDGE - 1
    width = 2 * key_width + value_width
    inputs = (query_in, key_in, value_in)
    taps = (conv_query, conv_key, convolution_value_taps)
    kept, given, tail, edge, scales = pl.pallas_call(
        functools.partial(logits_kernel, head_count),
        grid=(1,),
        in_specs=[full((1, heads))] * 2 + [full(hidden_states.shape), full(proj_ba.shape[::-1])]
        + [pl.BlockSpec((EDGE, x.shape[1]), lambda i: (0, 0)) for x in inputs]
        + [pl.BlockSpec((EDGE, x.shape[1]), lambda i: (last_rows, 0)) for x in inputs]
        + [full(x.shape) for x in taps],
        out_specs=[whole()] * 5,
        out_shape=[shape(head_count // 2, 2 * heads, tokens)] * 2
        + [shape(EDGE, width, dtype=bf16), shape(EDGE + 8, width), shape(heads, tokens)],
        scratch_shapes=[VMEM((head_count, 2 * heads, tokens), f32)],
        compiler_params=params(),
        name="logits",
    )(
        *[in_hbm(x.reshape(1, heads)) for x in (decay_scale, dt_bias)],
        *[in_hbm(x) for x in (hidden_states, proj_ba.T, *inputs, *inputs, *taps)],
    )

    taken = lax.ppermute(given, "head", [(i, i ^ 1) for i in range(head_count)])
    logits = [kept, taken] + [
        lax.ppermute(kept[n] + taken[n], "head", [(i, i ^ (2 * n)) for i in range(head_count)])
        for n in range(1, head_count // 2)
    ]
    before = lax.ppermute(tail, "seq", [(i, (i + 1) % seq) for i in range(seq)])

    pick = jnp.asarray(pick_matrix())

    def mix_shapes(count):
        return [(count, tokens, DK), (count, blocks, BLOCK, BLOCK), (count, tokens, 2 * DV)]

    def mix_scratch(count):
        return [
            VMEM((count, tokens, DK), bf16),
            VMEM((count, tokens, 2 * DV), bf16),
            VMEM((count, 3, tokens + 8, DK), f32),
            pltpu.SemaphoreType.DMA((count, 2)),
        ]

    def solve_shapes(count):
        return [shape(2, DK, 2 * DK)] * count + [
            shape(count, 2, tokens, 2 * DK),
            shape(count, 2, blocks - 1, DK, 2 * DK),
            shape(count, 2 * blocks, BLOCK),
            shape(count, BLOCK, DK),
        ]

    def mix(slots):
        count = len(slots)
        return pl.pallas_call(
            functools.partial(mix_kernel, slots, group, key_width),
            in_specs=[whole(), whole(pl.ANY), whole(pl.ANY)],
            out_specs=[whole()] * 3,
            out_shape=[shape(*dims) for dims in mix_shapes(count)],
            scratch_shapes=mix_scratch(count),
            compiler_params=params(),
            name="mix",
        )(edge, in_hbm(key_in), in_hbm(value_in))

    def solve(slots, start, logits, unit_keys, key_dots, mixed):
        count = len(slots)
        return pl.pallas_call(
            functools.partial(solve_kernel, slots, start, group, key_width, len(logits)),
            in_specs=[whole()] * (len(logits) + 7),
            out_specs=[whole()] * (count + 4),
            out_shape=solve_shapes(count),
            scratch_shapes=[VMEM((3, EDGE + 8, DK), f32)],
            compiler_params=params(),
            name="solve",
        )(scales, *logits, unit_keys, key_dots, mixed, before, edge, pick)

    def query(slots, start, unit_keys, solved, starts, cumulative, first_keys):
        count = len(slots)
        return pl.pallas_call(
            functools.partial(query_kernel, slots, start, group),
            in_specs=[whole()] * 8,
            out_specs=[whole()] * 3,
            out_shape=[shape(count, 2, tokens, DV)]
            + [shape(count, 2, tokens, DK, dtype=bf16)] * 2,
            scratch_shapes=[VMEM((tokens + 8, DK), f32)],
            compiler_params=params(),
            cost_estimate=pl.CostEstimate(
                flops=2_000_000_000 * count, bytes_accessed=2_000_000 * count, transcendentals=0
            ),
            name="query",
        )(query_in, before, edge, unit_keys, first_keys, cumulative, solved, starts)

    calls = solve_calls(group)
    mixed = mix(sum(calls, ()))
    messages, rest, start = [], [], 0
    for slots in calls:
        results = solve(slots, start, logits, *mixed)
        results, logits = lax.optimization_barrier((results, logits))
        messages += results[: len(slots)]
        rest.append([mixed[0], *results[len(slots) :]])
        start += len(slots)

    arrived = [None] * group
    for s in range(group):
        d = slot_partner(group, s)
        arrived[d] = (
            lax.ppermute(messages[s], "seq", [(i, i ^ d) for i in range(seq)]) if d else messages[s]
        )

    messages[-1], rest[0] = lax.optimization_barrier((messages[-1], rest[0]))
    reads = [query(calls[0], 0, *rest[0])]
    arrived, reads = lax.optimization_barrier((arrived, reads))
    chain, leaving = pl.pallas_call(
        functools.partial(prefix_kernel, group),
        in_specs=[whole(pl.ANY)] * group,
        out_specs=[whole()] * 2,
        out_shape=[shape(group, 2, DK, 2 * DK), shape(2, DK, DV)],
        scratch_shapes=[VMEM((group, 2, DK, 2 * DK), f32), pltpu.SemaphoreType.DMA((group,))],
        compiler_params=params(),
        name="prefix",
    )(*arrived)
    leaving, rest = lax.optimization_barrier((leaving, rest))
    starts = [sum(len(c) for c in calls[:k]) for k in range(len(calls))]
    def enter(received, onward):
        return pl.pallas_call(
            functools.partial(enter_kernel, group, onward),
            in_specs=[whole()] * 2,
            out_specs=[whole()] * (group + onward),
            out_shape=[shape(2, DK, DV)] * (group + onward),
            compiler_params=params(),
            name="enter",
        )(received, chain)

    hops = seq // group - 1
    if not hops:
        entering = enter(jnp.zeros((2, DK, DV), f32), False)
    for hop in range(hops):
        received = lax.ppermute(leaving, "seq", [(i, i + group) for i in range(seq - group)])
        if hop == 0:
            reads += [query(*x, *outs) for *x, outs in zip(calls[1:-1], starts[1:-1], rest[1:-1])]
            received, reads, rest = lax.optimization_barrier((received, reads, rest))
        entering = enter(received, hop < hops - 1)
        if hop < hops - 1:
            *entering, leaving = entering

    states = {0: entering[0]}
    for d in range(group - 1, 0, -1):
        states[d] = lax.ppermute(entering[d], "seq", [(i, i ^ d) for i in range(seq)])
    reads.append(query(calls[-1], starts[-1], *rest[-1]))
    where = {s: (k, at) for k, slots in enumerate(calls) for at, s in enumerate(slots)}

    def outputs(slots, written):
        operands = [x for s in slots for x in reads[where[s][0]]]
        operands += [states[slot_partner(group, s)] for s in slots]
        return pl.pallas_call(
            functools.partial(output_kernel, group, [(s, where[s][1]) for s in slots]),
            in_specs=[whole()] * len(operands) + [whole(pl.ANY)] * len(written),
            out_specs=whole(pl.ANY),
            out_shape=shape(tokens, value_width),
            scratch_shapes=[
                VMEM((len(slots), tokens, 2 * DV), f32),
                pltpu.SemaphoreType.DMA((len(slots),)),
            ],
            input_output_aliases={len(operands): 0} if written else {},
            compiler_params=params(),
            name="outputs",
        )(*operands, *written)

    first = [s for s in range(group) if slot_partner(group, s) < 1]
    written = outputs(first, [])
    return outputs([s for s in range(group) if s not in first], [written])


def solution(mesh):
    placed = (
        P("seq", "head"),
        P("head", None),
        P("seq", "head"),
        P("seq", "head"),
        P("seq", "head"),
        P(None, "head"),
        P(None, "head"),
        P(None, "head"),
        P("head"),
        P("head"),
    )
    return jax.shard_map(
        per_device, mesh=mesh, in_specs=placed, out_specs=P("seq", "head"), check_vma=False
    )
```

```python
import functools
import math

import jax
import jax.numpy as jnp
import numpy as np
from jax import lax
from jax.experimental import pallas as pl
from jax.experimental.pallas import tpu as pltpu
from jax.sharding import PartitionSpec as P

DK = 128
DV = 128
KCONV = 4
BLOCK = 128
SUB = 16
EDGE = 16

f32 = jnp.float32
bf16 = jnp.bfloat16
VMEM = pltpu.VMEM
FAR = -1e30


def split(x):
    hi = x.astype(bf16)
    return hi, (x - hi.astype(f32)).astype(bf16)


def dot_split(a, b, contract=((1,), (0,))):
    (ah, al), (bh, bl) = a, b
    (ca,), (cb,) = contract
    left = jnp.concatenate([ah, al, ah], axis=ca)
    right = jnp.concatenate([bh, bh, bl], axis=cb)
    return lax.dot_general(left, right, (contract, ((), ())), preferred_element_type=f32)


NN = ((1,), (0,))
NT = ((1,), (1,))
TN = ((0,), (0,))


def silu(x):
    return x / (1.0 + jnp.exp(-x))


def unit(x, factor=1.0):
    return x * (lax.rsqrt(jnp.sum(x * x, axis=-1, keepdims=True) + 1e-6) * factor)


def conv_rows(padded_ref, taps, rows):
    total = taps[0:1] * padded_ref[pl.ds(8 - KCONV + 1, rows), :]
    for j in range(1, KCONV):
        total = total + taps[j : j + 1] * padded_ref[pl.ds(8 - KCONV + 1 + j, rows), :]
    return silu(total)


def iotas(rows=BLOCK, columns=BLOCK):
    return (
        lax.broadcasted_iota(jnp.int32, (rows, columns), 0),
        lax.broadcasted_iota(jnp.int32, (rows, columns), 1),
    )


def slot_partner(group, slot):
    order = [d for d in range(group - 1, 0, -1) if d % 2] + [
        d for d in range(group - 1, 0, -1) if d % 2 == 0
    ]
    return (order + [0])[slot]


def solve_calls(group):
    return [(0,), tuple(range(1, group - 1)), (group - 1,)] if group > 2 else [(0,), (1,)]


def in_hbm(x):
    return pltpu.with_memory_space_constraint(x, pltpu.HBM)


def rows_before(before_ref, columns):
    rows = before_ref[:, columns].astype(f32)[EDGE - 8 :]
    return jnp.where(lax.axis_index("seq") > 0, rows, 0.0)


def lanes(start, size):
    return pl.ds(pl.multiple_of(start, 128), size)


def logits_kernel(
    head_count,
    scale_ref,
    bias_ref,
    hidden_ref,
    proj_ref,
    q_first,
    k_first,
    v_first,
    q_last,
    k_last,
    v_last,
    q_taps,
    k_taps,
    v_taps,
    kept_ref,
    given_ref,
    tail_ref,
    edge_ref,
    scales_ref,
    held,
):
    rows = proj_ref.shape[0] // head_count
    everything = lax.dot_general(
        proj_ref[...], hidden_ref[...], (NT, ((), ())), preferred_element_type=f32
    )
    for m in range(head_count):
        held[m] = everything[m * rows : (m + 1) * rows]
    me = lax.axis_index("head")
    for n in range(head_count // 2):
        kept_ref[n] = held[me ^ (2 * n)]
        given_ref[n] = held[me ^ (2 * n + 1)]
    heads = rows // 2
    row, column = iotas(heads, heads)
    scale, bias = (
        jnp.sum(jnp.where(row == column, ref[...], 0.0), axis=1, keepdims=True)
        for ref in (scale_ref, bias_ref)
    )
    scales_ref[...] = jnp.broadcast_to(scale, scales_ref.shape)
    for h in range(heads):
        kept_ref[0, 2 * h : 2 * h + 1, :] = kept_ref[0, 2 * h : 2 * h + 1, :] + bias[h : h + 1]
    edge_ref[...] = jnp.zeros_like(edge_ref)
    start = 0
    for first, last, taps in ((q_first, q_last, q_taps), (k_first, k_last, k_taps), (v_first, v_last, v_taps)):
        here = slice(start, start + first.shape[1])
        tail_ref[:, here] = last[...]
        edge_ref[0:EDGE, here] = first[...].astype(f32)
        edge_ref[EDGE : EDGE + KCONV, here] = taps[...].astype(f32)
        start += first.shape[1]


def mix_kernel(slots, group, key_width, edge_ref, k_ref, v_ref, unit_ref, dots_ref, mixed_ref, k_held, v_held, padded, sems):
    tokens = k_ref.shape[0]
    place = lax.axis_index("seq") % group
    copies = []
    for at, s in enumerate(slots):
        p = place ^ slot_partner(group, s)
        copies.append(
            (
                pltpu.make_async_copy(k_ref.at[:, lanes(p * DK, DK)], k_held.at[at], sems.at[at, 0]),
                pltpu.make_async_copy(
                    v_ref.at[:, lanes(p * 2 * DV, 2 * DV)], v_held.at[at], sems.at[at, 1]
                ),
            )
        )
    for both in copies:
        for copy in both:
            copy.start()
    for at, s in enumerate(slots):
        p = place ^ slot_partner(group, s)
        key_taps = edge_ref[EDGE : EDGE + KCONV, lanes(key_width + p * DK, DK)]
        value_taps = edge_ref[EDGE : EDGE + KCONV, lanes(2 * key_width + p * 2 * DV, 2 * DV)]
        for n in range(3):
            padded[at, n, 0:8] = jnp.zeros((8, DK), f32)
        copies[at][0].wait()
        padded[at, 0, 8:] = k_held[at].astype(f32)
        keys = unit(conv_rows(padded.at[at, 0], key_taps, tokens))
        unit_ref[at] = keys
        for c in range(1, tokens // BLOCK):
            part = split(keys[c * BLOCK : (c + 1) * BLOCK])
            dots_ref[at, c - 1] = dot_split(part, part, NT)
        copies[at][1].wait()
        for b in range(2):
            here = slice(b * DV, (b + 1) * DV)
            padded[at, 1 + b, 8:] = v_held[at, :, here].astype(f32)
            mixed_ref[at, :, here] = conv_rows(padded.at[at, 1 + b], value_taps[:, here], tokens)


def softplus(u):
    e = jnp.exp(-jnp.abs(u))
    small = e * (1.0 - e * (0.5 - e * (1.0 / 3.0 - e * (0.25 - e * 0.2))))
    return jnp.maximum(u, 0.0) + jnp.where(e < 0.03, small, jnp.log(1.0 + e))


def dot_wide(a, b):
    rows, columns = a[0].shape[0], b[0].shape[1]
    four = jnp.dot(
        jnp.concatenate(a, axis=0), jnp.concatenate(b, axis=1), preferred_element_type=f32
    )
    return four[:rows, :columns] + (four[:rows, columns:] + four[rows:, :columns])


def pick_matrix():
    row, column = np.arange(BLOCK)[:, None], np.arange((SUB - 1) * BLOCK)[None, :]
    pick = row == (column % BLOCK) // SUB * SUB + column // BLOCK
    return np.concatenate([pick, pick], axis=0).astype(bf16)


def invert_all(lowers, pick):
    count = len(lowers)
    row, column = iotas()
    blocks = (row // SUB) == (column // SUB)
    folded = []
    for lower in lowers:
        kept = jnp.where(blocks, lower, 0.0)
        total = kept[0:SUB]
        for b in range(1, BLOCK // SUB):
            total = total + kept[b * SUB : (b + 1) * SUB]
        folded.append(total)
    spread = jnp.concatenate(split(jnp.concatenate(folded, axis=0)), axis=1)
    wide = jnp.dot(spread, pick, preferred_element_type=f32).reshape(
        count, SUB, (SUB - 1) * BLOCK
    )
    srow, scolumn = iotas(SUB, BLOCK)
    inverse = jnp.broadcast_to(
        jnp.where(srow == scolumn % SUB, 1.0, 0.0)[None], (count, SUB, BLOCK)
    )
    for j in range(SUB - 1):
        inverse = inverse - wide[:, :, j * BLOCK : (j + 1) * BLOCK] * inverse[:, j : j + 1, :]
    inverses = [inverse[i] for i in range(count)]
    halves = [split(x) for x in lowers]
    size = SUB
    while size < BLOCK:
        same = (row // size) == (column // size)
        across = ((row // (2 * size)) == (column // (2 * size))) & ((row // size) > (column // size))
        same, across = (jnp.where(m, 1.0, 0.0).astype(bf16) for m in (same, across))
        odd = iotas(size, BLOCK)[1] // size % 2 == 1
        dot = dot_wide if size < 64 else dot_split
        parts = [split(x) for x in inverses]
        if 2 * size < BLOCK:
            first = [dot(x, tuple(h * across for h in low)) for x, low in zip(parts, halves)]
        else:
            first = [
                dot(split(jnp.where(odd, x, 0.0)), low) for x, low in zip(inverses, halves)
            ]
        spread = [
            tuple(jnp.concatenate([h] * (BLOCK // size), axis=0) * same for h in x) for x in parts
        ]
        second = [dot(split(x), y) for x, y in zip(first, spread)]
        inverses = [
            jnp.concatenate([jnp.where(odd, 0.0, x), jnp.where(odd, x, -y)], axis=0)
            for x, y in zip(inverses, second)
        ]
        size *= 2
    return inverses


def followed(later, both):
    added, move = later
    both = dot_split(split(move), split(both))
    return jnp.concatenate([both[:, :DV] + added, both[:, DV:]], axis=1)


def gates(p, scales_ref, logit_refs):
    row, column = iotas()
    decays, rates = [], []
    for b in range(2):
        h = 2 * p + b
        u = logit_refs[0][0, pl.ds(2 * h, 1), :] + logit_refs[1][0, pl.ds(2 * h, 1), :]
        w = logit_refs[0][0, pl.ds(2 * h + 1, 1), :] + logit_refs[1][0, pl.ds(2 * h + 1, 1), :]
        for ref in logit_refs[2:]:
            u = u + ref[pl.ds(2 * h, 1), :]
            w = w + ref[pl.ds(2 * h + 1, 1), :]
        decays.append(-scales_ref[pl.ds(h, 1), :] * softplus(u))
        rates.append(1.0 / (1.0 + jnp.exp(-w)))
    blocks = decays[0].shape[1] // BLOCK
    decay_rows, rate_rows = (
        jnp.concatenate(
            [x[:, c * BLOCK : (c + 1) * BLOCK] for x in both for c in range(blocks)], axis=0
        )
        for both in (decays, rates)
    )
    sums = jnp.dot(
        decay_rows,
        jnp.where(row <= column, 1.0, 0.0),
        precision=lax.Precision.HIGHEST,
        preferred_element_type=f32,
    )
    last = sums[:, BLOCK - 1 : BLOCK]
    columns = jnp.concatenate(
        [
            jnp.transpose(x)
            for x in (sums, rate_rows, rate_rows * jnp.exp(sums), jnp.exp(last - sums))
        ],
        axis=1,
    )
    return jnp.concatenate([sums, jnp.broadcast_to(jnp.exp(last), sums.shape)], axis=0), columns


def solve_kernel(
    slots,
    start,
    group,
    key_width,
    pieces,
    *refs,
):
    if pieces:
        (scales_ref, *logit_refs), refs = refs[: 1 + pieces], refs[1 + pieces :]
    else:
        (rows_ref, columns_ref), refs = refs[:2], refs[2:]
    (unit_ref, dots_ref, mixed_ref, before_ref, edge_ref, pick_ref), refs = refs[:6], refs[6:]
    count = len(slots)
    message_refs, refs = refs[:count], refs[count:]
    (solved_ref, starts_ref, first_ref), refs = refs[:3], refs[3:]
    if pieces:
        (rows_ref, columns_ref), refs = refs[:2], refs[2:]
    (padded,) = refs
    tokens = unit_ref.shape[1]
    blocks = tokens // BLOCK
    height = 2 * blocks
    place = lax.axis_index("seq") % group
    row, column = iotas()
    identity = row == column
    strict = row > column

    known = {}
    if pieces:
        for s in range(group):
            known[s] = gates(place ^ slot_partner(group, s), scales_ref, logit_refs)
            rows_ref[s], columns_ref[s] = known[s]
    systems, rights, tails, ends, key_parts = [], [], [], [], []
    for at, s in enumerate(slots):
        p = place ^ slot_partner(group, s)
        kcol, vcol = lanes(key_width + p * DK, DK), lanes(2 * key_width + p * 2 * DV, 2 * DV)
        rows, columns = known[s] if s in known else (rows_ref[s], columns_ref[s])
        key_taps = edge_ref[EDGE : EDGE + KCONV, kcol]
        value_taps = edge_ref[EDGE : EDGE + KCONV, vcol]
        padded[0, 0:8] = rows_before(before_ref, kcol)
        padded[0, 8:] = edge_ref[0:EDGE, kcol]
        edge_keys = unit(conv_rows(padded.at[0], key_taps, EDGE))
        first_values, edge_values = rows_before(before_ref, vcol), edge_ref[0:EDGE, vcol]
        edges = []
        for b in range(2):
            here = slice(b * DV, (b + 1) * DV)
            padded[1 + b, 0:8] = first_values[:, here]
            padded[1 + b, 8:] = edge_values[:, here]
            edges.append(conv_rows(padded.at[1 + b], value_taps[:, here], EDGE))
        edge_values = jnp.concatenate(edges, axis=1)
        for c in range(blocks):
            keys = unit_ref[start + at, pl.ds(c * BLOCK, BLOCK), :]
            values = mixed_ref[start + at, pl.ds(c * BLOCK, BLOCK), :]
            if c == 0:
                keys = jnp.concatenate([edge_keys, keys[EDGE:]], axis=0)
                values = jnp.concatenate([edge_values, values[EDGE:]], axis=0)
                first_ref[at] = keys
            parts = split(keys)
            key_parts.append(parts)
            dots = dot_split(parts, parts, NT) if c == 0 else dots_ref[start + at, c - 1]
            for b in range(2):
                r = b * blocks + c
                cum, rate, scaled, tail = (
                    columns[:, n * height + r : n * height + r + 1] for n in range(4)
                )
                spread = cum - rows[r : r + 1, :]
                table = jnp.exp(jnp.where(strict, spread, FAR))
                systems.append(rate * table * dots)
                rights.append(
                    jnp.concatenate(
                        [
                            rate * values[:, b * DV : (b + 1) * DV],
                            scaled * keys,
                        ],
                        axis=1,
                    )
                )
                tails.append(tail)
                ends.append(rows[height + r : height + r + 1, :])

    inverses = invert_all(systems, pick_ref[...])
    solved = [dot_split(split(x), split(r)) for x, r in zip(inverses, rights)]
    for at in range(count):
        moves = {}
        for c in range(blocks):
            i = (at * blocks + c) * 2
            both = jnp.concatenate([tails[i] * solved[i], tails[i + 1] * solved[i + 1]], axis=1)
            grown = dot_split(key_parts[at * blocks + c], split(both), TN)
            for b in range(2):
                solved_ref[at, b, pl.ds(c * BLOCK, BLOCK), :] = solved[i + b]
                added = grown[:, b * 2 * DK : b * 2 * DK + DV]
                move = (
                    jnp.where(identity, ends[i + b], 0.0)
                    - grown[:, b * 2 * DK + DV : (b + 1) * 2 * DK]
                )
                moves[b, c] = (added, move)
        for b in range(2):
            half = blocks // 2
            parts = []
            for begin in (0, half):
                both = jnp.concatenate(moves[b, begin], axis=1)
                for c in range(begin + 1, begin + half):
                    if begin == 0:
                        starts_ref[at, b, c - 1] = both
                    both = followed(moves[b, c], both)
                parts.append(both)
            starts_ref[at, b, half - 1] = parts[0]
            for c in range(half, blocks - 1):
                starts_ref[at, b, c] = jnp.concatenate(moves[b, c], axis=1)
            both = followed((parts[1][:, :DV], parts[1][:, DV:]), parts[0])
            message_refs[at][b] = both


def query_kernel(
    slots,
    start,
    group,
    q_ref,
    before_ref,
    edge_ref,
    unit_ref,
    first_ref,
    rows_ref,
    columns_ref,
    solved_ref,
    starts_ref,
    own_ref,
    high_ref,
    low_ref,
    padded,
):
    place = lax.axis_index("seq") % group
    tokens = q_ref.shape[0]
    blocks = tokens // BLOCK
    row, column = iotas()
    causal = row >= column
    work = []
    for at, s in enumerate(slots):
        p = place ^ slot_partner(group, s)
        columns = lanes(p * DK, DK)
        padded[0:8] = rows_before(before_ref, columns)
        padded[8:] = q_ref[:, columns].astype(f32)
        taps = edge_ref[EDGE : EDGE + KCONV, columns]
        queries = unit(conv_rows(padded, taps, tokens), 1.0 / math.sqrt(DK))
        sums, cum_columns = rows_ref[s], columns_ref[s]
        growth_columns = jnp.exp(cum_columns)
        for c in range(blocks):
            here = queries[c * BLOCK : (c + 1) * BLOCK]
            keys = first_ref[at] if c == 0 else unit_ref[start + at, pl.ds(c * BLOCK, BLOCK), :]
            dots = dot_split(split(here), split(keys), NT)
            for b in range(2):
                r = b * blocks + c
                spread = cum_columns[:, r : r + 1] - sums[r : r + 1, :]
                attend = dots * jnp.exp(jnp.where(causal, spread, FAR))
                grown = growth_columns[:, r : r + 1] * here
                work.append((at, b, c, split(attend), grown))
    seen = [
        dot_split(attend, split(solved_ref[at, b, pl.ds(c * BLOCK, BLOCK), :]))
        for at, b, c, attend, grown in work
    ]
    begins = {}
    for at in range(len(slots)):
        for b in range(2):
            for c in range(1, blocks):
                both = starts_ref[at, b, c - 1]
                if c > blocks // 2:
                    both = followed((both[:, :DV], both[:, DV:]), begins[at, b, c - 1])
                begins[at, b, c] = both
    for (at, b, c, attend, grown), one in zip(work, seen):
        own, reads = one[:, :DV], grown - one[:, DV:]
        if c > 0:
            through = dot_split(split(reads), split(begins[at, b, c]))
            own, reads = own + through[:, :DV], through[:, DV:]
        here = pl.ds(c * BLOCK, BLOCK)
        own_ref[at, b, here, :] = own
        high_ref[at, b, here, :], low_ref[at, b, here, :] = split(reads)


def prefix_kernel(group, *refs):
    messages, refs = refs[:group], refs[group:]
    chain_ref, leaving_ref, held, sems = refs
    place = lax.axis_index("seq") % group
    copies = [
        pltpu.make_async_copy(messages[d], held.at[place ^ d], sems.at[d]) for d in range(group)
    ]
    for copy in copies:
        copy.start()
    for copy in copies:
        copy.wait()
    heads = leaving_ref.shape[0]
    chain = [held[0, b] for b in range(heads)]
    for i in range(1, group):
        for b in range(heads):
            chain_ref[i - 1, b] = chain[b]
        chain = [
            dot_split(split(held[i, b, :, DV:]), split(chain[b])) for b in range(heads)
        ]
        chain = [
            jnp.concatenate([chain[b][:, :DV] + held[i, b, :, 0:DV], chain[b][:, DV:]], axis=1)
            for b in range(heads)
        ]
    for b in range(heads):
        chain_ref[group - 1, b] = chain[b]
        leaving_ref[b] = chain[b][:, :DV]


def enter_kernel(group, onward, entering_ref, chain_ref, *refs):
    outs = refs[:group]
    place = lax.axis_index("seq") % group
    heads = entering_ref.shape[0]
    count = group if onward else group - 1
    later = lax.axis_index("seq") >= group
    states = [[jnp.where(later, entering_ref[b], 0.0) for b in range(heads)]]
    states += [[] for i in range(count)]
    for b in range(heads):
        moves = jnp.concatenate([chain_ref[i, b, :, DV:] for i in range(count)], axis=0)
        moved = dot_split(split(moves), split(states[0][b]))
        for i in range(count):
            states[i + 1].append(chain_ref[i, b, :, 0:DV] + moved[i * DK : (i + 1) * DK])
    if onward:
        for b in range(heads):
            refs[group][b] = states[group][b]
    for j in range(group):

        @pl.when(place == j)
        def _():
            for i in range(group):
                for b in range(heads):
                    outs[j ^ i][b] = states[i][b]


def output_kernel(group, slots, *refs):
    reads, refs = refs[: 3 * len(slots)], refs[3 * len(slots) :]
    entering, (out_ref, held, sems) = refs[: len(slots)], refs[-3:]
    place = lax.axis_index("seq") % group
    copies = []
    for n, (s, at) in enumerate(slots):
        own_ref, high_ref, low_ref = reads[3 * n : 3 * n + 3]
        p = place ^ slot_partner(group, s)
        for b in range(2):
            product = dot_split((high_ref[at, b], low_ref[at, b]), split(entering[n][b]))
            held[n, :, b * DV : (b + 1) * DV] = own_ref[at, b] + product
        copies.append(
            pltpu.make_async_copy(held.at[n], out_ref.at[:, lanes(p * 2 * DV, 2 * DV)], sems.at[n])
        )
        copies[-1].start()
    for copy in copies:
        copy.wait()


def shape(*dims, dtype=f32):
    return jax.ShapeDtypeStruct(dims, dtype)


def params(mib=24):
    return pltpu.CompilerParams(vmem_limit_bytes=mib << 20)


def whole(space=VMEM):
    return pl.BlockSpec(memory_space=space)


def per_device(
    hidden_states,
    proj_ba,
    query_in,
    key_in,
    value_in,
    conv_query,
    conv_key,
    convolution_value_taps,
    decay_scale,
    dt_bias,
):
    tokens = hidden_states.shape[0]
    heads = decay_scale.shape[0]
    pairs = key_in.shape[1] // DK
    blocks = tokens // BLOCK
    key_width, value_width = key_in.shape[1], value_in.shape[1]
    seq, head_count = lax.axis_size("seq"), lax.axis_size("head")
    group = pairs

    def full(block):
        return pl.BlockSpec(block, lambda i: (0,) * len(block))

    last_rows = tokens // EDGE - 1
    width = 2 * key_width + value_width
    inputs = (query_in, key_in, value_in)
    taps = (conv_query, conv_key, convolution_value_taps)
    kept, given, tail, edge, scales = pl.pallas_call(
        functools.partial(logits_kernel, head_count),
        grid=(1,),
        in_specs=[full((1, heads))] * 2 + [full(hidden_states.shape), full(proj_ba.shape[::-1])]
        + [pl.BlockSpec((EDGE, x.shape[1]), lambda i: (0, 0)) for x in inputs]
        + [pl.BlockSpec((EDGE, x.shape[1]), lambda i: (last_rows, 0)) for x in inputs]
        + [full(x.shape) for x in taps],
        out_specs=[whole()] * 5,
        out_shape=[shape(head_count // 2, 2 * heads, tokens)] * 2
        + [shape(EDGE, width, dtype=bf16), shape(EDGE + 8, width), shape(heads, tokens)],
        scratch_shapes=[VMEM((head_count, 2 * heads, tokens), f32)],
        compiler_params=params(),
        name="logits",
    )(
        *[in_hbm(x.reshape(1, heads)) for x in (decay_scale, dt_bias)],
        *[in_hbm(x) for x in (hidden_states, proj_ba.T, *inputs, *inputs, *taps)],
    )

    taken = lax.ppermute(given, "head", [(i, i ^ 1) for i in range(head_count)])
    logits = [kept, taken] + [
        lax.ppermute(kept[n] + taken[n], "head", [(i, i ^ (2 * n)) for i in range(head_count)])
        for n in range(1, head_count // 2)
    ]
    before = lax.ppermute(tail, "seq", [(i, (i + 1) % seq) for i in range(seq)])

    pick = jnp.asarray(pick_matrix())

    def mix_shapes(count):
        return [(count, tokens, DK), (count, blocks - 1, BLOCK, BLOCK), (count, tokens, 2 * DV)]

    def mix_scratch(count):
        return [
            VMEM((count, tokens, DK), bf16),
            VMEM((count, tokens, 2 * DV), bf16),
            VMEM((count, 3, tokens + 8, DK), f32),
            pltpu.SemaphoreType.DMA((count, 2)),
        ]

    def mix(slots):
        count = len(slots)
        return pl.pallas_call(
            functools.partial(mix_kernel, slots, group, key_width),
            in_specs=[whole(), whole(pl.ANY), whole(pl.ANY)],
            out_specs=[whole()] * 3,
            out_shape=[shape(*dims) for dims in mix_shapes(count)],
            scratch_shapes=mix_scratch(count),
            compiler_params=params(),
            name="mix",
        )(edge, in_hbm(key_in), in_hbm(value_in))

    def solve(slots, start, known, first, unit_keys, key_dots, mixed):
        count = len(slots)
        gate_shapes = [
            shape(group, 4 * blocks, BLOCK),
            shape(group, BLOCK, 8 * blocks),
        ]
        return pl.pallas_call(
            functools.partial(
                solve_kernel, slots, start, group, key_width, len(known) - 1 if first else 0
            ),
            in_specs=[whole()] * (len(known) + 6),
            out_specs=[whole()] * (count + 3 + 2 * first),
            out_shape=[shape(2, DK, 2 * DK)] * count
            + [
                shape(count, 2, tokens, 2 * DK),
                shape(count, 2, blocks - 1, DK, 2 * DK),
                shape(count, BLOCK, DK),
            ]
            + gate_shapes * first,
            scratch_shapes=[VMEM((3, EDGE + 8, DK), f32)],
            compiler_params=params(),
            name="solve",
        )(*known, unit_keys, key_dots, mixed, before, edge, pick)

    def query(slots, start, unit_keys, solved, starts, first_keys):
        count = len(slots)
        return pl.pallas_call(
            functools.partial(query_kernel, slots, start, group),
            in_specs=[whole()] * 9,
            out_specs=[whole()] * 3,
            out_shape=[shape(count, 2, tokens, DV)]
            + [shape(count, 2, tokens, DK, dtype=bf16)] * 2,
            scratch_shapes=[VMEM((tokens + 8, DK), f32)],
            compiler_params=params(),
            cost_estimate=pl.CostEstimate(
                flops=2_000_000_000 * count, bytes_accessed=2_000_000 * count, transcendentals=0
            ),
            name="query",
        )(query_in, before, edge, unit_keys, first_keys, *known, solved, starts)

    calls = solve_calls(group)
    mixed = mix(sum(calls, ()))
    messages, rest, start = [], [], 0
    known = [scales, *logits]
    for slots in calls:
        results = solve(slots, start, known, not start, *mixed)
        if not start:
            *results, rows, columns = results
            known = [rows, columns]
        results, known = lax.optimization_barrier((results, known))
        messages += results[: len(slots)]
        rest.append([mixed[0], *results[len(slots) :]])
        start += len(slots)

    arrived = [None] * group
    for s in range(group):
        d = slot_partner(group, s)
        arrived[d] = (
            lax.ppermute(messages[s], "seq", [(i, i ^ d) for i in range(seq)]) if d else messages[s]
        )

    messages[-1], rest[0] = lax.optimization_barrier((messages[-1], rest[0]))
    reads = [query(calls[0], 0, *rest[0])]
    arrived, reads = lax.optimization_barrier((arrived, reads))
    chain, leaving = pl.pallas_call(
        functools.partial(prefix_kernel, group),
        in_specs=[whole(pl.ANY)] * group,
        out_specs=[whole()] * 2,
        out_shape=[shape(group, 2, DK, 2 * DK), shape(2, DK, DV)],
        scratch_shapes=[VMEM((group, 2, DK, 2 * DK), f32), pltpu.SemaphoreType.DMA((group,))],
        compiler_params=params(),
        name="prefix",
    )(*arrived)
    leaving, rest = lax.optimization_barrier((leaving, rest))
    starts = [sum(len(c) for c in calls[:k]) for k in range(len(calls))]
    def enter(received, onward):
        return pl.pallas_call(
            functools.partial(enter_kernel, group, onward),
            in_specs=[whole()] * 2,
            out_specs=[whole()] * (group + onward),
            out_shape=[shape(2, DK, DV)] * (group + onward),
            compiler_params=params(),
            name="enter",
        )(received, chain)

    hops = seq // group - 1
    if not hops:
        entering = enter(jnp.zeros((2, DK, DV), f32), False)
    for hop in range(hops):
        received = lax.ppermute(leaving, "seq", [(i, (i + group) % seq) for i in range(seq)])
        if hop == 0:
            reads += [query(*x, *outs) for *x, outs in zip(calls[1:-1], starts[1:-1], rest[1:-1])]
            received, reads, rest = lax.optimization_barrier((received, reads, rest))
        entering = enter(received, hop < hops - 1)
        if hop < hops - 1:
            *entering, leaving = entering

    states = {0: entering[0]}
    for d in range(group - 1, 0, -1):
        states[d] = lax.ppermute(entering[d], "seq", [(i, i ^ d) for i in range(seq)])
    reads.append(query(calls[-1], starts[-1], *rest[-1]))
    where = {s: (k, at) for k, slots in enumerate(calls) for at, s in enumerate(slots)}

    def outputs(slots, written):
        operands = [x for s in slots for x in reads[where[s][0]]]
        operands += [states[slot_partner(group, s)] for s in slots]
        return pl.pallas_call(
            functools.partial(output_kernel, group, [(s, where[s][1]) for s in slots]),
            in_specs=[whole()] * len(operands) + [whole(pl.ANY)] * len(written),
            out_specs=whole(pl.ANY),
            out_shape=shape(tokens, value_width),
            scratch_shapes=[
                VMEM((len(slots), tokens, 2 * DV), f32),
                pltpu.SemaphoreType.DMA((len(slots),)),
            ],
            input_output_aliases={len(operands): 0} if written else {},
            compiler_params=params(),
            name="outputs",
        )(*operands, *written)

    first = [s for s in range(group) if slot_partner(group, s) < 1]
    written = outputs(first, [])
    return outputs([s for s in range(group) if s not in first], [written])


def solution(mesh):
    placed = (
        P("seq", "head"),
        P("head", None),
        P("seq", "head"),
        P("seq", "head"),
        P("seq", "head"),
        P(None, "head"),
        P(None, "head"),
        P(None, "head"),
        P("head"),
        P("head"),
    )
    return jax.shard_map(
        per_device, mesh=mesh, in_specs=placed, out_specs=P("seq", "head"), check_vma=False
    )
```

```python
import functools
import math

import jax
import jax.numpy as jnp
import numpy as np
from jax import lax
from jax.experimental import pallas as pl
from jax.experimental.pallas import tpu as pltpu
from jax.sharding import PartitionSpec as P

DK = 128
DV = 128
KCONV = 4
BLOCK = 128
SUB = 16
EDGE = 16

f32 = jnp.float32
bf16 = jnp.bfloat16
VMEM = pltpu.VMEM
FAR = -1e30


def split(x):
    hi = x.astype(bf16)
    return hi, (x - hi.astype(f32)).astype(bf16)


def dot_split(a, b, contract=((1,), (0,))):
    (ah, al), (bh, bl) = a, b
    (ca,), (cb,) = contract
    left = jnp.concatenate([ah, al, ah], axis=ca)
    right = jnp.concatenate([bh, bh, bl], axis=cb)
    return lax.dot_general(left, right, (contract, ((), ())), preferred_element_type=f32)


NN = ((1,), (0,))
NT = ((1,), (1,))
TN = ((0,), (0,))


def silu(x):
    return x / (1.0 + jnp.exp(-x))


def unit(x, factor=1.0):
    return x * (lax.rsqrt(jnp.sum(x * x, axis=-1, keepdims=True) + 1e-6) * factor)


def conv_rows(padded_ref, taps, rows):
    total = taps[0:1] * padded_ref[pl.ds(8 - KCONV + 1, rows), :]
    for j in range(1, KCONV):
        total = total + taps[j : j + 1] * padded_ref[pl.ds(8 - KCONV + 1 + j, rows), :]
    return silu(total)


def iotas(rows=BLOCK, columns=BLOCK):
    return (
        lax.broadcasted_iota(jnp.int32, (rows, columns), 0),
        lax.broadcasted_iota(jnp.int32, (rows, columns), 1),
    )


def slot_partner(group, slot):
    order = [d for d in range(group - 1, 0, -1) if d % 2] + [
        d for d in range(group - 1, 0, -1) if d % 2 == 0
    ]
    return (order + [0])[slot]


def solve_calls(group):
    return [(0,), tuple(range(1, group - 1)), (group - 1,)] if group > 2 else [(0,), (1,)]


def in_hbm(x):
    return pltpu.with_memory_space_constraint(x, pltpu.HBM)


HELD = 4


def unpack_before(before_ref, earlier_ref):
    rows = before_ref[...]
    earlier_ref[...] = jnp.where(lax.axis_index("seq") > 0, rows, 0.0)


def fill_before(padded_ref, earlier_ref, tile):
    for i in range(1, KCONV):
        padded_ref[8 - KCONV + i : 9 - KCONV + i, :] = earlier_ref[pl.ds(HELD * tile + i, 1), :]


def lanes(start, size):
    return pl.ds(pl.multiple_of(start, 128), size)


def logits_kernel(
    head_count,
    scale_ref,
    bias_ref,
    hidden_ref,
    proj_ref,
    q_first,
    k_first,
    v_first,
    q_last,
    k_last,
    v_last,
    q_taps,
    k_taps,
    v_taps,
    kept_ref,
    given_ref,
    tail_ref,
    edge_ref,
    scales_ref,
    held,
    packed,
):
    rows = proj_ref.shape[0] // head_count
    everything = lax.dot_general(
        proj_ref[...], hidden_ref[...], (NT, ((), ())), preferred_element_type=f32
    )
    for m in range(head_count):
        held[m] = everything[m * rows : (m + 1) * rows]
    me = lax.axis_index("head")
    for n in range(head_count // 2):
        kept_ref[n] = held[me ^ (2 * n)]
        given_ref[n] = held[me ^ (2 * n + 1)]
    heads = rows // 2
    row, column = iotas(heads, heads)
    scale, bias = (
        jnp.sum(jnp.where(row == column, ref[...], 0.0), axis=1, keepdims=True)
        for ref in (scale_ref, bias_ref)
    )
    scales_ref[...] = jnp.broadcast_to(scale, scales_ref.shape)
    for h in range(heads):
        kept_ref[0, 2 * h : 2 * h + 1, :] = kept_ref[0, 2 * h : 2 * h + 1, :] + bias[h : h + 1]
    edge_ref[...] = jnp.zeros_like(edge_ref)
    packed[...] = jnp.zeros_like(packed)
    start = 0
    for first, last, taps in ((q_first, q_last, q_taps), (k_first, k_last, k_taps), (v_first, v_last, v_taps)):
        here = slice(start, start + first.shape[1])
        rows = last[...].astype(f32)[EDGE - KCONV + 1 :]
        for n in range(first.shape[1] // DK):
            at = HELD * (start // DK + n)
            packed[at + 1 : at + KCONV, :] = rows[:, n * DK : (n + 1) * DK]
        edge_ref[0:EDGE, here] = first[...].astype(f32)
        edge_ref[EDGE : EDGE + KCONV, here] = taps[...].astype(f32)
        start += first.shape[1]
    tail_ref[...] = packed[...]


def mix_kernel(slots, group, key_width, edge_ref, k_ref, v_ref, unit_ref, dots_ref, mixed_ref, k_held, v_held, padded, sems):
    tokens = k_ref.shape[0]
    place = lax.axis_index("seq") % group
    copies = []
    for at, s in enumerate(slots):
        p = place ^ slot_partner(group, s)
        copies.append(
            (
                pltpu.make_async_copy(k_ref.at[:, lanes(p * DK, DK)], k_held.at[at], sems.at[at, 0]),
                pltpu.make_async_copy(
                    v_ref.at[:, lanes(p * 2 * DV, 2 * DV)], v_held.at[at], sems.at[at, 1]
                ),
            )
        )
    for both in copies:
        for copy in both:
            copy.start()
    for at, s in enumerate(slots):
        p = place ^ slot_partner(group, s)
        key_taps = edge_ref[EDGE : EDGE + KCONV, lanes(key_width + p * DK, DK)]
        value_taps = edge_ref[EDGE : EDGE + KCONV, lanes(2 * key_width + p * 2 * DV, 2 * DV)]
        for n in range(3):
            padded[at, n, 0:8] = jnp.zeros((8, DK), f32)
        copies[at][0].wait()
        padded[at, 0, 8:] = k_held[at].astype(f32)
        keys = unit(conv_rows(padded.at[at, 0], key_taps, tokens))
        unit_ref[at] = keys
        for c in range(1, tokens // BLOCK):
            part = split(keys[c * BLOCK : (c + 1) * BLOCK])
            dots_ref[at, c - 1] = dot_split(part, part, NT)
        copies[at][1].wait()
        for b in range(2):
            here = slice(b * DV, (b + 1) * DV)
            padded[at, 1 + b, 8:] = v_held[at, :, here].astype(f32)
            mixed_ref[at, :, here] = conv_rows(padded.at[at, 1 + b], value_taps[:, here], tokens)


def softplus(u):
    e = jnp.exp(-jnp.abs(u))
    small = e * (1.0 - e * (0.5 - e * (1.0 / 3.0 - e * (0.25 - e * 0.2))))
    return jnp.maximum(u, 0.0) + jnp.where(e < 0.03, small, jnp.log(1.0 + e))


def dot_wide(a, b):
    rows, columns = a[0].shape[0], b[0].shape[1]
    four = jnp.dot(
        jnp.concatenate(a, axis=0), jnp.concatenate(b, axis=1), preferred_element_type=f32
    )
    return four[:rows, :columns] + (four[:rows, columns:] + four[rows:, :columns])


def pick_matrix():
    row, column = np.arange(BLOCK)[:, None], np.arange((SUB - 1) * BLOCK)[None, :]
    pick = row == (column % BLOCK) // SUB * SUB + column // BLOCK
    return np.concatenate([pick, pick], axis=0).astype(bf16)


def invert_all(lowers, pick):
    count = len(lowers)
    row, column = iotas()
    blocks = (row // SUB) == (column // SUB)
    folded = []
    for lower in lowers:
        kept = jnp.where(blocks, lower, 0.0)
        total = kept[0:SUB]
        for b in range(1, BLOCK // SUB):
            total = total + kept[b * SUB : (b + 1) * SUB]
        folded.append(total)
    spread = jnp.concatenate(split(jnp.concatenate(folded, axis=0)), axis=1)
    wide = jnp.dot(spread, pick, preferred_element_type=f32).reshape(
        count, SUB, (SUB - 1) * BLOCK
    )
    srow, scolumn = iotas(SUB, BLOCK)
    inverse = jnp.broadcast_to(
        jnp.where(srow == scolumn % SUB, 1.0, 0.0)[None], (count, SUB, BLOCK)
    )
    for j in range(SUB - 1):
        inverse = inverse - wide[:, :, j * BLOCK : (j + 1) * BLOCK] * inverse[:, j : j + 1, :]
    inverses = [inverse[i] for i in range(count)]
    halves = [split(x) for x in lowers]
    size = SUB
    while size < BLOCK:
        same = (row // size) == (column // size)
        across = ((row // (2 * size)) == (column // (2 * size))) & ((row // size) > (column // size))
        same, across = (jnp.where(m, 1.0, 0.0).astype(bf16) for m in (same, across))
        odd = iotas(size, BLOCK)[1] // size % 2 == 1
        dot = dot_wide if size < 64 else dot_split
        parts = [split(x) for x in inverses]
        if 2 * size < BLOCK:
            first = [dot(x, tuple(h * across for h in low)) for x, low in zip(parts, halves)]
        else:
            first = [
                dot(split(jnp.where(odd, x, 0.0)), low) for x, low in zip(inverses, halves)
            ]
        spread = [
            tuple(jnp.concatenate([h] * (BLOCK // size), axis=0) * same for h in x) for x in parts
        ]
        second = [dot(split(x), y) for x, y in zip(first, spread)]
        inverses = [
            jnp.concatenate([jnp.where(odd, 0.0, x), jnp.where(odd, x, -y)], axis=0)
            for x, y in zip(inverses, second)
        ]
        size *= 2
    return inverses


def followed(later, both):
    added, move = later
    both = dot_split(split(move), split(both))
    return jnp.concatenate([both[:, :DV] + added, both[:, DV:]], axis=1)


def gates(p, scales_ref, logit_refs):
    row, column = iotas()
    decays, rates = [], []
    for b in range(2):
        h = 2 * p + b
        u = logit_refs[0][0, pl.ds(2 * h, 1), :] + logit_refs[1][0, pl.ds(2 * h, 1), :]
        w = logit_refs[0][0, pl.ds(2 * h + 1, 1), :] + logit_refs[1][0, pl.ds(2 * h + 1, 1), :]
        for ref in logit_refs[2:]:
            u = u + ref[pl.ds(2 * h, 1), :]
            w = w + ref[pl.ds(2 * h + 1, 1), :]
        decays.append(-scales_ref[pl.ds(h, 1), :] * softplus(u))
        rates.append(1.0 / (1.0 + jnp.exp(-w)))
    blocks = decays[0].shape[1] // BLOCK
    decay_rows, rate_rows = (
        jnp.concatenate(
            [x[:, c * BLOCK : (c + 1) * BLOCK] for x in both for c in range(blocks)], axis=0
        )
        for both in (decays, rates)
    )
    sums = jnp.dot(
        decay_rows,
        jnp.where(row <= column, 1.0, 0.0),
        precision=lax.Precision.HIGHEST,
        preferred_element_type=f32,
    )
    last = sums[:, BLOCK - 1 : BLOCK]
    columns = jnp.concatenate(
        [
            jnp.transpose(x)
            for x in (sums, rate_rows, rate_rows * jnp.exp(sums), jnp.exp(last - sums))
        ],
        axis=1,
    )
    return jnp.concatenate([sums, jnp.broadcast_to(jnp.exp(last), sums.shape)], axis=0), columns


def solve_kernel(
    slots,
    start,
    group,
    key_width,
    pieces,
    *refs,
):
    if pieces:
        (scales_ref, *logit_refs), refs = refs[: 1 + pieces], refs[1 + pieces :]
    else:
        (rows_ref, columns_ref), refs = refs[:2], refs[2:]
    (unit_ref, dots_ref, mixed_ref, before_ref, edge_ref, pick_ref), refs = refs[:6], refs[6:]
    count = len(slots)
    message_refs, refs = refs[:count], refs[count:]
    (solved_ref, starts_ref, first_ref), refs = refs[:3], refs[3:]
    if pieces:
        (rows_ref, columns_ref), refs = refs[:2], refs[2:]
    padded, earlier = refs
    tokens = unit_ref.shape[1]
    blocks = tokens // BLOCK
    height = 2 * blocks
    place = lax.axis_index("seq") % group
    row, column = iotas()
    identity = row == column
    strict = row > column

    known = {}
    unpack_before(before_ref, earlier)
    if pieces:
        for s in range(group):
            known[s] = gates(place ^ slot_partner(group, s), scales_ref, logit_refs)
            rows_ref[s], columns_ref[s] = known[s]
    systems, rights, tails, ends, key_parts = [], [], [], [], []
    for at, s in enumerate(slots):
        p = place ^ slot_partner(group, s)
        kcol, vcol = lanes(key_width + p * DK, DK), lanes(2 * key_width + p * 2 * DV, 2 * DV)
        rows, columns = known[s] if s in known else (rows_ref[s], columns_ref[s])
        key_taps = edge_ref[EDGE : EDGE + KCONV, kcol]
        value_taps = edge_ref[EDGE : EDGE + KCONV, vcol]
        fill_before(padded.at[0], earlier, key_width // DK + p)
        padded[0, 8:] = edge_ref[0:EDGE, kcol]
        edge_keys = unit(conv_rows(padded.at[0], key_taps, EDGE))
        edge_values = edge_ref[0:EDGE, vcol]
        edges = []
        for b in range(2):
            here = slice(b * DV, (b + 1) * DV)
            fill_before(padded.at[1 + b], earlier, 2 * key_width // DK + 2 * p + b)
            padded[1 + b, 8:] = edge_values[:, here]
            edges.append(conv_rows(padded.at[1 + b], value_taps[:, here], EDGE))
        edge_values = jnp.concatenate(edges, axis=1)
        for c in range(blocks):
            keys = unit_ref[start + at, pl.ds(c * BLOCK, BLOCK), :]
            values = mixed_ref[start + at, pl.ds(c * BLOCK, BLOCK), :]
            if c == 0:
                keys = jnp.concatenate([edge_keys, keys[EDGE:]], axis=0)
                values = jnp.concatenate([edge_values, values[EDGE:]], axis=0)
                first_ref[at] = keys
            parts = split(keys)
            key_parts.append(parts)
            dots = dot_split(parts, parts, NT) if c == 0 else dots_ref[start + at, c - 1]
            for b in range(2):
                r = b * blocks + c
                cum, rate, scaled, tail = (
                    columns[:, n * height + r : n * height + r + 1] for n in range(4)
                )
                spread = cum - rows[r : r + 1, :]
                table = jnp.exp(jnp.where(strict, spread, FAR))
                systems.append(rate * table * dots)
                rights.append(
                    jnp.concatenate(
                        [
                            rate * values[:, b * DV : (b + 1) * DV],
                            scaled * keys,
                        ],
                        axis=1,
                    )
                )
                tails.append(tail)
                ends.append(rows[height + r : height + r + 1, :])

    inverses = invert_all(systems, pick_ref[...])
    solved = [dot_split(split(x), split(r)) for x, r in zip(inverses, rights)]
    for at in range(count):
        moves = {}
        for c in range(blocks):
            i = (at * blocks + c) * 2
            both = jnp.concatenate([tails[i] * solved[i], tails[i + 1] * solved[i + 1]], axis=1)
            grown = dot_split(key_parts[at * blocks + c], split(both), TN)
            for b in range(2):
                solved_ref[at, b, pl.ds(c * BLOCK, BLOCK), :] = solved[i + b]
                added = grown[:, b * 2 * DK : b * 2 * DK + DV]
                move = (
                    jnp.where(identity, ends[i + b], 0.0)
                    - grown[:, b * 2 * DK + DV : (b + 1) * 2 * DK]
                )
                moves[b, c] = (added, move)
        for b in range(2):
            half = blocks // 2
            parts = []
            for begin in (0, half):
                both = jnp.concatenate(moves[b, begin], axis=1)
                for c in range(begin + 1, begin + half):
                    if begin == 0:
                        starts_ref[at, b, c - 1] = both
                    both = followed(moves[b, c], both)
                parts.append(both)
            starts_ref[at, b, half - 1] = parts[0]
            for c in range(half, blocks - 1):
                starts_ref[at, b, c] = jnp.concatenate(moves[b, c], axis=1)
            both = followed((parts[1][:, :DV], parts[1][:, DV:]), parts[0])
            message_refs[at][b] = both


def query_kernel(
    slots,
    start,
    group,
    q_ref,
    before_ref,
    edge_ref,
    unit_ref,
    first_ref,
    rows_ref,
    columns_ref,
    solved_ref,
    starts_ref,
    own_ref,
    high_ref,
    low_ref,
    padded,
    earlier,
):
    place = lax.axis_index("seq") % group
    tokens = q_ref.shape[0]
    blocks = tokens // BLOCK
    row, column = iotas()
    causal = row >= column
    unpack_before(before_ref, earlier)
    work = []
    for at, s in enumerate(slots):
        p = place ^ slot_partner(group, s)
        columns = lanes(p * DK, DK)
        fill_before(padded, earlier, p)
        padded[8:] = q_ref[:, columns].astype(f32)
        taps = edge_ref[EDGE : EDGE + KCONV, columns]
        queries = unit(conv_rows(padded, taps, tokens), 1.0 / math.sqrt(DK))
        sums, cum_columns = rows_ref[s], columns_ref[s]
        growth_columns = jnp.exp(cum_columns)
        for c in range(blocks):
            here = queries[c * BLOCK : (c + 1) * BLOCK]
            keys = first_ref[at] if c == 0 else unit_ref[start + at, pl.ds(c * BLOCK, BLOCK), :]
            dots = dot_split(split(here), split(keys), NT)
            for b in range(2):
                r = b * blocks + c
                spread = cum_columns[:, r : r + 1] - sums[r : r + 1, :]
                attend = dots * jnp.exp(jnp.where(causal, spread, FAR))
                grown = growth_columns[:, r : r + 1] * here
                work.append((at, b, c, split(attend), grown))
    seen = [
        dot_split(attend, split(solved_ref[at, b, pl.ds(c * BLOCK, BLOCK), :]))
        for at, b, c, attend, grown in work
    ]
    begins = {}
    for at in range(len(slots)):
        for b in range(2):
            for c in range(1, blocks):
                both = starts_ref[at, b, c - 1]
                if c > blocks // 2:
                    both = followed((both[:, :DV], both[:, DV:]), begins[at, b, c - 1])
                begins[at, b, c] = both
    for (at, b, c, attend, grown), one in zip(work, seen):
        own, reads = one[:, :DV], grown - one[:, DV:]
        if c > 0:
            through = dot_split(split(reads), split(begins[at, b, c]))
            own, reads = own + through[:, :DV], through[:, DV:]
        here = pl.ds(c * BLOCK, BLOCK)
        own_ref[at, b, here, :] = own
        high_ref[at, b, here, :], low_ref[at, b, here, :] = split(reads)


def prefix_kernel(group, *refs):
    messages, (chain_ref, leaving_ref) = refs[:group], refs[group:]
    place = lax.axis_index("seq") % group
    heads = leaving_ref.shape[0]
    for j in range(group):

        @pl.when(place == j)
        def _():
            chain = [messages[j][b] for b in range(heads)]
            for i in range(1, group):
                for b in range(heads):
                    chain_ref[i - 1, b] = chain[b]
                later = messages[j ^ i]
                chain = [
                    followed((later[b, :, 0:DV], later[b, :, DV:]), chain[b]) for b in range(heads)
                ]
            for b in range(heads):
                chain_ref[group - 1, b] = chain[b]
                leaving_ref[b] = chain[b][:, :DV]


def enter_kernel(group, onward, entering_ref, chain_ref, *refs):
    outs = refs[:group]
    place = lax.axis_index("seq") % group
    heads = entering_ref.shape[0]
    count = group if onward else group - 1
    later = lax.axis_index("seq") >= group
    states = [[jnp.where(later, entering_ref[b], 0.0) for b in range(heads)]]
    states += [[] for i in range(count)]
    for b in range(heads):
        moves = jnp.concatenate([chain_ref[i, b, :, DV:] for i in range(count)], axis=0)
        moved = dot_split(split(moves), split(states[0][b]))
        for i in range(count):
            states[i + 1].append(chain_ref[i, b, :, 0:DV] + moved[i * DK : (i + 1) * DK])
    if onward:
        for b in range(heads):
            refs[group][b] = states[group][b]
    for j in range(group):

        @pl.when(place == j)
        def _():
            for i in range(group):
                for b in range(heads):
                    outs[j ^ i][b] = states[i][b]


def output_kernel(group, slots, *refs):
    reads, refs = refs[: 3 * len(slots)], refs[3 * len(slots) :]
    entering, (out_ref, held, sems) = refs[: len(slots)], refs[-3:]
    place = lax.axis_index("seq") % group
    copies = []
    for n, (s, at) in enumerate(slots):
        own_ref, high_ref, low_ref = reads[3 * n : 3 * n + 3]
        p = place ^ slot_partner(group, s)
        for b in range(2):
            state = jnp.concatenate(split(entering[n][b]), axis=1)
            product = jnp.dot(
                jnp.concatenate([high_ref[at, b], low_ref[at, b]], axis=1),
                jnp.concatenate([state, state], axis=0),
                preferred_element_type=f32,
            )
            held[n, b] = own_ref[at, b] + (product[:, :DV] + product[:, DV:])
            copies.append(
                pltpu.make_async_copy(
                    held.at[n, b], out_ref.at[:, lanes((p * 2 + b) * DV, DV)], sems.at[n, b]
                )
            )
            copies[-1].start()
    for copy in copies:
        copy.wait()


def shape(*dims, dtype=f32):
    return jax.ShapeDtypeStruct(dims, dtype)


def params(mib=24):
    return pltpu.CompilerParams(vmem_limit_bytes=mib << 20)


def whole(space=VMEM):
    return pl.BlockSpec(memory_space=space)


def per_device(
    hidden_states,
    proj_ba,
    query_in,
    key_in,
    value_in,
    conv_query,
    conv_key,
    convolution_value_taps,
    decay_scale,
    dt_bias,
):
    tokens = hidden_states.shape[0]
    heads = decay_scale.shape[0]
    pairs = key_in.shape[1] // DK
    blocks = tokens // BLOCK
    key_width, value_width = key_in.shape[1], value_in.shape[1]
    seq, head_count = lax.axis_size("seq"), lax.axis_size("head")
    group = pairs

    def full(block):
        return pl.BlockSpec(block, lambda i: (0,) * len(block))

    last_rows = tokens // EDGE - 1
    width = 2 * key_width + value_width
    inputs = (query_in, key_in, value_in)
    taps = (conv_query, conv_key, convolution_value_taps)
    kept, given, tail, edge, scales = pl.pallas_call(
        functools.partial(logits_kernel, head_count),
        grid=(1,),
        in_specs=[full((1, heads))] * 2 + [full(hidden_states.shape), full(proj_ba.shape[::-1])]
        + [pl.BlockSpec((EDGE, x.shape[1]), lambda i: (0, 0)) for x in inputs]
        + [pl.BlockSpec((EDGE, x.shape[1]), lambda i: (last_rows, 0)) for x in inputs]
        + [full(x.shape) for x in taps],
        out_specs=[whole()] * 5,
        out_shape=[shape(head_count // 2, 2 * heads, tokens)] * 2
        + [shape(HELD * width // DK, DK), shape(EDGE + 8, width), shape(heads, tokens)],
        scratch_shapes=[
            VMEM((head_count, 2 * heads, tokens), f32),
            VMEM((HELD * width // DK, DK), f32),
        ],
        compiler_params=params(),
        name="logits",
    )(
        *[in_hbm(x.reshape(1, heads)) for x in (decay_scale, dt_bias)],
        *[in_hbm(x) for x in (hidden_states, proj_ba.T, *inputs, *inputs, *taps)],
    )

    taken = lax.ppermute(given, "head", [(i, i ^ 1) for i in range(head_count)])
    logits = [kept, taken] + [
        lax.ppermute(kept[n] + taken[n], "head", [(i, i ^ (2 * n)) for i in range(head_count)])
        for n in range(1, head_count // 2)
    ]
    before = lax.ppermute(tail, "seq", [(i, (i + 1) % seq) for i in range(seq)])

    pick = jnp.asarray(pick_matrix())

    def mix_shapes(count):
        return [(count, tokens, DK), (count, blocks - 1, BLOCK, BLOCK), (count, tokens, 2 * DV)]

    def mix_scratch(count):
        return [
            VMEM((count, tokens, DK), bf16),
            VMEM((count, tokens, 2 * DV), bf16),
            VMEM((count, 3, tokens + 8, DK), f32),
            pltpu.SemaphoreType.DMA((count, 2)),
        ]

    def mix(slots, edge):
        count = len(slots)
        return pl.pallas_call(
            functools.partial(mix_kernel, slots, group, key_width),
            in_specs=[whole(), whole(pl.ANY), whole(pl.ANY)],
            out_specs=[whole()] * 3,
            out_shape=[shape(*dims) for dims in mix_shapes(count)],
            scratch_shapes=mix_scratch(count),
            compiler_params=params(),
            name="mix",
        )(edge, in_hbm(key_in), in_hbm(value_in))

    def solve(slots, start, known, first, unit_keys, key_dots, mixed):
        count = len(slots)
        gate_shapes = [
            shape(group, 4 * blocks, BLOCK),
            shape(group, BLOCK, 8 * blocks),
        ]
        return pl.pallas_call(
            functools.partial(
                solve_kernel, slots, start, group, key_width, len(known) - 1 if first else 0
            ),
            in_specs=[whole()] * (len(known) + 6),
            out_specs=[whole()] * (count + 3 + 2 * first),
            out_shape=[shape(2, DK, 2 * DK)] * count
            + [
                shape(count, 2, tokens, 2 * DK),
                shape(count, 2, blocks - 1, DK, 2 * DK),
                shape(count, BLOCK, DK),
            ]
            + gate_shapes * first,
            scratch_shapes=[VMEM((3, EDGE + 8, DK), f32), VMEM(before.shape, f32)],
            compiler_params=params(),
            name="solve",
        )(*known, unit_keys, key_dots, mixed, before, edge, pick)

    def query(slots, start, unit_keys, solved, starts, first_keys):
        count = len(slots)
        return pl.pallas_call(
            functools.partial(query_kernel, slots, start, group),
            in_specs=[whole()] * 9,
            out_specs=[whole()] * 3,
            out_shape=[shape(count, 2, tokens, DV)]
            + [shape(count, 2, tokens, DK, dtype=bf16)] * 2,
            scratch_shapes=[VMEM((tokens + 8, DK), f32), VMEM(before.shape, f32)],
            compiler_params=params(),
            cost_estimate=pl.CostEstimate(
                flops=2_000_000_000 * count, bytes_accessed=2_000_000 * count, transcendentals=0
            ),
            name="query",
        )(query_in, before, edge, unit_keys, first_keys, *known, solved, starts)

    calls = solve_calls(group)
    mixed = mix(sum(calls[:-1], ()), edge)
    messages, rest, start = [], [], 0
    known = [scales, *logits]
    for slots in calls:
        if slots == calls[-1]:
            known, late = lax.optimization_barrier((known, edge))
            mixed, start = mix(slots, late), 0
        results = solve(slots, start, known, not messages, *mixed)
        if not messages:
            *results, rows, columns = results
            known = [rows, columns]
        results, known = lax.optimization_barrier((results, known))
        messages += results[: len(slots)]
        rest.append([mixed[0], *results[len(slots) :]])
        start += len(slots)

    arrived = [None] * group
    for s in range(group):
        d = slot_partner(group, s)
        arrived[d] = (
            lax.ppermute(messages[s], "seq", [(i, i ^ d) for i in range(seq)]) if d else messages[s]
        )

    messages[-1], rest[0] = lax.optimization_barrier((messages[-1], rest[0]))
    reads = [query(calls[0], 0, *rest[0])]
    arrived, reads = lax.optimization_barrier((arrived, reads))
    chain, leaving = pl.pallas_call(
        functools.partial(prefix_kernel, group),
        in_specs=[whole()] * group,
        out_specs=[whole()] * 2,
        out_shape=[shape(group, 2, DK, 2 * DK), shape(2, DK, DV)],
        compiler_params=params(),
        name="prefix",
    )(*arrived)
    leaving, rest = lax.optimization_barrier((leaving, rest))
    starts = [sum(len(c) for c in calls[:k]) for k in range(len(calls) - 1)] + [0]
    def enter(received, onward):
        return pl.pallas_call(
            functools.partial(enter_kernel, group, onward),
            in_specs=[whole()] * 2,
            out_specs=[whole()] * (group + onward),
            out_shape=[shape(2, DK, DV)] * (group + onward),
            compiler_params=params(),
            name="enter",
        )(received, chain)

    hops = seq // group - 1
    if not hops:
        entering = enter(jnp.zeros((2, DK, DV), f32), False)
    for hop in range(hops):
        received = lax.ppermute(leaving, "seq", [(i, (i + group) % seq) for i in range(seq)])
        if hop == 0:
            reads += [query(*x, *outs) for *x, outs in zip(calls[1:-1], starts[1:-1], rest[1:-1])]
            received, reads, rest = lax.optimization_barrier((received, reads, rest))
        entering = enter(received, hop < hops - 1)
        if hop < hops - 1:
            *entering, leaving = entering

    states = {0: entering[0]}
    for d in range(group - 1, 0, -1):
        states[d] = lax.ppermute(entering[d], "seq", [(i, i ^ d) for i in range(seq)])
    reads.append(query(calls[-1], starts[-1], *rest[-1]))
    where = {s: (k, at) for k, slots in enumerate(calls) for at, s in enumerate(slots)}

    def outputs(slots, written):
        operands = [x for s in slots for x in reads[where[s][0]]]
        operands += [states[slot_partner(group, s)] for s in slots]
        return pl.pallas_call(
            functools.partial(output_kernel, group, [(s, where[s][1]) for s in slots]),
            in_specs=[whole()] * len(operands) + [whole(pl.ANY)] * len(written),
            out_specs=whole(pl.ANY),
            out_shape=shape(tokens, value_width),
            scratch_shapes=[
                VMEM((len(slots), 2, tokens, DV), f32),
                pltpu.SemaphoreType.DMA((len(slots), 2)),
            ],
            input_output_aliases={len(operands): 0} if written else {},
            compiler_params=params(),
            name="outputs",
        )(*operands, *written)

    first = [s for s in range(group) if slot_partner(group, s) < 1]
    written = outputs(first, [])
    return outputs([s for s in range(group) if s not in first], [written])


def solution(mesh):
    placed = (
        P("seq", "head"),
        P("head", None),
        P("seq", "head"),
        P("seq", "head"),
        P("seq", "head"),
        P(None, "head"),
        P(None, "head"),
        P(None, "head"),
        P("head"),
        P("head"),
    )
    return jax.shard_map(
        per_device, mesh=mesh, in_specs=placed, out_specs=P("seq", "head"), check_vma=False
    )
```

```python
import functools
import math

import jax
import jax.numpy as jnp
import numpy as np
from jax import lax
from jax.experimental import pallas as pl
from jax.experimental.pallas import tpu as pltpu
from jax.sharding import PartitionSpec as P

DK = 128
DV = 128
KCONV = 4
BLOCK = 128
SUB = 16
EDGE = 16

f32 = jnp.float32
bf16 = jnp.bfloat16
VMEM = pltpu.VMEM
FAR = -1e30


def split(x):
    hi = x.astype(bf16)
    return hi, (x - hi.astype(f32)).astype(bf16)


def dot_split(a, b, contract=((1,), (0,))):
    (ah, al), (bh, bl) = a, b
    (ca,), (cb,) = contract
    left = jnp.concatenate([ah, al, ah], axis=ca)
    right = jnp.concatenate([bh, bh, bl], axis=cb)
    return lax.dot_general(left, right, (contract, ((), ())), preferred_element_type=f32)


NN = ((1,), (0,))
NT = ((1,), (1,))
TN = ((0,), (0,))


def silu(x):
    return x / (1.0 + jnp.exp(-x))


def unit(x, factor=1.0):
    return x * (lax.rsqrt(jnp.sum(x * x, axis=-1, keepdims=True) + 1e-6) * factor)


def conv_rows(padded_ref, taps, rows):
    total = taps[0:1] * padded_ref[pl.ds(8 - KCONV + 1, rows), :]
    for j in range(1, KCONV):
        total = total + taps[j : j + 1] * padded_ref[pl.ds(8 - KCONV + 1 + j, rows), :]
    return silu(total)


def iotas(rows=BLOCK, columns=BLOCK):
    return (
        lax.broadcasted_iota(jnp.int32, (rows, columns), 0),
        lax.broadcasted_iota(jnp.int32, (rows, columns), 1),
    )


def slot_partner(group, slot):
    order = [d for d in range(group - 1, 0, -1) if d % 2] + [
        d for d in range(group - 1, 0, -1) if d % 2 == 0
    ]
    return (order + [0])[slot]


def solve_calls(group):
    return [(0,), tuple(range(1, group - 1)), (group - 1,)] if group > 2 else [(0,), (1,)]


def in_hbm(x):
    return pltpu.with_memory_space_constraint(x, pltpu.HBM)


HELD = 4


def unpack_before(before_ref, earlier_ref):
    rows = before_ref[...]
    earlier_ref[...] = jnp.where(lax.axis_index("seq") > 0, rows, 0.0)


def fill_before(padded_ref, earlier_ref, tile):
    for i in range(1, KCONV):
        padded_ref[8 - KCONV + i : 9 - KCONV + i, :] = earlier_ref[pl.ds(HELD * tile + i, 1), :]


def lanes(start, size):
    return pl.ds(pl.multiple_of(start, 128), size)


def logits_kernel(
    head_count,
    scale_ref,
    bias_ref,
    hidden_ref,
    proj_ref,
    q_first,
    k_first,
    v_first,
    q_last,
    k_last,
    v_last,
    q_taps,
    k_taps,
    v_taps,
    kept_ref,
    given_ref,
    tail_ref,
    edge_ref,
    scales_ref,
    held,
    packed,
):
    rows = proj_ref.shape[0] // head_count
    everything = lax.dot_general(
        proj_ref[...], hidden_ref[...], (NT, ((), ())), preferred_element_type=f32
    )
    for m in range(head_count):
        held[m] = everything[m * rows : (m + 1) * rows]
    me = lax.axis_index("head")
    for n in range(head_count // 2):
        kept_ref[n] = held[me ^ (2 * n)]
        given_ref[n] = held[me ^ (2 * n + 1)]
    heads = rows // 2
    row, column = iotas(heads, heads)
    scale, bias = (
        jnp.sum(jnp.where(row == column, ref[...], 0.0), axis=1, keepdims=True)
        for ref in (scale_ref, bias_ref)
    )
    scales_ref[...] = jnp.broadcast_to(scale, scales_ref.shape)
    for h in range(heads):
        kept_ref[0, 2 * h : 2 * h + 1, :] = kept_ref[0, 2 * h : 2 * h + 1, :] + bias[h : h + 1]
    edge_ref[...] = jnp.zeros_like(edge_ref)
    packed[...] = jnp.zeros_like(packed)
    start = 0
    for first, last, taps in ((q_first, q_last, q_taps), (k_first, k_last, k_taps), (v_first, v_last, v_taps)):
        here = slice(start, start + first.shape[1])
        rows = last[...].astype(f32)[EDGE - KCONV + 1 :]
        for n in range(first.shape[1] // DK):
            at = HELD * (start // DK + n)
            packed[at + 1 : at + KCONV, :] = rows[:, n * DK : (n + 1) * DK]
        edge_ref[0:EDGE, here] = first[...].astype(f32)
        edge_ref[EDGE : EDGE + KCONV, here] = taps[...].astype(f32)
        start += first.shape[1]
    tail_ref[...] = packed[...]


def mix_kernel(slots, group, key_width, edge_ref, k_ref, v_ref, unit_ref, dots_ref, mixed_ref, k_held, v_held, padded, sems):
    tokens = k_ref.shape[0]
    place = lax.axis_index("seq") % group
    copies = []
    for at, s in enumerate(slots):
        p = place ^ slot_partner(group, s)
        copies.append(
            (
                pltpu.make_async_copy(k_ref.at[:, lanes(p * DK, DK)], k_held.at[at], sems.at[at, 0]),
                pltpu.make_async_copy(
                    v_ref.at[:, lanes(p * 2 * DV, 2 * DV)], v_held.at[at], sems.at[at, 1]
                ),
            )
        )
    for both in copies:
        for copy in both:
            copy.start()
    for at, s in enumerate(slots):
        p = place ^ slot_partner(group, s)
        key_taps = edge_ref[EDGE : EDGE + KCONV, lanes(key_width + p * DK, DK)]
        value_taps = edge_ref[EDGE : EDGE + KCONV, lanes(2 * key_width + p * 2 * DV, 2 * DV)]
        for n in range(3):
            padded[at, n, 0:8] = jnp.zeros((8, DK), f32)
        copies[at][0].wait()
        padded[at, 0, 8:] = k_held[at].astype(f32)
        keys = unit(conv_rows(padded.at[at, 0], key_taps, tokens))
        unit_ref[at] = keys
        for c in range(1, tokens // BLOCK):
            part = split(keys[c * BLOCK : (c + 1) * BLOCK])
            dots_ref[at, c - 1] = dot_split(part, part, NT)
        copies[at][1].wait()
        for b in range(2):
            here = slice(b * DV, (b + 1) * DV)
            padded[at, 1 + b, 8:] = v_held[at, :, here].astype(f32)
            mixed_ref[at, :, here] = conv_rows(padded.at[at, 1 + b], value_taps[:, here], tokens)


def softplus(u):
    e = jnp.exp(-jnp.abs(u))
    small = e * (1.0 - e * (0.5 - e * (1.0 / 3.0 - e * (0.25 - e * 0.2))))
    return jnp.maximum(u, 0.0) + jnp.where(e < 0.03, small, jnp.log(1.0 + e))


def dot_wide(a, b):
    rows, columns = a[0].shape[0], b[0].shape[1]
    four = jnp.dot(
        jnp.concatenate(a, axis=0), jnp.concatenate(b, axis=1), preferred_element_type=f32
    )
    return four[:rows, :columns] + (four[:rows, columns:] + four[rows:, :columns])


def pick_matrix():
    row, column = np.arange(BLOCK)[:, None], np.arange((SUB - 1) * BLOCK)[None, :]
    pick = row == (column % BLOCK) // SUB * SUB + column // BLOCK
    return np.concatenate([pick, pick], axis=0).astype(bf16)


def invert_all(lowers, pick):
    count = len(lowers)
    row, column = iotas()
    blocks = (row // SUB) == (column // SUB)
    folded = []
    for lower in lowers:
        kept = jnp.where(blocks, lower, 0.0)
        total = kept[0:SUB]
        for b in range(1, BLOCK // SUB):
            total = total + kept[b * SUB : (b + 1) * SUB]
        folded.append(total)
    spread = jnp.concatenate(split(jnp.concatenate(folded, axis=0)), axis=1)
    wide = jnp.dot(spread, pick, preferred_element_type=f32).reshape(
        count, SUB, (SUB - 1) * BLOCK
    )
    srow, scolumn = iotas(SUB, BLOCK)
    inverse = jnp.broadcast_to(
        jnp.where(srow == scolumn % SUB, 1.0, 0.0)[None], (count, SUB, BLOCK)
    )
    for j in range(SUB - 1):
        inverse = inverse - wide[:, :, j * BLOCK : (j + 1) * BLOCK] * inverse[:, j : j + 1, :]
    inverses = [inverse[i] for i in range(count)]
    halves = [split(x) for x in lowers]
    size = SUB
    while size < BLOCK:
        same = (row // size) == (column // size)
        across = ((row // (2 * size)) == (column // (2 * size))) & ((row // size) > (column // size))
        same, across = (jnp.where(m, 1.0, 0.0).astype(bf16) for m in (same, across))
        odd = iotas(size, BLOCK)[1] // size % 2 == 1
        dot = dot_wide if size < 64 else dot_split
        parts = [split(x) for x in inverses]
        if 2 * size < BLOCK:
            first = [dot(x, tuple(h * across for h in low)) for x, low in zip(parts, halves)]
        else:
            first = [
                dot(split(jnp.where(odd, x, 0.0)), low) for x, low in zip(inverses, halves)
            ]
        spread = [
            tuple(jnp.concatenate([h] * (BLOCK // size), axis=0) * same for h in x) for x in parts
        ]
        second = [dot(split(x), y) for x, y in zip(first, spread)]
        inverses = [
            jnp.concatenate([jnp.where(odd, 0.0, x), jnp.where(odd, x, -y)], axis=0)
            for x, y in zip(inverses, second)
        ]
        size *= 2
    return inverses


def followed(later, both):
    added, move = later
    both = dot_split(split(move), split(both))
    return jnp.concatenate([both[:, :DV] + added, both[:, DV:]], axis=1)


def gates(p, scales_ref, logit_refs):
    row, column = iotas()
    decays, rates = [], []
    for b in range(2):
        h = 2 * p + b
        u = logit_refs[0][0, pl.ds(2 * h, 1), :] + logit_refs[1][0, pl.ds(2 * h, 1), :]
        w = logit_refs[0][0, pl.ds(2 * h + 1, 1), :] + logit_refs[1][0, pl.ds(2 * h + 1, 1), :]
        for ref in logit_refs[2:]:
            u = u + ref[pl.ds(2 * h, 1), :]
            w = w + ref[pl.ds(2 * h + 1, 1), :]
        decays.append(-scales_ref[pl.ds(h, 1), :] * softplus(u))
        rates.append(1.0 / (1.0 + jnp.exp(-w)))
    blocks = decays[0].shape[1] // BLOCK
    decay_rows, rate_rows = (
        jnp.concatenate(
            [x[:, c * BLOCK : (c + 1) * BLOCK] for x in both for c in range(blocks)], axis=0
        )
        for both in (decays, rates)
    )
    sums = jnp.dot(
        decay_rows,
        jnp.where(row <= column, 1.0, 0.0),
        precision=lax.Precision.HIGHEST,
        preferred_element_type=f32,
    )
    last = sums[:, BLOCK - 1 : BLOCK]
    columns = jnp.concatenate(
        [
            jnp.transpose(x)
            for x in (sums, rate_rows, rate_rows * jnp.exp(sums), jnp.exp(last - sums))
        ],
        axis=1,
    )
    return jnp.concatenate([sums, jnp.broadcast_to(jnp.exp(last), sums.shape)], axis=0), columns


def solve_kernel(
    slots,
    start,
    group,
    key_width,
    pieces,
    *refs,
):
    if pieces:
        (scales_ref, *logit_refs), refs = refs[: 1 + pieces], refs[1 + pieces :]
    else:
        (rows_ref, columns_ref), refs = refs[:2], refs[2:]
    (unit_ref, dots_ref, mixed_ref, before_ref, edge_ref, pick_ref), refs = refs[:6], refs[6:]
    count = len(slots)
    message_refs, refs = refs[:count], refs[count:]
    (solved_ref, starts_ref, first_ref), refs = refs[:3], refs[3:]
    if pieces:
        (rows_ref, columns_ref), refs = refs[:2], refs[2:]
    padded, earlier = refs
    tokens = unit_ref.shape[1]
    blocks = tokens // BLOCK
    height = 2 * blocks
    place = lax.axis_index("seq") % group
    row, column = iotas()
    identity = row == column
    strict = row > column

    known = {}
    unpack_before(before_ref, earlier)
    if pieces:
        for s in range(group):
            known[s] = gates(place ^ slot_partner(group, s), scales_ref, logit_refs)
            rows_ref[s], columns_ref[s] = known[s]
    systems, rights, tails, ends, key_parts = [], [], [], [], []
    for at, s in enumerate(slots):
        p = place ^ slot_partner(group, s)
        kcol, vcol = lanes(key_width + p * DK, DK), lanes(2 * key_width + p * 2 * DV, 2 * DV)
        rows, columns = known[s] if s in known else (rows_ref[s], columns_ref[s])
        key_taps = edge_ref[EDGE : EDGE + KCONV, kcol]
        value_taps = edge_ref[EDGE : EDGE + KCONV, vcol]
        fill_before(padded.at[0], earlier, key_width // DK + p)
        padded[0, 8:] = edge_ref[0:EDGE, kcol]
        edge_keys = unit(conv_rows(padded.at[0], key_taps, EDGE))
        edge_values = edge_ref[0:EDGE, vcol]
        edges = []
        for b in range(2):
            here = slice(b * DV, (b + 1) * DV)
            fill_before(padded.at[1 + b], earlier, 2 * key_width // DK + 2 * p + b)
            padded[1 + b, 8:] = edge_values[:, here]
            edges.append(conv_rows(padded.at[1 + b], value_taps[:, here], EDGE))
        edge_values = jnp.concatenate(edges, axis=1)
        for c in range(blocks):
            keys = unit_ref[start + at, pl.ds(c * BLOCK, BLOCK), :]
            values = mixed_ref[start + at, pl.ds(c * BLOCK, BLOCK), :]
            if c == 0:
                keys = jnp.concatenate([edge_keys, keys[EDGE:]], axis=0)
                values = jnp.concatenate([edge_values, values[EDGE:]], axis=0)
                first_ref[at] = keys
            parts = split(keys)
            key_parts.append(parts)
            dots = dot_split(parts, parts, NT) if c == 0 else dots_ref[start + at, c - 1]
            for b in range(2):
                r = b * blocks + c
                cum, rate, scaled, tail = (
                    columns[:, n * height + r : n * height + r + 1] for n in range(4)
                )
                spread = cum - rows[r : r + 1, :]
                table = jnp.exp(jnp.where(strict, spread, FAR))
                systems.append(rate * table * dots)
                rights.append(
                    jnp.concatenate(
                        [
                            rate * values[:, b * DV : (b + 1) * DV],
                            scaled * keys,
                        ],
                        axis=1,
                    )
                )
                tails.append(tail)
                ends.append(rows[height + r : height + r + 1, :])

    inverses = invert_all(systems, pick_ref[...])
    solved = [dot_split(split(x), split(r)) for x, r in zip(inverses, rights)]
    for at in range(count):
        moves = {}
        for c in range(blocks):
            i = (at * blocks + c) * 2
            both = jnp.concatenate([tails[i] * solved[i], tails[i + 1] * solved[i + 1]], axis=1)
            grown = dot_split(key_parts[at * blocks + c], split(both), TN)
            for b in range(2):
                solved_ref[at, b, pl.ds(c * BLOCK, BLOCK), :] = solved[i + b]
                added = grown[:, b * 2 * DK : b * 2 * DK + DV]
                move = (
                    jnp.where(identity, ends[i + b], 0.0)
                    - grown[:, b * 2 * DK + DV : (b + 1) * 2 * DK]
                )
                moves[b, c] = (added, move)
        for b in range(2):
            half = blocks // 2
            parts = []
            for begin in (0, half):
                both = jnp.concatenate(moves[b, begin], axis=1)
                for c in range(begin + 1, begin + half):
                    if begin == 0:
                        starts_ref[at, b, c - 1] = both
                    both = followed(moves[b, c], both)
                parts.append(both)
            starts_ref[at, b, half - 1] = parts[0]
            for c in range(half, blocks - 1):
                starts_ref[at, b, c] = jnp.concatenate(moves[b, c], axis=1)
            both = followed((parts[1][:, :DV], parts[1][:, DV:]), parts[0])
            message_refs[at][b] = both


def query_kernel(
    slots,
    start,
    group,
    q_ref,
    before_ref,
    edge_ref,
    unit_ref,
    first_ref,
    rows_ref,
    columns_ref,
    solved_ref,
    starts_ref,
    own_ref,
    high_ref,
    low_ref,
    padded,
    earlier,
):
    place = lax.axis_index("seq") % group
    tokens = q_ref.shape[0]
    blocks = tokens // BLOCK
    row, column = iotas()
    causal = row >= column
    unpack_before(before_ref, earlier)
    work = []
    for at, s in enumerate(slots):
        p = place ^ slot_partner(group, s)
        columns = lanes(p * DK, DK)
        fill_before(padded, earlier, p)
        padded[8:] = q_ref[:, columns].astype(f32)
        taps = edge_ref[EDGE : EDGE + KCONV, columns]
        queries = unit(conv_rows(padded, taps, tokens), 1.0 / math.sqrt(DK))
        sums, cum_columns = rows_ref[s], columns_ref[s]
        growth_columns = jnp.exp(cum_columns)
        for c in range(blocks):
            here = queries[c * BLOCK : (c + 1) * BLOCK]
            keys = first_ref[at] if c == 0 else unit_ref[start + at, pl.ds(c * BLOCK, BLOCK), :]
            dots = dot_split(split(here), split(keys), NT)
            for b in range(2):
                r = b * blocks + c
                spread = cum_columns[:, r : r + 1] - sums[r : r + 1, :]
                attend = dots * jnp.exp(jnp.where(causal, spread, FAR))
                grown = growth_columns[:, r : r + 1] * here
                work.append((at, b, c, split(attend), grown))
    seen = [
        dot_split(attend, split(solved_ref[at, b, pl.ds(c * BLOCK, BLOCK), :]))
        for at, b, c, attend, grown in work
    ]
    begins = {}
    for at in range(len(slots)):
        for b in range(2):
            for c in range(1, blocks):
                both = starts_ref[at, b, c - 1]
                if c > blocks // 2:
                    both = followed((both[:, :DV], both[:, DV:]), begins[at, b, c - 1])
                begins[at, b, c] = both
    for (at, b, c, attend, grown), one in zip(work, seen):
        own, reads = one[:, :DV], grown - one[:, DV:]
        if c > 0:
            through = dot_split(split(reads), split(begins[at, b, c]))
            own, reads = own + through[:, :DV], through[:, DV:]
        here = pl.ds(c * BLOCK, BLOCK)
        own_ref[at, b, here, :] = own
        high_ref[at, b, here, :], low_ref[at, b, here, :] = split(reads)


def prefix_kernel(group, *refs):
    messages, (chain_ref, leaving_ref) = refs[:group], refs[group:]
    place = lax.axis_index("seq") % group
    heads = leaving_ref.shape[0]
    for j in range(group):

        @pl.when(place == j)
        def _():
            chain = [messages[j][b] for b in range(heads)]
            for i in range(1, group):
                for b in range(heads):
                    chain_ref[i - 1, b] = chain[b]
                later = messages[j ^ i]
                chain = [
                    followed((later[b, :, 0:DV], later[b, :, DV:]), chain[b]) for b in range(heads)
                ]
            for b in range(heads):
                chain_ref[group - 1, b] = chain[b]
                leaving_ref[b] = chain[b][:, :DV]


def enter_kernel(group, onward, entering_ref, chain_ref, *refs):
    outs = refs[:group]
    place = lax.axis_index("seq") % group
    heads = entering_ref.shape[0]
    count = group if onward else group - 1
    later = lax.axis_index("seq") >= group
    states = [[jnp.where(later, entering_ref[b], 0.0) for b in range(heads)]]
    states += [[] for i in range(count)]
    for b in range(heads):
        moves = jnp.concatenate([chain_ref[i, b, :, DV:] for i in range(count)], axis=0)
        moved = dot_split(split(moves), split(states[0][b]))
        for i in range(count):
            states[i + 1].append(chain_ref[i, b, :, 0:DV] + moved[i * DK : (i + 1) * DK])
    if onward:
        for b in range(heads):
            refs[group][b] = states[group][b]
    for j in range(group):

        @pl.when(place == j)
        def _():
            for i in range(group):
                for b in range(heads):
                    outs[j ^ i][b] = states[i][b]


def output_kernel(group, slots, *refs):
    reads, refs = refs[: 3 * len(slots)], refs[3 * len(slots) :]
    entering, (out_ref, held, sems) = refs[: len(slots)], refs[-3:]
    place = lax.axis_index("seq") % group
    copies = []
    for n, (s, at) in enumerate(slots):
        own_ref, high_ref, low_ref = reads[3 * n : 3 * n + 3]
        p = place ^ slot_partner(group, s)
        for b in range(2):
            state = jnp.concatenate(split(entering[n][b]), axis=1)
            product = jnp.dot(
                jnp.concatenate([high_ref[at, b], low_ref[at, b]], axis=1),
                jnp.concatenate([state, state], axis=0),
                preferred_element_type=f32,
            )
            held[n, b] = own_ref[at, b] + (product[:, :DV] + product[:, DV:])
            copies.append(
                pltpu.make_async_copy(
                    held.at[n, b], out_ref.at[:, lanes((p * 2 + b) * DV, DV)], sems.at[n, b]
                )
            )
            copies[-1].start()
    for copy in copies:
        copy.wait()


def shape(*dims, dtype=f32):
    return jax.ShapeDtypeStruct(dims, dtype)


def params(mib=24):
    return pltpu.CompilerParams(vmem_limit_bytes=mib << 20)


def whole(space=VMEM):
    return pl.BlockSpec(memory_space=space)


def per_device(
    hidden_states,
    proj_ba,
    query_in,
    key_in,
    value_in,
    conv_query,
    conv_key,
    convolution_value_taps,
    decay_scale,
    dt_bias,
):
    tokens = hidden_states.shape[0]
    heads = decay_scale.shape[0]
    pairs = key_in.shape[1] // DK
    blocks = tokens // BLOCK
    key_width, value_width = key_in.shape[1], value_in.shape[1]
    seq, head_count = lax.axis_size("seq"), lax.axis_size("head")
    group = pairs

    def full(block):
        return pl.BlockSpec(block, lambda i: (0,) * len(block))

    last_rows = tokens // EDGE - 1
    width = 2 * key_width + value_width
    inputs = (query_in, key_in, value_in)
    taps = (conv_query, conv_key, convolution_value_taps)
    kept, given, tail, edge, scales = pl.pallas_call(
        functools.partial(logits_kernel, head_count),
        grid=(1,),
        in_specs=[full((1, heads))] * 2 + [full(hidden_states.shape), full(proj_ba.shape[::-1])]
        + [pl.BlockSpec((EDGE, x.shape[1]), lambda i: (0, 0)) for x in inputs]
        + [pl.BlockSpec((EDGE, x.shape[1]), lambda i: (last_rows, 0)) for x in inputs]
        + [full(x.shape) for x in taps],
        out_specs=[whole()] * 5,
        out_shape=[shape(head_count // 2, 2 * heads, tokens)] * 2
        + [shape(HELD * width // DK, DK), shape(EDGE + 8, width), shape(heads, tokens)],
        scratch_shapes=[
            VMEM((head_count, 2 * heads, tokens), f32),
            VMEM((HELD * width // DK, DK), f32),
        ],
        compiler_params=params(),
        name="logits",
    )(
        *[in_hbm(x.reshape(1, heads)) for x in (decay_scale, dt_bias)],
        *[in_hbm(x) for x in (hidden_states, proj_ba.T, *inputs, *inputs, *taps)],
    )

    taken = lax.ppermute(given, "head", [(i, i ^ 1) for i in range(head_count)])
    logits = [kept, taken] + [
        lax.ppermute(kept[n] + taken[n], "head", [(i, i ^ (2 * n)) for i in range(head_count)])
        for n in range(1, head_count // 2)
    ]
    before = lax.ppermute(tail, "seq", [(i, (i + 1) % seq) for i in range(seq)])

    pick = jnp.asarray(pick_matrix())

    def mix_shapes(count):
        return [(count, tokens, DK), (count, blocks - 1, BLOCK, BLOCK), (count, tokens, 2 * DV)]

    def mix_scratch(count):
        return [
            VMEM((count, tokens, DK), bf16),
            VMEM((count, tokens, 2 * DV), bf16),
            VMEM((count, 3, tokens + 8, DK), f32),
            pltpu.SemaphoreType.DMA((count, 2)),
        ]

    def mix(slots, edge):
        count = len(slots)
        return pl.pallas_call(
            functools.partial(mix_kernel, slots, group, key_width),
            in_specs=[whole(), whole(pl.ANY), whole(pl.ANY)],
            out_specs=[whole()] * 3,
            out_shape=[shape(*dims) for dims in mix_shapes(count)],
            scratch_shapes=mix_scratch(count),
            compiler_params=params(),
            name="mix",
        )(edge, in_hbm(key_in), in_hbm(value_in))

    def solve(slots, start, known, first, unit_keys, key_dots, mixed):
        count = len(slots)
        gate_shapes = [
            shape(group, 4 * blocks, BLOCK),
            shape(group, BLOCK, 8 * blocks),
        ]
        return pl.pallas_call(
            functools.partial(
                solve_kernel, slots, start, group, key_width, len(known) - 1 if first else 0
            ),
            in_specs=[whole()] * (len(known) + 6),
            out_specs=[whole()] * (count + 3 + 2 * first),
            out_shape=[shape(2, DK, 2 * DK)] * count
            + [
                shape(count, 2, tokens, 2 * DK),
                shape(count, 2, blocks - 1, DK, 2 * DK),
                shape(count, BLOCK, DK),
            ]
            + gate_shapes * first,
            scratch_shapes=[VMEM((3, EDGE + 8, DK), f32), VMEM(before.shape, f32)],
            compiler_params=params(),
            name="solve",
        )(*known, unit_keys, key_dots, mixed, before, edge, pick)

    def query(slots, start, unit_keys, solved, starts, first_keys):
        count = len(slots)
        return pl.pallas_call(
            functools.partial(query_kernel, slots, start, group),
            in_specs=[whole()] * 9,
            out_specs=[whole()] * 3,
            out_shape=[shape(count, 2, tokens, DV)]
            + [shape(count, 2, tokens, DK, dtype=bf16)] * 2,
            scratch_shapes=[VMEM((tokens + 8, DK), f32), VMEM(before.shape, f32)],
            compiler_params=params(),
            cost_estimate=pl.CostEstimate(
                flops=2_000_000_000 * count, bytes_accessed=2_000_000 * count, transcendentals=0
            ),
            name="query",
        )(query_in, before, edge, unit_keys, first_keys, *known, solved, starts)

    calls = solve_calls(group)
    mixed = mix(sum(calls[:-1], ()), edge)
    messages, rest, start = [], [], 0
    known = [scales, *logits]
    for slots in calls:
        if slots == calls[-1]:
            known, late = lax.optimization_barrier((known, edge))
            mixed, start = mix(slots, late), 0
        results = solve(slots, start, known, not messages, *mixed)
        if not messages:
            *results, rows, columns = results
            known = [rows, columns]
        results, known = lax.optimization_barrier((results, known))
        messages += results[: len(slots)]
        rest.append([mixed[0], *results[len(slots) :]])
        start += len(slots)

    arrived = [None] * group
    for s in range(group):
        d = slot_partner(group, s)
        arrived[d] = (
            lax.ppermute(messages[s], "seq", [(i, i ^ d) for i in range(seq)]) if d else messages[s]
        )

    messages[-1], rest[0] = lax.optimization_barrier((messages[-1], rest[0]))
    reads = []
    chain, leaving = pl.pallas_call(
        functools.partial(prefix_kernel, group),
        in_specs=[whole()] * group,
        out_specs=[whole()] * 2,
        out_shape=[shape(group, 2, DK, 2 * DK), shape(2, DK, DV)],
        compiler_params=params(),
        name="prefix",
    )(*arrived)
    leaving, rest = lax.optimization_barrier((leaving, rest))
    starts = [sum(len(c) for c in calls[:k]) for k in range(len(calls) - 1)] + [0]
    def enter(received, onward):
        return pl.pallas_call(
            functools.partial(enter_kernel, group, onward),
            in_specs=[whole()] * 2,
            out_specs=[whole()] * (group + onward),
            out_shape=[shape(2, DK, DV)] * (group + onward),
            compiler_params=params(),
            name="enter",
        )(received, chain)

    hops = seq // group - 1
    if not hops:
        entering = enter(jnp.zeros((2, DK, DV), f32), False)
    for hop in range(hops):
        received = lax.ppermute(leaving, "seq", [(i, (i + group) % seq) for i in range(seq)])
        if hop == 0:
            reads += [query(*x, *outs) for *x, outs in zip(calls[:-1], starts[:-1], rest[:-1])]
            received, reads, rest = lax.optimization_barrier((received, reads, rest))
        entering = enter(received, hop < hops - 1)
        if hop < hops - 1:
            *entering, leaving = entering

    states = {0: entering[0]}
    for d in range(group - 1, 0, -1):
        states[d] = lax.ppermute(entering[d], "seq", [(i, i ^ d) for i in range(seq)])
    reads.append(query(calls[-1], starts[-1], *rest[-1]))
    where = {s: (k, at) for k, slots in enumerate(calls) for at, s in enumerate(slots)}

    def outputs(slots, written):
        operands = [x for s in slots for x in reads[where[s][0]]]
        operands += [states[slot_partner(group, s)] for s in slots]
        return pl.pallas_call(
            functools.partial(output_kernel, group, [(s, where[s][1]) for s in slots]),
            in_specs=[whole()] * len(operands) + [whole(pl.ANY)] * len(written),
            out_specs=whole(pl.ANY),
            out_shape=shape(tokens, value_width),
            scratch_shapes=[
                VMEM((len(slots), 2, tokens, DV), f32),
                pltpu.SemaphoreType.DMA((len(slots), 2)),
            ],
            input_output_aliases={len(operands): 0} if written else {},
            compiler_params=params(),
            name="outputs",
        )(*operands, *written)

    first = [s for s in range(group) if slot_partner(group, s) < 1]
    written = outputs(first, [])
    return outputs([s for s in range(group) if s not in first], [written])


def solution(mesh):
    placed = (
        P("seq", "head"),
        P("head", None),
        P("seq", "head"),
        P("seq", "head"),
        P("seq", "head"),
        P(None, "head"),
        P(None, "head"),
        P(None, "head"),
        P("head"),
        P("head"),
    )
    return jax.shard_map(
        per_device, mesh=mesh, in_specs=placed, out_specs=P("seq", "head"), check_vma=False
    )
```

```python
import functools
import math

import jax
import jax.numpy as jnp
import numpy as np
from jax import lax
from jax.experimental import pallas as pl
from jax.experimental.pallas import tpu as pltpu
from jax.sharding import PartitionSpec as P

DK = 128
DV = 128
KCONV = 4
BLOCK = 128
SUB = 16
EDGE = 16

f32 = jnp.float32
bf16 = jnp.bfloat16
VMEM = pltpu.VMEM
FAR = -1e30


def split(x):
    hi = x.astype(bf16)
    return hi, (x - hi.astype(f32)).astype(bf16)


def dot_split(a, b, contract=((1,), (0,))):
    (ah, al), (bh, bl) = a, b
    (ca,), (cb,) = contract
    left = jnp.concatenate([ah, al, ah], axis=ca)
    right = jnp.concatenate([bh, bh, bl], axis=cb)
    return lax.dot_general(left, right, (contract, ((), ())), preferred_element_type=f32)


NN = ((1,), (0,))
NT = ((1,), (1,))
TN = ((0,), (0,))


def silu(x):
    return x / (1.0 + jnp.exp(-x))


def unit(x, factor=1.0):
    return x * (lax.rsqrt(jnp.sum(x * x, axis=-1, keepdims=True) + 1e-6) * factor)


def conv_rows(padded_ref, taps, rows):
    total = taps[0:1] * padded_ref[pl.ds(8 - KCONV + 1, rows), :]
    for j in range(1, KCONV):
        total = total + taps[j : j + 1] * padded_ref[pl.ds(8 - KCONV + 1 + j, rows), :]
    return silu(total)


def iotas(rows=BLOCK, columns=BLOCK):
    return (
        lax.broadcasted_iota(jnp.int32, (rows, columns), 0),
        lax.broadcasted_iota(jnp.int32, (rows, columns), 1),
    )


def slot_partner(group, slot):
    order = [d for d in range(group - 1, 0, -1) if d % 2] + [
        d for d in range(group - 1, 0, -1) if d % 2 == 0
    ]
    return (order + [0])[slot]


def solve_calls(group):
    return [(0,), tuple(range(1, group - 1)), (group - 1,)] if group > 2 else [(0,), (1,)]


def in_hbm(x):
    return pltpu.with_memory_space_constraint(x, pltpu.HBM)


HELD = 4


def unpack_before(before_ref, earlier_ref):
    rows = before_ref[...]
    earlier_ref[...] = jnp.where(lax.axis_index("seq") > 0, rows, 0.0)


def fill_before(padded_ref, earlier_ref, tile):
    for i in range(1, KCONV):
        padded_ref[8 - KCONV + i : 9 - KCONV + i, :] = earlier_ref[pl.ds(HELD * tile + i, 1), :]


def lanes(start, size):
    return pl.ds(pl.multiple_of(start, 128), size)


def logits_kernel(
    head_count,
    scale_ref,
    bias_ref,
    hidden_ref,
    proj_ref,
    q_first,
    k_first,
    v_first,
    q_last,
    k_last,
    v_last,
    q_taps,
    k_taps,
    v_taps,
    kept_ref,
    given_ref,
    tail_ref,
    edge_ref,
    scales_ref,
    held,
    packed,
):
    rows = proj_ref.shape[0] // head_count
    everything = lax.dot_general(
        proj_ref[...], hidden_ref[...], (NT, ((), ())), preferred_element_type=f32
    )
    for m in range(head_count):
        held[m] = everything[m * rows : (m + 1) * rows]
    me = lax.axis_index("head")
    for n in range(head_count // 2):
        kept_ref[n] = held[me ^ (2 * n)]
        given_ref[n] = held[me ^ (2 * n + 1)]
    heads = rows // 2
    row, column = iotas(heads, heads)
    scale, bias = (
        jnp.sum(jnp.where(row == column, ref[...], 0.0), axis=1, keepdims=True)
        for ref in (scale_ref, bias_ref)
    )
    scales_ref[...] = jnp.broadcast_to(scale, scales_ref.shape)
    for h in range(heads):
        kept_ref[0, 2 * h : 2 * h + 1, :] = kept_ref[0, 2 * h : 2 * h + 1, :] + bias[h : h + 1]
    edge_ref[...] = jnp.zeros_like(edge_ref)
    packed[...] = jnp.zeros_like(packed)
    start = 0
    for first, last, taps in ((q_first, q_last, q_taps), (k_first, k_last, k_taps), (v_first, v_last, v_taps)):
        here = slice(start, start + first.shape[1])
        rows = last[...].astype(f32)[EDGE - KCONV + 1 :]
        for n in range(first.shape[1] // DK):
            at = HELD * (start // DK + n)
            packed[at + 1 : at + KCONV, :] = rows[:, n * DK : (n + 1) * DK]
        edge_ref[0:EDGE, here] = first[...].astype(f32)
        edge_ref[EDGE : EDGE + KCONV, here] = taps[...].astype(f32)
        start += first.shape[1]
    tail_ref[...] = packed[...]


def mix_kernel(slots, group, key_width, edge_ref, k_ref, v_ref, unit_ref, dots_ref, mixed_ref, k_held, v_held, padded, sems):
    tokens = k_ref.shape[0]
    place = lax.axis_index("seq") % group
    copies = []
    for at, s in enumerate(slots):
        p = place ^ slot_partner(group, s)
        copies.append(
            (
                pltpu.make_async_copy(k_ref.at[:, lanes(p * DK, DK)], k_held.at[at], sems.at[at, 0]),
                pltpu.make_async_copy(
                    v_ref.at[:, lanes(p * 2 * DV, 2 * DV)], v_held.at[at], sems.at[at, 1]
                ),
            )
        )
    for both in copies:
        for copy in both:
            copy.start()
    for at, s in enumerate(slots):
        p = place ^ slot_partner(group, s)
        key_taps = edge_ref[EDGE : EDGE + KCONV, lanes(key_width + p * DK, DK)]
        value_taps = edge_ref[EDGE : EDGE + KCONV, lanes(2 * key_width + p * 2 * DV, 2 * DV)]
        for n in range(3):
            padded[at, n, 0:8] = jnp.zeros((8, DK), f32)
        copies[at][0].wait()
        padded[at, 0, 8:] = k_held[at].astype(f32)
        keys = unit(conv_rows(padded.at[at, 0], key_taps, tokens))
        unit_ref[at] = keys
        for c in range(1, tokens // BLOCK):
            part = split(keys[c * BLOCK : (c + 1) * BLOCK])
            dots_ref[at, c - 1] = dot_split(part, part, NT)
        copies[at][1].wait()
        for b in range(2):
            here = slice(b * DV, (b + 1) * DV)
            padded[at, 1 + b, 8:] = v_held[at, :, here].astype(f32)
            mixed_ref[at, :, here] = conv_rows(padded.at[at, 1 + b], value_taps[:, here], tokens)


def softplus(u):
    e = jnp.exp(-jnp.abs(u))
    small = e * (1.0 - e * (0.5 - e * (1.0 / 3.0 - e * (0.25 - e * 0.2))))
    return jnp.maximum(u, 0.0) + jnp.where(e < 0.03, small, jnp.log(1.0 + e))


def dot_wide(a, b):
    rows, columns = a[0].shape[0], b[0].shape[1]
    four = jnp.dot(
        jnp.concatenate(a, axis=0), jnp.concatenate(b, axis=1), preferred_element_type=f32
    )
    return four[:rows, :columns] + (four[:rows, columns:] + four[rows:, :columns])


def pick_matrix():
    row, column = np.arange(BLOCK)[:, None], np.arange((SUB - 1) * BLOCK)[None, :]
    pick = row == (column % BLOCK) // SUB * SUB + column // BLOCK
    return np.concatenate([pick, pick], axis=0).astype(bf16)


def invert_all(lowers, pick):
    count = len(lowers)
    row, column = iotas()
    blocks = (row // SUB) == (column // SUB)
    folded = []
    for lower in lowers:
        kept = jnp.where(blocks, lower, 0.0)
        total = kept[0:SUB]
        for b in range(1, BLOCK // SUB):
            total = total + kept[b * SUB : (b + 1) * SUB]
        folded.append(total)
    spread = jnp.concatenate(split(jnp.concatenate(folded, axis=0)), axis=1)
    wide = jnp.dot(spread, pick, preferred_element_type=f32).reshape(
        count, SUB, (SUB - 1) * BLOCK
    )
    srow, scolumn = iotas(SUB, BLOCK)
    inverse = jnp.broadcast_to(
        jnp.where(srow == scolumn % SUB, 1.0, 0.0)[None], (count, SUB, BLOCK)
    )
    for j in range(SUB - 1):
        inverse = inverse - wide[:, :, j * BLOCK : (j + 1) * BLOCK] * inverse[:, j : j + 1, :]
    inverses = [inverse[i] for i in range(count)]
    halves = [split(x) for x in lowers]
    size = SUB
    while size < BLOCK:
        same = (row // size) == (column // size)
        across = ((row // (2 * size)) == (column // (2 * size))) & ((row // size) > (column // size))
        same, across = (jnp.where(m, 1.0, 0.0).astype(bf16) for m in (same, across))
        odd = iotas(size, BLOCK)[1] // size % 2 == 1
        dot = dot_wide if size < 64 else dot_split
        parts = [split(x) for x in inverses]
        if 2 * size < BLOCK:
            first = [dot(x, tuple(h * across for h in low)) for x, low in zip(parts, halves)]
        else:
            first = [
                dot(split(jnp.where(odd, x, 0.0)), low) for x, low in zip(inverses, halves)
            ]
        spread = [
            tuple(jnp.concatenate([h] * (BLOCK // size), axis=0) * same for h in x) for x in parts
        ]
        second = [dot(split(x), y) for x, y in zip(first, spread)]
        inverses = [
            jnp.concatenate([jnp.where(odd, 0.0, x), jnp.where(odd, x, -y)], axis=0)
            for x, y in zip(inverses, second)
        ]
        size *= 2
    return inverses


def followed(later, both):
    added, move = later
    both = dot_split(split(move), split(both))
    return jnp.concatenate([both[:, :DV] + added, both[:, DV:]], axis=1)


def gates(p, scales_ref, logit_refs):
    row, column = iotas()
    decays, rates = [], []
    for b in range(2):
        h = 2 * p + b
        u = logit_refs[0][0, pl.ds(2 * h, 1), :] + logit_refs[1][0, pl.ds(2 * h, 1), :]
        w = logit_refs[0][0, pl.ds(2 * h + 1, 1), :] + logit_refs[1][0, pl.ds(2 * h + 1, 1), :]
        for ref in logit_refs[2:]:
            u = u + ref[pl.ds(2 * h, 1), :]
            w = w + ref[pl.ds(2 * h + 1, 1), :]
        decays.append(-scales_ref[pl.ds(h, 1), :] * softplus(u))
        rates.append(1.0 / (1.0 + jnp.exp(-w)))
    blocks = decays[0].shape[1] // BLOCK
    decay_rows, rate_rows = (
        jnp.concatenate(
            [x[:, c * BLOCK : (c + 1) * BLOCK] for x in both for c in range(blocks)], axis=0
        )
        for both in (decays, rates)
    )
    sums = jnp.dot(
        decay_rows,
        jnp.where(row <= column, 1.0, 0.0),
        precision=lax.Precision.HIGHEST,
        preferred_element_type=f32,
    )
    last = sums[:, BLOCK - 1 : BLOCK]
    columns = jnp.concatenate(
        [
            jnp.transpose(x)
            for x in (sums, rate_rows, rate_rows * jnp.exp(sums), jnp.exp(last - sums))
        ],
        axis=1,
    )
    return jnp.concatenate([sums, jnp.broadcast_to(jnp.exp(last), sums.shape)], axis=0), columns


def solve_kernel(
    slots,
    start,
    group,
    key_width,
    pieces,
    *refs,
):
    if pieces:
        (scales_ref, *logit_refs), refs = refs[: 1 + pieces], refs[1 + pieces :]
    else:
        (rows_ref, columns_ref), refs = refs[:2], refs[2:]
    (unit_ref, dots_ref, mixed_ref, before_ref, edge_ref, pick_ref), refs = refs[:6], refs[6:]
    count = len(slots)
    message_refs, refs = refs[:count], refs[count:]
    (solved_ref, starts_ref, first_ref), refs = refs[:3], refs[3:]
    if pieces:
        (rows_ref, columns_ref), refs = refs[:2], refs[2:]
    padded, earlier = refs
    tokens = unit_ref.shape[1]
    blocks = tokens // BLOCK
    height = 2 * blocks
    place = lax.axis_index("seq") % group
    row, column = iotas()
    identity = row == column
    strict = row > column

    known = {}
    unpack_before(before_ref, earlier)
    if pieces:
        for s in range(group):
            known[s] = gates(place ^ slot_partner(group, s), scales_ref, logit_refs)
            rows_ref[s], columns_ref[s] = known[s]
    systems, rights, tails, ends, key_parts = [], [], [], [], []
    for at, s in enumerate(slots):
        p = place ^ slot_partner(group, s)
        kcol, vcol = lanes(key_width + p * DK, DK), lanes(2 * key_width + p * 2 * DV, 2 * DV)
        rows, columns = known[s] if s in known else (rows_ref[s], columns_ref[s])
        key_taps = edge_ref[EDGE : EDGE + KCONV, kcol]
        value_taps = edge_ref[EDGE : EDGE + KCONV, vcol]
        fill_before(padded.at[0], earlier, key_width // DK + p)
        padded[0, 8:] = edge_ref[0:EDGE, kcol]
        edge_keys = unit(conv_rows(padded.at[0], key_taps, EDGE))
        edge_values = edge_ref[0:EDGE, vcol]
        edges = []
        for b in range(2):
            here = slice(b * DV, (b + 1) * DV)
            fill_before(padded.at[1 + b], earlier, 2 * key_width // DK + 2 * p + b)
            padded[1 + b, 8:] = edge_values[:, here]
            edges.append(conv_rows(padded.at[1 + b], value_taps[:, here], EDGE))
        edge_values = jnp.concatenate(edges, axis=1)
        for c in range(blocks):
            keys = unit_ref[start + at, pl.ds(c * BLOCK, BLOCK), :]
            values = mixed_ref[start + at, pl.ds(c * BLOCK, BLOCK), :]
            if c == 0:
                keys = jnp.concatenate([edge_keys, keys[EDGE:]], axis=0)
                values = jnp.concatenate([edge_values, values[EDGE:]], axis=0)
                first_ref[at] = keys
            parts = split(keys)
            key_parts.append(parts)
            dots = dot_split(parts, parts, NT) if c == 0 else dots_ref[start + at, c - 1]
            for b in range(2):
                r = b * blocks + c
                cum, rate, scaled, tail = (
                    columns[:, n * height + r : n * height + r + 1] for n in range(4)
                )
                spread = cum - rows[r : r + 1, :]
                table = jnp.exp(jnp.where(strict, spread, FAR))
                systems.append(rate * table * dots)
                rights.append(
                    jnp.concatenate(
                        [
                            rate * values[:, b * DV : (b + 1) * DV],
                            scaled * keys,
                        ],
                        axis=1,
                    )
                )
                tails.append(tail)
                ends.append(rows[height + r : height + r + 1, :])

    inverses = invert_all(systems, pick_ref[...])
    solved = [dot_split(split(x), split(r)) for x, r in zip(inverses, rights)]
    for at in range(count):
        moves = {}
        for c in range(blocks):
            i = (at * blocks + c) * 2
            both = jnp.concatenate([tails[i] * solved[i], tails[i + 1] * solved[i + 1]], axis=1)
            grown = dot_split(key_parts[at * blocks + c], split(both), TN)
            for b in range(2):
                solved_ref[at, b, pl.ds(c * BLOCK, BLOCK), :] = solved[i + b]
                added = grown[:, b * 2 * DK : b * 2 * DK + DV]
                move = (
                    jnp.where(identity, ends[i + b], 0.0)
                    - grown[:, b * 2 * DK + DV : (b + 1) * 2 * DK]
                )
                moves[b, c] = (added, move)
        for b in range(2):
            half = blocks // 2
            parts = []
            for begin in (0, half):
                both = jnp.concatenate(moves[b, begin], axis=1)
                for c in range(begin + 1, begin + half):
                    if begin == 0:
                        starts_ref[at, b, c - 1] = both
                    both = followed(moves[b, c], both)
                parts.append(both)
            starts_ref[at, b, half - 1] = parts[0]
            for c in range(half, blocks - 1):
                starts_ref[at, b, c] = jnp.concatenate(moves[b, c], axis=1)
            both = followed((parts[1][:, :DV], parts[1][:, DV:]), parts[0])
            message_refs[at][b] = both


def query_kernel(
    slots,
    start,
    group,
    q_ref,
    before_ref,
    edge_ref,
    unit_ref,
    first_ref,
    rows_ref,
    columns_ref,
    solved_ref,
    starts_ref,
    own_ref,
    high_ref,
    low_ref,
    padded,
    earlier,
):
    place = lax.axis_index("seq") % group
    tokens = q_ref.shape[0]
    blocks = tokens // BLOCK
    row, column = iotas()
    causal = row >= column
    unpack_before(before_ref, earlier)
    work = []
    for at, s in enumerate(slots):
        p = place ^ slot_partner(group, s)
        columns = lanes(p * DK, DK)
        fill_before(padded, earlier, p)
        padded[8:] = q_ref[:, columns].astype(f32)
        taps = edge_ref[EDGE : EDGE + KCONV, columns]
        queries = unit(conv_rows(padded, taps, tokens), 1.0 / math.sqrt(DK))
        sums, cum_columns = rows_ref[s], columns_ref[s]
        growth_columns = jnp.exp(cum_columns)
        for c in range(blocks):
            here = queries[c * BLOCK : (c + 1) * BLOCK]
            keys = first_ref[at] if c == 0 else unit_ref[start + at, pl.ds(c * BLOCK, BLOCK), :]
            dots = dot_split(split(here), split(keys), NT)
            for b in range(2):
                r = b * blocks + c
                spread = cum_columns[:, r : r + 1] - sums[r : r + 1, :]
                attend = dots * jnp.exp(jnp.where(causal, spread, FAR))
                grown = growth_columns[:, r : r + 1] * here
                work.append((at, b, c, split(attend), grown))
    seen = [
        dot_split(attend, split(solved_ref[at, b, pl.ds(c * BLOCK, BLOCK), :]))
        for at, b, c, attend, grown in work
    ]
    begins = {}
    for at in range(len(slots)):
        for b in range(2):
            for c in range(1, blocks):
                both = starts_ref[at, b, c - 1]
                if c > blocks // 2:
                    both = followed((both[:, :DV], both[:, DV:]), begins[at, b, c - 1])
                begins[at, b, c] = both
    for (at, b, c, attend, grown), one in zip(work, seen):
        own, reads = one[:, :DV], grown - one[:, DV:]
        if c > 0:
            through = dot_split(split(reads), split(begins[at, b, c]))
            own, reads = own + through[:, :DV], through[:, DV:]
        here = pl.ds(c * BLOCK, BLOCK)
        own_ref[at, b, here, :] = own
        high_ref[at, b, here, :], low_ref[at, b, here, :] = split(reads)


def prefix_kernel(group, onward, *refs):
    messages, (chain_ref, leaving_ref) = refs[:group], refs[group:]
    place = lax.axis_index("seq") % group
    heads = leaving_ref.shape[0]
    for j in range(group):

        @pl.when(place == j)
        def _():
            chain = [messages[j][b] for b in range(heads)]
            for i in range(1, group):
                for b in range(heads):
                    chain_ref[i - 1, b] = chain[b]
                later = messages[j ^ i]
                if i == group - 1 and not onward:
                    chain = [chain[b][:, :DV] for b in range(heads)]
                    chain = [
                        later[b, :, 0:DV] + dot_split(split(later[b, :, DV:]), split(chain[b]))
                        for b in range(heads)
                    ]
                    break
                chain = [
                    followed((later[b, :, 0:DV], later[b, :, DV:]), chain[b]) for b in range(heads)
                ]
            for b in range(heads):
                if onward:
                    chain_ref[group - 1, b] = chain[b]
                leaving_ref[b] = chain[b][:, :DV]


def enter_kernel(group, onward, entering_ref, chain_ref, *refs):
    outs = refs[:group]
    place = lax.axis_index("seq") % group
    heads = entering_ref.shape[0]
    count = group if onward else group - 1
    later = lax.axis_index("seq") >= group
    states = [[jnp.where(later, entering_ref[b], 0.0) for b in range(heads)]]
    states += [[] for i in range(count)]
    for b in range(heads):
        moves = jnp.concatenate([chain_ref[i, b, :, DV:] for i in range(count)], axis=0)
        moved = dot_split(split(moves), split(states[0][b]))
        for i in range(count):
            states[i + 1].append(chain_ref[i, b, :, 0:DV] + moved[i * DK : (i + 1) * DK])
    if onward:
        for b in range(heads):
            refs[group][b] = states[group][b]
    for j in range(group):

        @pl.when(place == j)
        def _():
            for i in range(group):
                for b in range(heads):
                    outs[j ^ i][b] = states[i][b]


def output_kernel(group, slots, *refs):
    reads, refs = refs[: 3 * len(slots)], refs[3 * len(slots) :]
    entering, (out_ref, held, sems) = refs[: len(slots)], refs[-3:]
    place = lax.axis_index("seq") % group
    copies = []
    for n, (s, at) in enumerate(slots):
        own_ref, high_ref, low_ref = reads[3 * n : 3 * n + 3]
        p = place ^ slot_partner(group, s)
        for b in range(2):
            state = jnp.concatenate(split(entering[n][b]), axis=1)
            product = jnp.dot(
                jnp.concatenate([high_ref[at, b], low_ref[at, b]], axis=1),
                jnp.concatenate([state, state], axis=0),
                preferred_element_type=f32,
            )
            held[n, b] = own_ref[at, b] + (product[:, :DV] + product[:, DV:])
            copies.append(
                pltpu.make_async_copy(
                    held.at[n, b], out_ref.at[:, lanes((p * 2 + b) * DV, DV)], sems.at[n, b]
                )
            )
            copies[-1].start()
    for copy in copies:
        copy.wait()


def shape(*dims, dtype=f32):
    return jax.ShapeDtypeStruct(dims, dtype)


def params(mib=24):
    return pltpu.CompilerParams(vmem_limit_bytes=mib << 20)


def whole(space=VMEM):
    return pl.BlockSpec(memory_space=space)


def per_device(
    hidden_states,
    proj_ba,
    query_in,
    key_in,
    value_in,
    conv_query,
    conv_key,
    convolution_value_taps,
    decay_scale,
    dt_bias,
):
    tokens = hidden_states.shape[0]
    heads = decay_scale.shape[0]
    pairs = key_in.shape[1] // DK
    blocks = tokens // BLOCK
    key_width, value_width = key_in.shape[1], value_in.shape[1]
    seq, head_count = lax.axis_size("seq"), lax.axis_size("head")
    group = pairs

    def full(block):
        return pl.BlockSpec(block, lambda i: (0,) * len(block))

    last_rows = tokens // EDGE - 1
    width = 2 * key_width + value_width
    inputs = (query_in, key_in, value_in)
    taps = (conv_query, conv_key, convolution_value_taps)
    kept, given, tail, edge, scales = pl.pallas_call(
        functools.partial(logits_kernel, head_count),
        grid=(1,),
        in_specs=[full((1, heads))] * 2 + [full(hidden_states.shape), full(proj_ba.shape[::-1])]
        + [pl.BlockSpec((EDGE, x.shape[1]), lambda i: (0, 0)) for x in inputs]
        + [pl.BlockSpec((EDGE, x.shape[1]), lambda i: (last_rows, 0)) for x in inputs]
        + [full(x.shape) for x in taps],
        out_specs=[whole()] * 5,
        out_shape=[shape(head_count // 2, 2 * heads, tokens)] * 2
        + [shape(HELD * width // DK, DK), shape(EDGE + 8, width), shape(heads, tokens)],
        scratch_shapes=[
            VMEM((head_count, 2 * heads, tokens), f32),
            VMEM((HELD * width // DK, DK), f32),
        ],
        compiler_params=params(),
        name="logits",
    )(
        *[in_hbm(x.reshape(1, heads)) for x in (decay_scale, dt_bias)],
        *[in_hbm(x) for x in (hidden_states, proj_ba.T, *inputs, *inputs, *taps)],
    )

    taken = lax.ppermute(given, "head", [(i, i ^ 1) for i in range(head_count)])
    logits = [kept, taken] + [
        lax.ppermute(kept[n] + taken[n], "head", [(i, i ^ (2 * n)) for i in range(head_count)])
        for n in range(1, head_count // 2)
    ]
    before = lax.ppermute(tail, "seq", [(i, (i + 1) % seq) for i in range(seq)])

    pick = jnp.asarray(pick_matrix())

    def mix_shapes(count):
        return [(count, tokens, DK), (count, blocks - 1, BLOCK, BLOCK), (count, tokens, 2 * DV)]

    def mix_scratch(count):
        return [
            VMEM((count, tokens, DK), bf16),
            VMEM((count, tokens, 2 * DV), bf16),
            VMEM((count, 3, tokens + 8, DK), f32),
            pltpu.SemaphoreType.DMA((count, 2)),
        ]

    def mix(slots, edge):
        count = len(slots)
        return pl.pallas_call(
            functools.partial(mix_kernel, slots, group, key_width),
            in_specs=[whole(), whole(pl.ANY), whole(pl.ANY)],
            out_specs=[whole()] * 3,
            out_shape=[shape(*dims) for dims in mix_shapes(count)],
            scratch_shapes=mix_scratch(count),
            compiler_params=params(),
            name="mix",
        )(edge, in_hbm(key_in), in_hbm(value_in))

    def solve(slots, start, known, first, unit_keys, key_dots, mixed):
        count = len(slots)
        gate_shapes = [
            shape(group, 4 * blocks, BLOCK),
            shape(group, BLOCK, 8 * blocks),
        ]
        return pl.pallas_call(
            functools.partial(
                solve_kernel, slots, start, group, key_width, len(known) - 1 if first else 0
            ),
            in_specs=[whole()] * (len(known) + 6),
            out_specs=[whole()] * (count + 3 + 2 * first),
            out_shape=[shape(2, DK, 2 * DK)] * count
            + [
                shape(count, 2, tokens, 2 * DK),
                shape(count, 2, blocks - 1, DK, 2 * DK),
                shape(count, BLOCK, DK),
            ]
            + gate_shapes * first,
            scratch_shapes=[VMEM((3, EDGE + 8, DK), f32), VMEM(before.shape, f32)],
            compiler_params=params(),
            name="solve",
        )(*known, unit_keys, key_dots, mixed, before, edge, pick)

    def query(slots, start, unit_keys, solved, starts, first_keys):
        count = len(slots)
        return pl.pallas_call(
            functools.partial(query_kernel, slots, start, group),
            in_specs=[whole()] * 9,
            out_specs=[whole()] * 3,
            out_shape=[shape(count, 2, tokens, DV)]
            + [shape(count, 2, tokens, DK, dtype=bf16)] * 2,
            scratch_shapes=[VMEM((tokens + 8, DK), f32), VMEM(before.shape, f32)],
            compiler_params=params(),
            cost_estimate=pl.CostEstimate(
                flops=2_000_000_000 * count, bytes_accessed=2_000_000 * count, transcendentals=0
            ),
            name="query",
        )(query_in, before, edge, unit_keys, first_keys, *known, solved, starts)

    calls = solve_calls(group)
    mixed = mix(sum(calls[:-1], ()), edge)
    messages, rest, start = [], [], 0
    known = [scales, *logits]
    for slots in calls:
        if slots == calls[-1]:
            known, late = lax.optimization_barrier((known, edge))
            mixed, start = mix(slots, late), 0
        results = solve(slots, start, known, not messages, *mixed)
        if not messages:
            *results, rows, columns = results
            known = [rows, columns]
        results, known = lax.optimization_barrier((results, known))
        messages += results[: len(slots)]
        rest.append([mixed[0], *results[len(slots) :]])
        start += len(slots)

    arrived = [None] * group
    for s in range(group):
        d = slot_partner(group, s)
        arrived[d] = (
            lax.ppermute(messages[s], "seq", [(i, i ^ d) for i in range(seq)]) if d else messages[s]
        )

    messages[-1], rest[0] = lax.optimization_barrier((messages[-1], rest[0]))
    reads = [query(calls[0], 0, *rest[0])]
    arrived, reads = lax.optimization_barrier((arrived, reads))
    hops = seq // group - 1
    chain, leaving = pl.pallas_call(
        functools.partial(prefix_kernel, group, hops > 1),
        in_specs=[whole()] * group,
        out_specs=[whole()] * 2,
        out_shape=[shape(group if hops > 1 else group - 1, 2, DK, 2 * DK), shape(2, DK, DV)],
        compiler_params=params(),
        name="prefix",
    )(*arrived)
    leaving, rest = lax.optimization_barrier((leaving, rest))
    starts = [sum(len(c) for c in calls[:k]) for k in range(len(calls) - 1)] + [0]
    def enter(received, onward):
        return pl.pallas_call(
            functools.partial(enter_kernel, group, onward),
            in_specs=[whole()] * 2,
            out_specs=[whole()] * (group + onward),
            out_shape=[shape(2, DK, DV)] * (group + onward),
            compiler_params=params(),
            name="enter",
        )(received, chain)

    if not hops:
        entering = enter(jnp.zeros((2, DK, DV), f32), False)
    for hop in range(hops):
        received = lax.ppermute(leaving, "seq", [(i, (i + group) % seq) for i in range(seq)])
        if hop == 0:
            reads += [query(*x, *outs) for *x, outs in zip(calls[1:-1], starts[1:-1], rest[1:-1])]
            received, reads, rest = lax.optimization_barrier((received, reads, rest))
        entering = enter(received, hop < hops - 1)
        if hop < hops - 1:
            *entering, leaving = entering

    states = {0: entering[0]}
    for d in range(group - 1, 0, -1):
        states[d] = lax.ppermute(entering[d], "seq", [(i, i ^ d) for i in range(seq)])
    reads.append(query(calls[-1], starts[-1], *rest[-1]))
    where = {s: (k, at) for k, slots in enumerate(calls) for at, s in enumerate(slots)}

    def outputs(slots, written):
        operands = [x for s in slots for x in reads[where[s][0]]]
        operands += [states[slot_partner(group, s)] for s in slots]
        return pl.pallas_call(
            functools.partial(output_kernel, group, [(s, where[s][1]) for s in slots]),
            in_specs=[whole()] * len(operands) + [whole(pl.ANY)] * len(written),
            out_specs=whole(pl.ANY),
            out_shape=shape(tokens, value_width),
            scratch_shapes=[
                VMEM((len(slots), 2, tokens, DV), f32),
                pltpu.SemaphoreType.DMA((len(slots), 2)),
            ],
            input_output_aliases={len(operands): 0} if written else {},
            compiler_params=params(),
            name="outputs",
        )(*operands, *written)

    first = [s for s in range(group) if slot_partner(group, s) < 1]
    written = outputs(first, [])
    return outputs([s for s in range(group) if s not in first], [written])


def solution(mesh):
    placed = (
        P("seq", "head"),
        P("head", None),
        P("seq", "head"),
        P("seq", "head"),
        P("seq", "head"),
        P(None, "head"),
        P(None, "head"),
        P(None, "head"),
        P("head"),
        P("head"),
    )
    return jax.shard_map(
        per_device, mesh=mesh, in_specs=placed, out_specs=P("seq", "head"), check_vma=False
    )
```
